128 devices in a mesh: sub: 32 (over y, z, core), grp: 4 (over x).
Axes of the slice: x: 4, y: 4, z: 4, core: 2. Of those that a mesh axis runs over, the one named last changes fastest.
Arguments:
- flex: float32 [64, 4, 1024, 1024], P('sub', 'grp'), may hold values from -4 to 29, as said below
- coupling: float32 [64, 4, 64, 1024], P('sub', 'grp'), may hold values from -0.375 to 0.375
- weight: float32 [64, 4, 1024], P('sub', 'grp'), may hold values from 1 to 18, as said below
- iface_size: int32 [64, 4], P('sub', 'grp'), may hold values from 128 to 1024, as said below
- partner: int32 [64, 4, 1024], P('sub', 'grp'), may hold values from 0 to 65535, as said below
- corner_map: int32 [64, 4, 64], P('sub', 'grp'), may hold values from 0 to 255
- coarse_factor: float32 [32, 256, 256], P('sub', 'grp'), may hold values from -1 to 2.5, as said below
- lam: float32 [64, 4, 1024, 256], P('sub', 'grp'), may hold values from -8 to 8, as said below
- resid: float32 [64, 4, 1024, 256], P('sub', 'grp'), may hold values from -8 to 8, as said below
- direc: float32 [64, 4, 1024, 256], P('sub', 'grp'), may hold values from -8 to 8, as said below
Outputs:
- lam_next: float32 [64, 4, 1024, 256], P('sub', 'grp')
- resid_next: float32 [64, 4, 1024, 256], P('sub', 'grp')
- direc_next: float32 [64, 4, 1024, 256], P('sub', 'grp')
- ratio: float32 [256], replicated
The draws below stay inside these ranges and needn't reach their ends.
Inputs may be any that keep to these rules, and one draw needn't show every extreme that they name: `iface_size`: every subdomain has at least 128 and at most 1024 live interface dofs, and some subdomain has exactly 1024 in every draw. `partner`: each live dof is matched with exactly one live dof of the subdomain just before or just after it along the chain, in the same cycle position; matching is mutual; a dof that is not live names itself. Two neighbouring subdomains share at most 512 matched pairs, reached between two devices' subdomains in every draw. `weight`: equal at the two dofs of every matched pair. `flex`: each block is symmetric. `coarse_factor`: each cluster's block is lower triangular with a positive diagonal. `lam`: equal and opposite at the two dofs of every matched pair; zero at dofs that are not live. `resid`: equal and opposite at the two dofs of every matched pair; zero at dofs that are not live. `direc`: equal and opposite at the two dofs of every matched pair; zero at dofs that are not live.
All inputs are finite; a program needn't handle non-finite values.
Results may differ from the reference program's by a relative error of at most 0.000094.
Values sent between devices are 32-bit elements; how exact they have to be, the bound alone decides.
No kernel may reach another device: no remote copies, remote signals or barrier semaphores. Data moves between devices by JAX's collectives and lax.ppermute only.
A program may use at most 128 MiB of HBM per device.

```python
import math
import jax
import jax.numpy as jnp
from jax import lax

NI = 1024
NCP = 64
SUB_DEV = 2
LOADS = 256
CHAIN = 64
CYCLE = 4
CLUSTERS = 32
NCO = 256


def layout(key):
    faces = jax.random.randint(jax.random.fold_in(key, 101), (CYCLE, CHAIN + 1), NI // 8, NI // 2 + 1)
    face_index = jnp.arange(CHAIN + 1, dtype=jnp.int32)[None, :]
    faces = jnp.where((face_index == 0) | (face_index == CHAIN), 0, faces)
    forced = (face_index == 1) | (face_index == SUB_DEV) | (face_index == SUB_DEV + 1)
    faces = jnp.where(forced, NI // 2, faces)
    before = faces[:, :CHAIN]
    after = faces[:, 1:]
    totals = before + after
    places = jnp.arange(NI, dtype=jnp.int32)
    scores = jax.random.randint(jax.random.fold_in(key, 102), (CYCLE, CHAIN, NI), 0, NI) * NI + places
    scores = jnp.where(places < totals[..., None], scores, NI * NI + places)
    ordering = jnp.argsort(scores, axis=-1).astype(jnp.int32)
    slot_of = jnp.argsort(ordering, axis=-1).astype(jnp.int32)
    chain_pos = jnp.arange(CHAIN, dtype=jnp.int32)[None, :, None]
    fore_here = before[..., None]
    to_prev = slot_of < fore_here
    to_next = (slot_of >= fore_here) & (slot_of < totals[..., None])
    fore_prev = jnp.roll(before, 1, axis=1)[..., None]
    peer_chain = jnp.where(to_prev, chain_pos - 1, jnp.where(to_next, chain_pos + 1, chain_pos))
    peer_slot = jnp.where(to_prev, fore_prev + slot_of, jnp.where(to_next, slot_of - fore_here, slot_of))
    peer_chain = jnp.clip(peer_chain, 0, CHAIN - 1)
    peer_slot = jnp.clip(peer_slot, 0, NI - 1)
    flat_order = ordering.reshape(CYCLE, CHAIN * NI)
    lookup = (peer_chain * NI + peer_slot).reshape(CYCLE, CHAIN * NI)
    peer_place = jnp.take_along_axis(flat_order, lookup, axis=1).reshape(CYCLE, CHAIN, NI)
    matched = to_prev | to_next
    partner = jnp.where(matched, peer_chain * NI + peer_place, chain_pos * NI + places)
    return (jnp.transpose(totals, (1, 0)).astype(jnp.int32), jnp.transpose(partner, (1, 0, 2)).astype(jnp.int32))


def pair_gather(values, partner):
    load_len = values.shape[3]
    flat = jnp.moveaxis(values, 1, 0).reshape(CYCLE, CHAIN * NI, load_len)
    index = jnp.moveaxis(partner, 1, 0).reshape(CYCLE, CHAIN * NI, 1)
    picked = jnp.take_along_axis(flat, index, axis=1)
    return jnp.moveaxis(picked.reshape(CYCLE, CHAIN, NI, load_len), 0, 1)


def chain_rise(factor):
    return jnp.exp(math.log(factor) * jnp.arange(CHAIN, dtype=jnp.float32) / (CHAIN - 1))


def antisym(key, salt):
    totals, partner = layout(key)
    noise_key = jax.random.fold_in(key, salt)
    shape = (CHAIN, CYCLE, NI, LOADS)
    values = jnp.clip(jax.random.normal(noise_key, shape), -4.0, 4.0)
    other = pair_gather(values, partner)
    live = jnp.arange(NI, dtype=jnp.int32)[None, None, :] < totals[:, :, None]
    return jnp.where(live[..., None], values - other, 0.0).astype(jnp.float32)


def draw_iface_size(key, part):
    return layout(key)[0]


def draw_partner(key, part):
    return layout(key)[1]


def draw_lam(key, part):
    return antisym(key, 201)


def draw_resid(key, part):
    return antisym(key, 202)


def draw_direc(key, part):
    return antisym(key, 203)


def draw_weight(key, part):
    totals, partner = layout(key)
    rising = chain_rise(3.0)
    jitter = jnp.exp(jax.random.uniform(jax.random.fold_in(key, 301), (CHAIN, CYCLE, NI), minval=math.log(0.5), maxval=0.0))
    base = rising[:, None, None] * jitter
    return (base + pair_gather(base[..., None], partner)[..., 0]).astype(jnp.float32)


def draw_flex(key, part):
    shape = (CHAIN, CYCLE, NI, NI)
    noise = jnp.clip(jax.random.normal(jax.random.fold_in(key, 401), shape), -4.0, 4.0)
    rising = chain_rise(3.0)
    symmetric = (noise + jnp.swapaxes(noise, -1, -2)) * (0.35 / math.sqrt(2.0 * NI))
    diagonal = jax.random.uniform(jax.random.fold_in(key, 402), (CHAIN, CYCLE, NI), minval=1.0, maxval=2.0)
    jitter = jnp.exp(jax.random.uniform(jax.random.fold_in(key, 403), (CHAIN, CYCLE), minval=math.log(0.7), maxval=math.log(1.4)))
    scale = rising[:, None] * jitter
    identity = jnp.eye(NI, dtype=jnp.float32)
    return (scale[..., None, None] * (symmetric + identity * diagonal[..., None, :])).astype(jnp.float32)


def draw_coarse_factor(key, part):
    shape = (CLUSTERS, NCO, NCO)
    noise = jnp.clip(jax.random.normal(jax.random.fold_in(key, 501), shape), -4.0, 4.0)
    lower = jnp.tril(noise, -1) * (0.5 / math.sqrt(NCO))
    diagonal = jnp.exp(jax.random.uniform(jax.random.fold_in(key, 502), (CLUSTERS, NCO), minval=math.log(0.5), maxval=math.log(2.0)))
    identity = jnp.eye(NCO, dtype=jnp.float32)
    return (lower + identity * diagonal[..., None, :]).astype(jnp.float32)


def place_ends(entries, stream_key, low, top_value):
    spot = [jax.random.randint(jax.random.fold_in(stream_key, axis), (), 0, length) for axis, length in enumerate(entries.shape)]
    longest = entries.shape.index(max(entries.shape))
    next_to = spot[:longest] + [(spot[longest] + 1) % entries.shape[longest]] + spot[longest + 1:]
    return entries.at[tuple(spot)].set(low).at[tuple(next_to)].set(top_value)


def shard_levels(key, dims, split, smallest, largest):
    def one(axis_at, parts):
        draws = jax.random.uniform(jax.random.fold_in(jax.random.fold_in(key, 6), axis_at), (parts,), jnp.float32, smallest / len(split), largest / len(split))
        return jnp.repeat(jnp.exp(draws), dims[axis_at] // parts).reshape((-1,) + (1,) * (len(dims) - axis_at - 1))

    loudness = one(*split[0])
    for cut in split[1:]:
        loudness = loudness * one(*cut)
    return loudness


def scatter_about(rng, dims, width, bound, cuts=(), kind=jnp.bfloat16):
    result = jax.random.normal(rng, dims, jnp.float32) * width
    if len(cuts) > 0:
        result = shard_levels(rng, dims, cuts, -0.22, 0.18) * result
    return jnp.clip(result, min=-bound, max=bound).astype(kind)


def setup_inputs(seed: int = 0) -> dict:
    streams_of = jax.random.split(jax.random.key(seed), 11)
    flex = draw_flex(jax.random.fold_in(streams_of[10], 71), 0)
    coupling = scatter_about(streams_of[1], (CHAIN, CYCLE, NCP, NI), (NI // 4) ** -0.5, 0.375, ((0, 32), (1, 4)), jnp.float32)
    weight = draw_weight(jax.random.fold_in(streams_of[10], 71), 0)
    iface_size = draw_iface_size(jax.random.fold_in(streams_of[10], 71), 0)
    partner = draw_partner(jax.random.fold_in(streams_of[10], 71), 0)
    corner_map = place_ends(jax.random.randint(streams_of[5], (CHAIN, CYCLE, NCP), 0, NCO), jax.random.fold_in(streams_of[5], 1), 0, NCO - 1).astype(jnp.int32)
    coarse_factor = draw_coarse_factor(jax.random.fold_in(streams_of[10], 71), 0)
    lam = draw_lam(jax.random.fold_in(streams_of[10], 71), 0)
    resid = draw_resid(jax.random.fold_in(streams_of[10], 71), 0)
    direc = draw_direc(jax.random.fold_in(streams_of[10], 71), 0)
    return dict(flex=flex, coupling=coupling, weight=weight, iface_size=iface_size, partner=partner, corner_map=corner_map, coarse_factor=coarse_factor, lam=lam, resid=resid, direc=direc)


def pair_values(values, partner):
    chain_len, cycle_len, dof_len = partner.shape
    load_len = values.shape[3]
    flat = jnp.moveaxis(values, 1, 0).reshape(cycle_len, chain_len * dof_len, load_len)
    index = jnp.moveaxis(partner, 1, 0).reshape(cycle_len, chain_len * dof_len, 1)
    picked = jnp.take_along_axis(flat, index, axis=1)
    return jnp.moveaxis(picked.reshape(cycle_len, chain_len, dof_len, load_len), 0, 1)


def reference(flex, coupling, weight, iface_size, partner, corner_map, coarse_factor, lam, resid, direc):
    highest = lax.Precision.HIGHEST
    live = (jnp.arange(NI, dtype=jnp.int32)[None, None, :] < iface_size[:, :, None])[..., None]
    masked = jnp.where(live, direc, 0.0)
    local = jnp.einsum('gbij,gbjl->gbil', flex, masked, precision=highest)
    primal = jnp.einsum('gbcj,gbjl->gbcl', coupling, masked, precision=highest)
    cluster = (jnp.arange(CHAIN, dtype=jnp.int32) // SUB_DEV)[:, None, None]
    segment = (cluster * NCO + corner_map).reshape(-1).astype(jnp.int32)
    coarse_rhs = jax.ops.segment_sum(primal.reshape(-1, LOADS), segment, num_segments=CLUSTERS * NCO)
    coarse_rhs = coarse_rhs.reshape(CLUSTERS, NCO, LOADS)
    coarse_mid = jnp.einsum('amn,anl->aml', coarse_factor, coarse_rhs, precision=highest)
    coarse_sol = jnp.einsum('anm,anl->aml', coarse_factor, coarse_mid, precision=highest)
    picked = jnp.take(coarse_sol.reshape(CLUSTERS * NCO, LOADS), segment, axis=0)
    picked = picked.reshape(CHAIN, CYCLE, NCP, LOADS)
    image = local + jnp.einsum('gbcj,gbcl->gbjl', coupling, picked, precision=highest)
    jump = jnp.where(live, image - pair_values(image, partner), 0.0)
    precond = jnp.where(live, weight[..., None] * resid, 0.0)
    rz_old = jnp.sum(resid * precond, axis=(0, 1, 2))
    curvature = jnp.sum(direc * jump, axis=(0, 1, 2))
    alpha = rz_old / curvature
    lam_next = lam + alpha * direc
    resid_next = resid - alpha * jump
    precond_next = jnp.where(live, weight[..., None] * resid_next, 0.0)
    rz_new = jnp.sum(resid_next * precond_next, axis=(0, 1, 2))
    ratio = rz_new / rz_old
    direc_next = precond_next + ratio * direc
    return lam_next, resid_next, direc_next, ratio
```

```python
import functools

import jax
import jax.numpy as jnp
from jax import lax
from jax.experimental import pallas as pl
from jax.experimental.pallas import tpu as pltpu
from jax.sharding import PartitionSpec as P

F32 = jnp.float32
BF16 = jnp.bfloat16
N = 1024
L = 256
C = 64
HALF = 512
MIB = 1 << 20


def dot(a, b):
    return lax.dot_general(a, b, (((1,), (0,)), ((), ())), preferred_element_type=F32)


def dot_t(a, b):
    return lax.dot_general(a, b, (((0,), (0,)), ((), ())), preferred_element_type=F32)


def split(x):
    high = x.astype(BF16)
    low = (x - high.astype(F32)).astype(BF16)
    return high, low


def iota(shape, dim):
    return lax.broadcasted_iota(jnp.int32, shape, dim)


def one_hot(test):
    return jnp.where(test, 1.0, 0.0).astype(BF16)


def fold(x):
    return jnp.sum(x.reshape(-1, 8, x.shape[-1]), axis=0)


def column(row):
    tall = jnp.transpose(jnp.broadcast_to(row, (128, row.shape[1])))
    return jnp.concatenate([tall, tall], axis=1)


def primal_kernel(direc_ref, coup_ref, map_ref, factor_ref, pay_ref):
    for s in range(2):
        dh, dl = split(direc_ref[s])
        ch, cl = split(coup_ref[s])
        pay_ref[s * C : (s + 1) * C] = dot(ch, dh) + dot(ch, dl) + dot(cl, dh)
    pay_ref[2 * C : 3 * C] = factor_ref[...]
    pay_ref[3 * C :] = jnp.zeros((8, L), F32)
    for s in range(2):
        pay_ref[3 * C + s : 3 * C + s + 1, 0:C] = map_ref[s].astype(F32)


def local_kernel(flex_ref, direc_ref, out_ref, high, low):
    @pl.when(pl.program_id(1) == 0)
    def _():
        dh, dl = split(direc_ref[0])
        high[...] = dh
        low[...] = dl

    ah, al = split(flex_ref[0])
    out_ref[0] = dot(ah, high[...]) + dot(ah, low[...]) + dot(al, high[...])


def running_count(mask):
    total = mask.astype(jnp.int32)
    lane = iota(total.shape, 1)
    step = 1
    while step < total.shape[1]:
        total = total + jnp.where(lane >= step, pltpu.roll(total, step, 1), 0)
        step *= 2
    return total


def selector(pay_ref):
    first = pay_ref[3 * C : 3 * C + 1, 0:C]
    second = pay_ref[3 * C + 1 : 3 * C + 2, 0:C]
    both = jnp.concatenate([first, second], axis=1).astype(jnp.int32)
    return one_hot(iota((L, 2 * C), 0) == both)


def image_kernel(
    place_ref, local_ref, pay_ref, one_ref, two_ref, three_ref, coup_ref, partner_ref,
    image_ref, cross_ref, near_ref, high, low,
):
    me = place_ref[0]
    odd = lax.rem(me, 2)
    members = (pay_ref, one_ref, two_ref, three_ref)
    rhs = jnp.zeros((L, L), F32)
    for member in members:
        sel = selector(member)
        ph, pl_ = split(member[0 : 2 * C])
        rhs = rhs + dot(sel, ph) + dot(sel, pl_)
    factor = jnp.concatenate([m[2 * C : 3 * C] for m in members], axis=0)
    fh, fl = split(factor)
    rh, rl = split(rhs)
    mid = dot(fh, rh) + dot(fh, rl) + dot(fl, rh)
    mh, ml = split(mid)
    sol = dot_t(fh, mh) + dot_t(fh, ml) + dot_t(fl, mh)
    sh, sl = split(sol)
    own = selector(pay_ref)
    picked = dot_t(own, sh) + dot_t(own, sl)
    for s in range(2):
        ch, cl = split(coup_ref[s])
        qh, ql = split(picked[s * C : (s + 1) * C])
        left = jnp.concatenate([ch, ch, cl], axis=0)
        right = jnp.concatenate([qh, ql, qh], axis=0)
        for r in range(0, N, L):
            image = local_ref[s, r : r + L] + dot_t(left[:, r : r + L], right)
            image_ref[s, r : r + L] = image
            ih, il = split(image)
            high[r : r + L] = ih
            low[r : r + L] = il
        target = partner_ref[s] - (2 * me - 1) * N
        match = (target >= 3 * N) if s else (target < N)
        key = jnp.where(match, running_count(match) - 1, -1)
        name = jnp.where(match, jnp.bitwise_and(target, N - 1) + 1, 0)
        coarse = lax.shift_right_logical(name, 5)
        fine = jnp.bitwise_and(name, 31)
        digits = jnp.concatenate(
            [coarse, fine, jnp.zeros((6, N), jnp.int32)], axis=0
        ).astype(F32).astype(BF16)

        def pack(ref):
            ref[HALF:] = jnp.zeros((8, L), F32)
            for c in range(2):
                place = one_hot(iota((L, N), 0) + c * L == key)
                ref[c * L : (c + 1) * L] = dot(place, high[...]) + dot(place, low[...])
                names = lax.dot_general(
                    digits, place, (((1,), (1,)), ((), ())), preferred_element_type=F32
                )
                ref[HALF + c : HALF + c + 1] = names[0:1] * 32.0 + names[1:2]

        pl.when(odd == s)(functools.partial(pack, cross_ref))
        pl.when(odd != s)(functools.partial(pack, near_ref))


def inner_kernel(place_ref, image_ref, direc_ref, resid_ref, weight_ref, partner_ref, jump_ref, sums_ref, high, low):
    me = place_ref[0]
    old = jnp.zeros((8, L), F32)
    curve = jnp.zeros((8, L), F32)
    mixed = jnp.zeros((8, L), F32)
    for s in range(2):
        other = 1 - s
        for r in range(0, N, L):
            ih, il = split(image_ref[other, r : r + L])
            high[r : r + L] = ih
            low[r : r + L] = il
        theirs = partner_ref[other] - (2 * me - 1 + 1 + s) * N
        mine = partner_ref[s]
        awake = jnp.where(lax.shift_right_arithmetic(mine, 10) != 2 * me + s, 1.0, 0.0)
        for r in range(0, N, L):
            rows = slice(r, r + L)
            place = one_hot(iota((L, N), 0) + r == theirs)
            opposite = dot(place, high[...]) + dot(place, low[...])
            image = image_ref[s, rows]
            jump_ref[s, rows] = column(awake[:, rows]) * image - opposite
            scaled = column(weight_ref[s][:, rows]) * resid_ref[s, rows]
            old = old + fold(scaled * resid_ref[s, rows])
            curve = curve + fold(direc_ref[s, rows] * image)
            mixed = mixed + fold(scaled * image)
    sums_ref[0] = old
    sums_ref[1] = curve
    sums_ref[2] = mixed


def outer_kernel(place_ref, part_ref, cross_ref, near_ref, weight_ref, sums_ref, jump_ref, total_ref):
    odd = lax.rem(place_ref[0], 2)
    square = jnp.zeros((8, L), F32)
    for ref, s in ((cross_ref, odd), (near_ref, 1 - odd)):
        pieces = [split(ref[c * L : (c + 1) * L]) for c in range(2)]
        for r in range(0, N, L):
            opposite = jnp.zeros((L, L), F32)
            for c in range(2):
                name = ref[HALF + c : HALF + c + 1].astype(jnp.int32)
                place = one_hot(iota((L, L), 0) + (r + 1) == name)
                opposite = opposite + dot(place, pieces[c][0]) + dot(place, pieces[c][1])
            jump = part_ref[s, r : r + L] - opposite
            jump_ref[s, r : r + L] = jump
            square = square + fold(column(weight_ref[s][:, r : r + L]) * jump * jump)
    rows = [jnp.sum(x, axis=0, keepdims=True) for x in (sums_ref[0], sums_ref[1], sums_ref[2], square)]
    total_ref[...] = jnp.concatenate(rows + [jnp.zeros((4, L), F32)], axis=0)


def final_kernel(total_ref, weight_ref, lam_ref, resid_ref, direc_ref, jump_ref, lam_out, resid_out, direc_out, ratio_out):
    old = total_ref[0:1]
    alpha = old / (2.0 * total_ref[1:2])
    new = old + alpha * (alpha * total_ref[3:4] - 4.0 * total_ref[2:3])
    ratio = new / old
    ratio_out[...] = ratio
    direc = direc_ref[0]
    resid = resid_ref[0] - alpha * jump_ref[0]
    lam_out[0] = lam_ref[0] + alpha * direc
    resid_out[0] = resid
    direc_out[0] = column(weight_ref[0]) * resid + ratio * direc


def vmem():
    return pl.BlockSpec(memory_space=pltpu.VMEM)


def smem():
    return pl.BlockSpec(memory_space=pltpu.SMEM)


def exchange(x, axes, size, route):
    pairs = []
    for i in range(size):
        j = route(i)
        if j is not None:
            pairs.append((i, j))
    return lax.ppermute(x, axes, pairs)


def per_device(
    flex, coupling, weight, iface_size, partner, corner_map, coarse_factor, lam, resid, direc
):
    del iface_size
    blocks, links, scale = flex[:, 0], coupling[:, 0], weight
    lam2, resid2, direc2 = lam[:, 0], resid[:, 0], direc[:, 0]
    chain = lax.axis_size("sub")
    place = lax.axis_index("sub").astype(jnp.int32).reshape(1)

    pay = pl.pallas_call(
        primal_kernel,
        out_shape=jax.ShapeDtypeStruct((3 * C + 8, L), F32),
        in_specs=[vmem()] * 4,
        out_specs=vmem(),
        name="primal",
        compiler_params=pltpu.CompilerParams(vmem_limit_bytes=16 * MIB),
        cost_estimate=pl.CostEstimate(flops=200_000_000, bytes_accessed=3 * MIB, transcendentals=0),
    )(direc2, links, corner_map, coarse_factor[0])
    others = [exchange(pay, "grp", 4, lambda i, m=m: i ^ m) for m in (1, 3, 2)]

    local = pl.pallas_call(
        local_kernel,
        grid=(2, 4),
        out_shape=jax.ShapeDtypeStruct((2, N, L), F32),
        in_specs=[
            pl.BlockSpec((1, L, N), lambda s, r: (s, r, 0)),
            pl.BlockSpec((1, N, L), lambda s, r: (s, 0, 0)),
        ],
        out_specs=pl.BlockSpec((1, L, L), lambda s, r: (s, r, 0)),
        scratch_shapes=[pltpu.VMEM((N, L), BF16)] * 2,
        name="local",
        compiler_params=pltpu.CompilerParams(vmem_limit_bytes=24 * MIB),
        cost_estimate=pl.CostEstimate(flops=3_300_000_000, bytes_accessed=12 * MIB, transcendentals=0),
    )(blocks, direc2)

    packed = jax.ShapeDtypeStruct((HALF + 8, L), F32)
    image, cross, near = pl.pallas_call(
        image_kernel,
        out_shape=(jax.ShapeDtypeStruct((2, N, L), F32), packed, packed),
        in_specs=[smem()] + [vmem()] * 7,
        out_specs=(vmem(), vmem(), vmem()),
        scratch_shapes=[pltpu.VMEM((N, L), BF16)] * 2,
        name="image",
        compiler_params=pltpu.CompilerParams(vmem_limit_bytes=24 * MIB),
    )(place, local, pay, *others, links, partner)

    def across(i):
        j = i + 1 if i % 2 else i - 1
        return j if 0 <= j < chain else None

    got_cross = exchange(cross, "sub", chain, across)
    got_near = exchange(near, "sub", chain, lambda i: i ^ 1)

    part, sums = pl.pallas_call(
        inner_kernel,
        out_shape=(jax.ShapeDtypeStruct((2, N, L), F32), jax.ShapeDtypeStruct((3, 8, L), F32)),
        in_specs=[smem()] + [vmem()] * 5,
        out_specs=(vmem(), vmem()),
        scratch_shapes=[pltpu.VMEM((N, L), BF16)] * 2,
        name="inner",
        compiler_params=pltpu.CompilerParams(vmem_limit_bytes=24 * MIB),
        cost_estimate=pl.CostEstimate(flops=2_200_000_000, bytes_accessed=8 * MIB, transcendentals=0),
    )(place, image, direc2, resid2, scale, partner)

    jump, total = pl.pallas_call(
        outer_kernel,
        out_shape=(jax.ShapeDtypeStruct((2, N, L), F32), jax.ShapeDtypeStruct((8, L), F32)),
        in_specs=[smem()] + [vmem()] * 5,
        out_specs=(vmem(), vmem()),
        name="outer",
        compiler_params=pltpu.CompilerParams(vmem_limit_bytes=24 * MIB),
    )(place, part, got_cross, got_near, scale, sums)

    total = total + exchange(total, "sub", chain, lambda i: i ^ 1)
    for m in (1, 3):
        total = total + exchange(total, "grp", 4, lambda i, m=m: i ^ m)
    for bit in (2, 8):
        for m in (1, 3):
            total = total + exchange(total, "sub", chain, lambda i, m=m, bit=bit: i ^ (m * bit))

    def rows(s, r):
        return (s, r, 0)

    spec = pl.BlockSpec((1, L, L), rows)
    whole = jax.ShapeDtypeStruct((2, N, L), F32)
    lam_next, resid_next, direc_next, ratio = pl.pallas_call(
        final_kernel,
        grid=(2, 4),
        out_shape=(whole, whole, whole, jax.ShapeDtypeStruct((1, L), F32)),
        in_specs=[
            pl.BlockSpec((8, L), lambda s, r: (0, 0)),
            pl.BlockSpec((1, 1, L), lambda s, r: (s, 0, r)),
            spec, spec, spec, spec,
        ],
        out_specs=(spec, spec, spec, pl.BlockSpec((1, L), lambda s, r: (0, 0))),
        name="final",
        compiler_params=pltpu.CompilerParams(vmem_limit_bytes=16 * MIB),
    )(total, scale, lam2, resid2, direc2, jump)
    return (lam_next[:, None], resid_next[:, None], direc_next[:, None], ratio[0])


def solution(mesh):
    placed = (
        P("sub", "grp", None, None),
        P("sub", "grp", None, None),
        P("sub", "grp", None),
        P("sub", "grp"),
        P("sub", "grp", None),
        P("sub", "grp", None),
        P("sub", "grp", None),
        P("sub", "grp", None, None),
        P("sub", "grp", None, None),
        P("sub", "grp", None, None),
    )
    return jax.shard_map(
        per_device,
        mesh=mesh,
        in_specs=placed,
        out_specs=(
            P("sub", "grp", None, None),
            P("sub", "grp", None, None),
            P("sub", "grp", None, None),
            P(),
        ),
        check_vma=False,
    )
```

```python
import functools

import jax
import jax.numpy as jnp
from jax import lax
from jax.experimental import pallas as pl
from jax.experimental.pallas import tpu as pltpu
from jax.sharding import PartitionSpec as P

F32 = jnp.float32
BF16 = jnp.bfloat16
N = 1024
L = 256
C = 64
HALF = 512
NAMES = HALF + 2 * C
STRIP = 512
ROUNDS = N // STRIP
MIB = 1 << 20


def dot(a, b):
    return lax.dot_general(a, b, (((1,), (0,)), ((), ())), preferred_element_type=F32)


def dot_t(a, b):
    return lax.dot_general(a, b, (((0,), (0,)), ((), ())), preferred_element_type=F32)


def split(x):
    high = x.astype(BF16)
    low = (x - high.astype(F32)).astype(BF16)
    return high, low


def iota(shape, dim):
    return lax.broadcasted_iota(jnp.int32, shape, dim)


def one_hot(test):
    return jnp.where(test, 1.0, 0.0).astype(BF16)


def fold(x):
    return jnp.sum(x.reshape(-1, 8, x.shape[-1]), axis=0)


def column(row):
    tall = jnp.transpose(jnp.broadcast_to(row, (128, row.shape[1])))
    return jnp.concatenate([tall, tall], axis=1)


def primal_kernel(direc_hbm, coup_hbm, map_hbm, factor_hbm, pay_ref, direc, coup, corner, sems):
    copies = [
        pltpu.make_async_copy(coup_hbm, coup, sems.at[0]),
        pltpu.make_async_copy(direc_hbm.at[0], direc.at[0], sems.at[1]),
        pltpu.make_async_copy(direc_hbm.at[1], direc.at[1], sems.at[2]),
        pltpu.make_async_copy(map_hbm, corner, sems.at[3]),
        pltpu.make_async_copy(factor_hbm, pay_ref.at[pl.ds(2 * C, C)], sems.at[4]),
    ]
    for copy in copies:
        copy.start()
    pay_ref[3 * C :] = jnp.zeros((8, L), F32)
    copies[0].wait()
    for s in range(2):
        ch, cl = split(coup[s])
        copies[1 + s].wait()
        dh, dl = split(direc[s])
        pay_ref[s * C : (s + 1) * C] = dot(ch, dh) + dot(ch, dl) + dot(cl, dh)
    copies[3].wait()
    for s in range(2):
        pay_ref[3 * C + s : 3 * C + s + 1, 0:C] = corner[s].astype(F32)
    copies[4].wait()


def running_count(mask):
    total = mask.astype(jnp.int32)
    lane = iota(total.shape, 1)
    step = 1
    while step < total.shape[1]:
        total = total + jnp.where(lane >= step, pltpu.roll(total, step, 1), 0)
        step *= 2
    return total


def local_kernel(
    place_ref, flex_hbm, direc_ref, coup_ref, partner_ref,
    local_ref, cross_ref, near_ref, flex, right, high, low, sems,
):
    copies = []
    for s in range(2):
        for r in range(ROUNDS):
            rows = pl.ds(r * STRIP, STRIP)
            copy = pltpu.make_async_copy(
                flex_hbm.at[s, rows], flex.at[s, rows], sems.at[s * ROUNDS + r]
            )
            copy.start()
            copies.append(copy)
    me = place_ref[0]
    odd = lax.rem(me, 2)
    for s in range(2):
        dh, dl = split(direc_ref[s])
        right[0:N] = dh
        right[N : 2 * N] = dl
        right[2 * N :] = dh
        for r in range(ROUNDS):
            rows = slice(r * STRIP, (r + 1) * STRIP)
            copies[s * ROUNDS + r].wait()
            ah, al = split(flex[s, rows])
            out = dot(jnp.concatenate([ah, ah, al], axis=1), right[...])
            local_ref[s, rows] = out
            oh, ol = split(out)
            high[rows] = oh
            low[rows] = ol
        target = partner_ref[s] - (2 * me - 1) * N
        match = (target >= 3 * N) if s else (target < N)
        key = jnp.where(match, running_count(match) - 1, -1)
        name = jnp.where(match, jnp.bitwise_and(target, N - 1) + 1, 0)
        coarse = lax.shift_right_logical(name, 5)
        fine = jnp.bitwise_and(name, 31)
        digits = jnp.concatenate(
            [coarse, fine, jnp.zeros((14, N), jnp.int32)], axis=0
        ).astype(F32).astype(BF16)
        ch, cl = split(coup_ref[s])
        left = jnp.concatenate([ch, cl, digits], axis=0)

        def pack(ref):
            ref[NAMES:] = jnp.zeros((8, L), F32)
            for c in range(2):
                place = one_hot(iota((L, N), 0) + c * L == key)
                ref[c * L : (c + 1) * L] = dot(place, high[...]) + dot(place, low[...])
                extra = lax.dot_general(
                    left, place, (((1,), (1,)), ((), ())), preferred_element_type=F32
                )
                ref[HALF + c * C : HALF + (c + 1) * C] = extra[0:C] + extra[C : 2 * C]
                ref[NAMES + c : NAMES + c + 1] = extra[2 * C : 2 * C + 1] * 32.0 + extra[2 * C + 1 : 2 * C + 2]

        pl.when(odd == s)(functools.partial(pack, cross_ref))
        pl.when(odd != s)(functools.partial(pack, near_ref))


def selector(pay_ref):
    first = pay_ref[3 * C : 3 * C + 1, 0:C]
    second = pay_ref[3 * C + 1 : 3 * C + 2, 0:C]
    both = jnp.concatenate([first, second], axis=1).astype(jnp.int32)
    return one_hot(iota((L, 2 * C), 0) == both)


def coarse_kernel(place_ref, pay_ref, one_ref, two_ref, three_ref, cross_ref, near_ref):
    odd = lax.rem(place_ref[0], 2)
    members = (pay_ref, one_ref, two_ref, three_ref)
    sels, parts = [], []
    for member in members:
        sel = selector(member)
        ph, pl_ = split(member[0 : 2 * C])
        sels += [sel, sel]
        parts += [ph, pl_]
    rhs = dot(jnp.concatenate(sels, axis=1), jnp.concatenate(parts, axis=0))
    factor = jnp.concatenate([m[2 * C : 3 * C] for m in members], axis=0)
    fh, fl = split(factor)
    rh, rl = split(rhs)
    mid = dot(jnp.concatenate([fh, fh, fl], axis=1), jnp.concatenate([rh, rl, rh], axis=0))
    mh, ml = split(mid)
    sol = dot_t(jnp.concatenate([fh, fh, fl], axis=0), jnp.concatenate([mh, ml, mh], axis=0))
    sh, sl = split(sol)
    own = sels[0]
    picked = dot_t(jnp.concatenate([own, own], axis=0), jnp.concatenate([sh, sl], axis=0))

    @pl.when(odd == 0)
    def _():
        cross_ref[...] = picked[0:C]
        near_ref[...] = picked[C:]

    @pl.when(odd == 1)
    def _():
        near_ref[...] = picked[0:C]
        cross_ref[...] = picked[C:]


def inner_kernel(
    place_ref, local_ref, cross_ref, near_ref, coup_ref, direc_ref, resid_ref, weight_ref, partner_ref,
    jump_ref, sums_ref, image_ref, high, low,
):
    me = place_ref[0]
    odd = lax.rem(me, 2) == 1
    old = jnp.zeros((8, L), F32)
    curve = jnp.zeros((8, L), F32)
    mixed = jnp.zeros((8, L), F32)
    for s in range(2):
        ch, cl = split(coup_ref[s])
        qh, ql = split(jnp.where(odd == (s == 1), cross_ref[...], near_ref[...]))
        left = jnp.concatenate([ch, ch, cl], axis=0)
        right = jnp.concatenate([qh, ql, qh], axis=0)
        for r in range(0, N, L):
            image = local_ref[s, r : r + L] + dot_t(left[:, r : r + L], right)
            image_ref[s, r : r + L] = image
            ih, il = split(image)
            high[s, r : r + L] = ih
            low[s, r : r + L] = il
    for s in range(2):
        other = 1 - s
        theirs = partner_ref[other] - (2 * me + s) * N
        mine = partner_ref[s]
        awake = jnp.where(lax.shift_right_arithmetic(mine, 10) != 2 * me + s, 1.0, 0.0)
        for r in range(0, N, L):
            rows = slice(r, r + L)
            place = one_hot(iota((L, N), 0) + r == theirs)
            opposite = dot(place, high[other]) + dot(place, low[other])
            image = image_ref[s, rows]
            jump_ref[s, rows] = column(awake[:, rows]) * image - opposite
            scaled = column(weight_ref[s][:, rows]) * resid_ref[s, rows]
            old = old + fold(scaled * resid_ref[s, rows])
            curve = curve + fold(direc_ref[s, rows] * image)
            mixed = mixed + fold(scaled * image)
    sums_ref[0] = old
    sums_ref[1] = curve
    sums_ref[2] = mixed


def outer_kernel(
    place_ref, part_ref, cross_ref, near_ref, cross_pick_ref, near_pick_ref, weight_ref, sums_ref,
    jump_ref, total_ref,
):
    odd = lax.rem(place_ref[0], 2)
    square = jnp.zeros((8, L), F32)
    for ref, pick_ref, s in ((cross_ref, cross_pick_ref, odd), (near_ref, near_pick_ref, 1 - odd)):
        qh, ql = split(pick_ref[...])
        right = jnp.concatenate([qh, ql, qh], axis=0)
        highs, lows = [], []
        for c in range(2):
            ch, cl = split(ref[HALF + c * C : HALF + (c + 1) * C])
            left = jnp.concatenate([ch, ch, cl], axis=0)
            image_high, image_low = split(ref[c * L : (c + 1) * L] + dot_t(left, right))
            highs.append(image_high)
            lows.append(image_low)
        stacked = jnp.concatenate(highs + lows, axis=0)
        names = [ref[NAMES + c : NAMES + c + 1].astype(jnp.int32) for c in range(2)]
        for r in range(0, N, L):
            places = [one_hot(iota((L, L), 0) + (r + 1) == name) for name in names]
            opposite = dot(jnp.concatenate(places + places, axis=1), stacked)
            jump = part_ref[s, r : r + L] - opposite
            jump_ref[s, r : r + L] = jump
            square = square + fold(column(weight_ref[s][:, r : r + L]) * jump * jump)
    rows = [jnp.sum(x, axis=0, keepdims=True) for x in (sums_ref[0], sums_ref[1], sums_ref[2], square)]
    total_ref[...] = jnp.concatenate(rows + [jnp.zeros((4, L), F32)], axis=0)


def final_kernel(
    total_ref, weight_ref, lam_ref, resid_ref, direc_ref, jump_ref,
    lam_hbm, resid_hbm, direc_hbm, ratio_ref, lam_out, resid_out, direc_out, sems,
):
    old = total_ref[0:1]
    alpha = old / (2.0 * total_ref[1:2])
    new = old + alpha * (alpha * total_ref[3:4] - 4.0 * total_ref[2:3])
    ratio = new / old
    ratio_ref[...] = ratio
    copies = []
    for s in range(2):
        for r in range(4):
            rows = slice(r * L, (r + 1) * L)
            direc = direc_ref[s, rows]
            resid = resid_ref[s, rows] - alpha * jump_ref[s, rows]
            lam_out[s, rows] = lam_ref[s, rows] + alpha * direc
            resid_out[s, rows] = resid
            direc_out[s, rows] = column(weight_ref[s][:, rows]) * resid + ratio * direc
            piece = pl.ds(r * L, L)
            for k, (here, there) in enumerate(
                ((lam_out, lam_hbm), (resid_out, resid_hbm), (direc_out, direc_hbm))
            ):
                copy = pltpu.make_async_copy(
                    here.at[s, piece], there.at[s, piece], sems.at[(s * 4 + r) * 3 + k]
                )
                copy.start()
                copies.append(copy)
    for copy in copies:
        copy.wait()


def vmem():
    return pl.BlockSpec(memory_space=pltpu.VMEM)


def hbm():
    return pl.BlockSpec(memory_space=pltpu.HBM)


def smem():
    return pl.BlockSpec(memory_space=pltpu.SMEM)


def exchange(x, axes, size, route):
    pairs = []
    for i in range(size):
        j = route(i)
        if j is not None:
            pairs.append((i, j))
    return lax.ppermute(x, axes, pairs)


def per_device(
    flex, coupling, weight, iface_size, partner, corner_map, coarse_factor, lam, resid, direc
):
    del iface_size
    blocks, links, scale = flex[:, 0], coupling[:, 0], weight
    lam2, resid2, direc2 = lam[:, 0], resid[:, 0], direc[:, 0]
    chain = lax.axis_size("sub")
    place = lax.axis_index("sub").astype(jnp.int32).reshape(1)

    pay = pl.pallas_call(
        primal_kernel,
        out_shape=jax.ShapeDtypeStruct((3 * C + 8, L), F32),
        in_specs=[hbm()] * 4,
        out_specs=vmem(),
        scratch_shapes=[
            pltpu.VMEM((2, N, L), F32),
            pltpu.VMEM((2, C, N), F32),
            pltpu.VMEM((2, 1, C), jnp.int32),
            pltpu.SemaphoreType.DMA((5,)),
        ],
        name="primal",
        compiler_params=pltpu.CompilerParams(vmem_limit_bytes=16 * MIB),
        cost_estimate=pl.CostEstimate(flops=200_000_000, bytes_accessed=3 * MIB, transcendentals=0),
    )(direc2, links, corner_map, coarse_factor[0])
    others = [exchange(pay, "grp", 4, lambda i, m=m: i ^ m) for m in (1, 3, 2)]

    packed = jax.ShapeDtypeStruct((NAMES + 8, L), F32)
    local, cross, near = pl.pallas_call(
        local_kernel,
        out_shape=(jax.ShapeDtypeStruct((2, N, L), F32), packed, packed),
        in_specs=[smem(), hbm()] + [vmem()] * 3,
        out_specs=(vmem(), vmem(), vmem()),
        scratch_shapes=[
            pltpu.VMEM((2, N, N), F32),
            pltpu.VMEM((3 * N, L), BF16),
            pltpu.VMEM((N, L), BF16),
            pltpu.VMEM((N, L), BF16),
            pltpu.SemaphoreType.DMA((2 * ROUNDS,)),
        ],
        name="local",
        compiler_params=pltpu.CompilerParams(vmem_limit_bytes=32 * MIB),
        cost_estimate=pl.CostEstimate(flops=4_000_000_000, bytes_accessed=12 * MIB, transcendentals=0),
    )(place, blocks, direc2, links, partner)

    def across(i):
        j = i + 1 if i % 2 else i - 1
        return j if 0 <= j < chain else None

    def beside(i):
        return i ^ 1

    got_cross = exchange(cross, "sub", chain, across)
    got_near = exchange(near, "sub", chain, beside)

    piece = jax.ShapeDtypeStruct((C, L), F32)
    cross_pick, near_pick = pl.pallas_call(
        coarse_kernel,
        out_shape=(piece, piece),
        in_specs=[smem()] + [vmem()] * 4,
        out_specs=(vmem(), vmem()),
        name="coarse",
        compiler_params=pltpu.CompilerParams(vmem_limit_bytes=16 * MIB),
        cost_estimate=pl.CostEstimate(flops=500_000_000, bytes_accessed=MIB, transcendentals=0),
    )(place, pay, *others)
    got_cross_pick = exchange(cross_pick, "sub", chain, across)
    got_near_pick = exchange(near_pick, "sub", chain, beside)

    whole = jax.ShapeDtypeStruct((2, N, L), F32)
    part, sums = pl.pallas_call(
        inner_kernel,
        out_shape=(whole, jax.ShapeDtypeStruct((3, 8, L), F32)),
        in_specs=[smem()] + [vmem()] * 8,
        out_specs=(vmem(), vmem()),
        scratch_shapes=[
            pltpu.VMEM((2, N, L), F32),
            pltpu.VMEM((2, N, L), BF16),
            pltpu.VMEM((2, N, L), BF16),
        ],
        name="inner",
        compiler_params=pltpu.CompilerParams(vmem_limit_bytes=24 * MIB),
        cost_estimate=pl.CostEstimate(flops=2_500_000_000, bytes_accessed=8 * MIB, transcendentals=0),
    )(place, local, cross_pick, near_pick, links, direc2, resid2, scale, partner)

    jump, total = pl.pallas_call(
        outer_kernel,
        out_shape=(whole, jax.ShapeDtypeStruct((8, L), F32)),
        in_specs=[smem()] + [vmem()] * 7,
        out_specs=(vmem(), vmem()),
        name="outer",
        compiler_params=pltpu.CompilerParams(vmem_limit_bytes=24 * MIB),
    )(place, part, got_cross, got_near, got_cross_pick, got_near_pick, scale, sums)

    total = total + exchange(total, "sub", chain, beside)
    for m in (1, 3):
        total = total + exchange(total, "grp", 4, lambda i, m=m: i ^ m)
    for bit in (2, 8):
        for m in (1, 3):
            total = total + exchange(total, "sub", chain, lambda i, m=m, bit=bit: i ^ (m * bit))

    lam_next, resid_next, direc_next, ratio = pl.pallas_call(
        final_kernel,
        out_shape=(whole, whole, whole, jax.ShapeDtypeStruct((1, L), F32)),
        in_specs=[vmem()] * 6,
        out_specs=(hbm(), hbm(), hbm(), vmem()),
        scratch_shapes=[pltpu.VMEM((2, N, L), F32)] * 3 + [pltpu.SemaphoreType.DMA((24,))],
        name="final",
        compiler_params=pltpu.CompilerParams(vmem_limit_bytes=24 * MIB),
    )(total, scale, lam2, resid2, direc2, jump)
    return (lam_next[:, None], resid_next[:, None], direc_next[:, None], ratio[0])


def solution(mesh):
    placed = (
        P("sub", "grp", None, None),
        P("sub", "grp", None, None),
        P("sub", "grp", None),
        P("sub", "grp"),
        P("sub", "grp", None),
        P("sub", "grp", None),
        P("sub", "grp", None),
        P("sub", "grp", None, None),
        P("sub", "grp", None, None),
        P("sub", "grp", None, None),
    )
    return jax.shard_map(
        per_device,
        mesh=mesh,
        in_specs=placed,
        out_specs=(
            P("sub", "grp", None, None),
            P("sub", "grp", None, None),
            P("sub", "grp", None, None),
            P(),
        ),
        check_vma=False,
    )
```

```python
import functools

import jax
import jax.numpy as jnp
from jax import lax
from jax.experimental import pallas as pl
from jax.experimental.pallas import tpu as pltpu
from jax.sharding import PartitionSpec as P

F32 = jnp.float32
BF16 = jnp.bfloat16
N = 1024
L = 256
C = 64
HALF = 512
NAMES = HALF + 2 * C
STRIP = 256
ROUNDS = N // STRIP
AHEAD = 3
MIB = 1 << 20


def dot(a, b):
    return lax.dot_general(a, b, (((1,), (0,)), ((), ())), preferred_element_type=F32)


def dot_t(a, b):
    return lax.dot_general(a, b, (((0,), (0,)), ((), ())), preferred_element_type=F32)


def split(x):
    high = x.astype(BF16)
    low = (x - high.astype(F32)).astype(BF16)
    return high, low


def iota(shape, dim):
    return lax.broadcasted_iota(jnp.int32, shape, dim)


def one_hot(test):
    return jnp.where(test, 1.0, 0.0).astype(BF16)


def fold(x):
    return jnp.sum(x.reshape(-1, 8, x.shape[-1]), axis=0)


def column(row):
    tall = jnp.transpose(jnp.broadcast_to(row, (128, row.shape[1])))
    return jnp.concatenate([tall, tall], axis=1)


def primal_kernel(direc_hbm, coup_hbm, map_hbm, factor_hbm, pay_ref, direc, coup, corner, sems):
    copies = [
        pltpu.make_async_copy(coup_hbm, coup, sems.at[0]),
        pltpu.make_async_copy(direc_hbm.at[0], direc.at[0], sems.at[1]),
        pltpu.make_async_copy(direc_hbm.at[1], direc.at[1], sems.at[2]),
        pltpu.make_async_copy(map_hbm, corner, sems.at[3]),
        pltpu.make_async_copy(factor_hbm, pay_ref.at[pl.ds(2 * C, C)], sems.at[4]),
    ]
    for copy in copies:
        copy.start()
    pay_ref[3 * C :] = jnp.zeros((8, L), F32)
    copies[0].wait()
    for s in range(2):
        ch, cl = split(coup[s])
        copies[1 + s].wait()
        dh, dl = split(direc[s])
        pay_ref[s * C : (s + 1) * C] = dot(ch, dh) + dot(ch, dl) + dot(cl, dh)
    copies[3].wait()
    for s in range(2):
        pay_ref[3 * C + s : 3 * C + s + 1, 0:C] = corner[s].astype(F32)
    copies[4].wait()


def running_count(mask):
    total = mask.astype(jnp.int32)
    lane = iota(total.shape, 1)
    step = 1
    while step < total.shape[1]:
        total = total + jnp.where(lane >= step, pltpu.roll(total, step, 1), 0)
        step *= 2
    return total


def local_kernel(
    place_ref, pay_hbm, flex_hbm, direc_hbm, coup_hbm, partner_hbm,
    local_hbm, cross_hbm, near_hbm,
    flex, direc, coup, partner, local, packed, right, left, high, low, sems, out_sems,
):
    del pay_hbm
    strips = 2 * ROUNDS
    flex_copies, local_copies = [], []
    for t in range(strips):
        s, rows = t // ROUNDS, pl.ds((t % ROUNDS) * STRIP, STRIP)
        flex_copies.append(
            pltpu.make_async_copy(flex_hbm.at[s, rows], flex.at[s, rows], sems.at[t])
        )
        local_copies.append(
            pltpu.make_async_copy(local.at[s, rows], local_hbm.at[s, rows], out_sems.at[t])
        )
    others = [
        pltpu.make_async_copy(direc_hbm.at[0], direc.at[0], sems.at[strips]),
        pltpu.make_async_copy(direc_hbm.at[1], direc.at[1], sems.at[strips + 1]),
        pltpu.make_async_copy(coup_hbm, coup, sems.at[strips + 2]),
        pltpu.make_async_copy(partner_hbm, partner, sems.at[strips + 3]),
    ]
    others[0].start()
    flex_copies[0].start()
    others[1].start()
    for t in range(1, AHEAD):
        flex_copies[t].start()
    others[2].start()
    others[3].start()
    me = place_ref[0]
    odd = lax.rem(me, 2)
    for s in range(2):
        others[s].wait()
        dh, dl = split(direc[s])
        right[s, 0:N] = dh
        right[s, N:] = dl
    waited = False
    for t in range(strips + 1):
        if t < strips:
            s, start = t // ROUNDS, (t % ROUNDS) * STRIP
            flex_copies[t].wait()
            if t + AHEAD < strips:
                flex_copies[t + AHEAD].start()
            ah, al = split(flex[s, start : start + STRIP])
            left[t % 2, :, 0:N] = ah
            left[t % 2, :, N:] = al
        if t == 0:
            continue
        u = t - 1
        s, start = u // ROUNDS, (u % ROUNDS) * STRIP
        upper = left[u % 2, :, 0:N]
        out = dot(upper, right[s, 0:N]) + dot(upper, right[s, N:]) + dot(left[u % 2, :, N:], right[s, 0:N])
        local[s, start : start + STRIP] = out
        oh, ol = split(out)
        high[s, start : start + STRIP] = oh
        low[s, start : start + STRIP] = ol
        local_copies[u].start()
        if start + STRIP < N:
            continue
        if not waited:
            others[2].wait()
            others[3].wait()
            waited = True
        target = partner[s] - (2 * me - 1) * N
        match = (target >= 3 * N) if s else (target < N)
        key = jnp.where(match, running_count(match) - 1, -1)
        name = jnp.where(match, jnp.bitwise_and(target, N - 1) + 1, 0)
        coarse = lax.shift_right_logical(name, 5)
        fine = jnp.bitwise_and(name, 31)
        digits = jnp.concatenate(
            [coarse, fine, jnp.zeros((14, N), jnp.int32)], axis=0
        ).astype(F32).astype(BF16)
        ch, cl = split(coup[s])
        stack = jnp.concatenate([ch, cl, digits], axis=0)
        packed[s, NAMES:] = jnp.zeros((8, L), F32)
        for c in range(2):
            place = one_hot(iota((L, N), 0) + c * L == key)
            packed[s, c * L : (c + 1) * L] = dot(place, high[s]) + dot(place, low[s])
            extra = lax.dot_general(
                stack, place, (((1,), (1,)), ((), ())), preferred_element_type=F32
            )
            packed[s, HALF + c * C : HALF + (c + 1) * C] = extra[0:C] + extra[C : 2 * C]
            packed[s, NAMES + c : NAMES + c + 1] = (
                extra[2 * C : 2 * C + 1] * 32.0 + extra[2 * C + 1 : 2 * C + 2]
            )
    cross_copy = pltpu.make_async_copy(packed.at[odd], cross_hbm, out_sems.at[strips])
    near_copy = pltpu.make_async_copy(packed.at[1 - odd], near_hbm, out_sems.at[strips + 1])
    cross_copy.start()
    near_copy.start()
    for copy in local_copies:
        copy.wait()
    cross_copy.wait()
    near_copy.wait()


def selector(pay_ref):
    first = pay_ref[3 * C : 3 * C + 1, 0:C]
    second = pay_ref[3 * C + 1 : 3 * C + 2, 0:C]
    both = jnp.concatenate([first, second], axis=1).astype(jnp.int32)
    return one_hot(iota((L, 2 * C), 0) == both)


def coarse_kernel(place_ref, pay_ref, one_ref, two_ref, three_ref, cross_ref, near_ref):
    odd = lax.rem(place_ref[0], 2)
    members = (pay_ref, one_ref, two_ref, three_ref)
    sels, parts = [], []
    for member in members:
        sel = selector(member)
        ph, pl_ = split(member[0 : 2 * C])
        sels += [sel, sel]
        parts += [ph, pl_]
    rhs = dot(jnp.concatenate(sels, axis=1), jnp.concatenate(parts, axis=0))
    factor = jnp.concatenate([m[2 * C : 3 * C] for m in members], axis=0)
    fh, fl = split(factor)
    rh, rl = split(rhs)
    mid = dot(jnp.concatenate([fh, fh, fl], axis=1), jnp.concatenate([rh, rl, rh], axis=0))
    mh, ml = split(mid)
    sol = dot_t(jnp.concatenate([fh, fh, fl], axis=0), jnp.concatenate([mh, ml, mh], axis=0))
    sh, sl = split(sol)
    own = sels[0]
    picked = dot_t(jnp.concatenate([own, own], axis=0), jnp.concatenate([sh, sl], axis=0))

    @pl.when(odd == 0)
    def _():
        cross_ref[...] = picked[0:C]
        near_ref[...] = picked[C:]

    @pl.when(odd == 1)
    def _():
        near_ref[...] = picked[0:C]
        cross_ref[...] = picked[C:]


def inner_kernel(
    place_ref, local_ref, cross_ref, near_ref, coup_ref, direc_ref, resid_ref, weight_ref, partner_ref,
    jump_ref, sums_ref, image_ref, high, low,
):
    me = place_ref[0]
    odd = lax.rem(me, 2) == 1
    old = jnp.zeros((8, L), F32)
    curve = jnp.zeros((8, L), F32)
    mixed = jnp.zeros((8, L), F32)
    for s in range(2):
        ch, cl = split(coup_ref[s])
        qh, ql = split(jnp.where(odd == (s == 1), cross_ref[...], near_ref[...]))
        left = jnp.concatenate([ch, ch, cl], axis=0)
        right = jnp.concatenate([qh, ql, qh], axis=0)
        for r in range(0, N, L):
            image = local_ref[s, r : r + L] + dot_t(left[:, r : r + L], right)
            image_ref[s, r : r + L] = image
            ih, il = split(image)
            high[s, r : r + L] = ih
            low[s, r : r + L] = il
    for s in range(2):
        other = 1 - s
        theirs = partner_ref[other] - (2 * me + s) * N
        mine = partner_ref[s]
        awake = jnp.where(lax.shift_right_arithmetic(mine, 10) != 2 * me + s, 1.0, 0.0)
        for r in range(0, N, L):
            rows = slice(r, r + L)
            place = one_hot(iota((L, N), 0) + r == theirs)
            opposite = dot(place, high[other]) + dot(place, low[other])
            image = image_ref[s, rows]
            jump_ref[s, rows] = column(awake[:, rows]) * image - opposite
            scaled = column(weight_ref[s][:, rows]) * resid_ref[s, rows]
            old = old + fold(scaled * resid_ref[s, rows])
            curve = curve + fold(direc_ref[s, rows] * image)
            mixed = mixed + fold(scaled * image)
    sums_ref[0] = old
    sums_ref[1] = curve
    sums_ref[2] = mixed


def outer_kernel(
    place_ref, part_ref, cross_ref, near_ref, cross_pick_ref, near_pick_ref, weight_ref, sums_ref,
    jump_ref, total_ref,
):
    odd = lax.rem(place_ref[0], 2)
    square = jnp.zeros((8, L), F32)
    for ref, pick_ref, s in ((cross_ref, cross_pick_ref, odd), (near_ref, near_pick_ref, 1 - odd)):
        qh, ql = split(pick_ref[...])
        right = jnp.concatenate([qh, ql, qh], axis=0)
        highs, lows = [], []
        for c in range(2):
            ch, cl = split(ref[HALF + c * C : HALF + (c + 1) * C])
            left = jnp.concatenate([ch, ch, cl], axis=0)
            image_high, image_low = split(ref[c * L : (c + 1) * L] + dot_t(left, right))
            highs.append(image_high)
            lows.append(image_low)
        stacked = jnp.concatenate(highs + lows, axis=0)
        names = [ref[NAMES + c : NAMES + c + 1].astype(jnp.int32) for c in range(2)]
        for r in range(0, N, L):
            places = [one_hot(iota((L, L), 0) + (r + 1) == name) for name in names]
            opposite = dot(jnp.concatenate(places + places, axis=1), stacked)
            jump = part_ref[s, r : r + L] - opposite
            jump_ref[s, r : r + L] = jump
            square = square + fold(column(weight_ref[s][:, r : r + L]) * jump * jump)
    rows = [jnp.sum(x, axis=0, keepdims=True) for x in (sums_ref[0], sums_ref[1], sums_ref[2], square)]
    total_ref[...] = jnp.concatenate(rows + [jnp.zeros((4, L), F32)], axis=0)


def final_kernel(
    total_ref, weight_ref, lam_ref, resid_ref, direc_ref, jump_ref,
    lam_hbm, resid_hbm, direc_hbm, ratio_ref, lam_out, resid_out, direc_out, sems,
):
    old = total_ref[0:1]
    alpha = old / (2.0 * total_ref[1:2])
    new = old + alpha * (alpha * total_ref[3:4] - 4.0 * total_ref[2:3])
    ratio = new / old
    ratio_ref[...] = ratio
    copies = []
    for s in range(2):
        for r in range(4):
            rows = slice(r * L, (r + 1) * L)
            direc = direc_ref[s, rows]
            resid = resid_ref[s, rows] - alpha * jump_ref[s, rows]
            lam_out[s, rows] = lam_ref[s, rows] + alpha * direc
            resid_out[s, rows] = resid
            direc_out[s, rows] = column(weight_ref[s][:, rows]) * resid + ratio * direc
            piece = pl.ds(r * L, L)
            for k, (here, there) in enumerate(
                ((lam_out, lam_hbm), (resid_out, resid_hbm), (direc_out, direc_hbm))
            ):
                copy = pltpu.make_async_copy(
                    here.at[s, piece], there.at[s, piece], sems.at[(s * 4 + r) * 3 + k]
                )
                copy.start()
                copies.append(copy)
    for copy in copies:
        copy.wait()


def vmem():
    return pl.BlockSpec(memory_space=pltpu.VMEM)


def hbm():
    return pl.BlockSpec(memory_space=pltpu.HBM)


def smem():
    return pl.BlockSpec(memory_space=pltpu.SMEM)


def exchange(x, axes, size, route):
    pairs = []
    for i in range(size):
        j = route(i)
        if j is not None:
            pairs.append((i, j))
    return lax.ppermute(x, axes, pairs)


def per_device(
    flex, coupling, weight, iface_size, partner, corner_map, coarse_factor, lam, resid, direc
):
    del iface_size
    blocks, links, scale = flex[:, 0], coupling[:, 0], weight
    lam2, resid2, direc2 = lam[:, 0], resid[:, 0], direc[:, 0]
    chain = lax.axis_size("sub")
    place = lax.axis_index("sub").astype(jnp.int32).reshape(1)

    whole = jax.ShapeDtypeStruct((2, N, L), F32)
    pay = pl.pallas_call(
        primal_kernel,
        out_shape=jax.ShapeDtypeStruct((3 * C + 8, L), F32),
        in_specs=[hbm()] * 4,
        out_specs=vmem(),
        scratch_shapes=[
            pltpu.VMEM((2, N, L), F32),
            pltpu.VMEM((2, C, N), F32),
            pltpu.VMEM((2, 1, C), jnp.int32),
            pltpu.SemaphoreType.DMA((5,)),
        ],
        name="primal",
        compiler_params=pltpu.CompilerParams(vmem_limit_bytes=58 * MIB),
        cost_estimate=pl.CostEstimate(flops=200_000_000, bytes_accessed=3 * MIB, transcendentals=0),
    )(direc2, links, corner_map, coarse_factor[0])
    others = [exchange(pay, "grp", 4, lambda i, m=m: i ^ m) for m in (1, 3, 2)]

    packed = jax.ShapeDtypeStruct((NAMES + 8, L), F32)
    local, cross, near = pl.pallas_call(
        local_kernel,
        out_shape=(jax.ShapeDtypeStruct((2, N, L), F32), packed, packed),
        in_specs=[smem()] + [hbm()] * 5,
        out_specs=(hbm(), hbm(), hbm()),
        scratch_shapes=[
            pltpu.VMEM((2, N, N), F32),
            pltpu.VMEM((2, N, L), F32),
            pltpu.VMEM((2, C, N), F32),
            pltpu.VMEM((2, 1, N), jnp.int32),
            pltpu.VMEM((2, N, L), F32),
            pltpu.VMEM((2, NAMES + 8, L), F32),
            pltpu.VMEM((2, 2 * N, L), BF16),
            pltpu.VMEM((2, STRIP, 2 * N), BF16),
            pltpu.VMEM((2, N, L), BF16),
            pltpu.VMEM((2, N, L), BF16),
            pltpu.SemaphoreType.DMA((2 * ROUNDS + 4,)),
            pltpu.SemaphoreType.DMA((2 * ROUNDS + 2,)),
        ],
        name="local",
        compiler_params=pltpu.CompilerParams(vmem_limit_bytes=58 * MIB),
        cost_estimate=pl.CostEstimate(flops=4_000_000_000, bytes_accessed=12 * MIB, transcendentals=0),
    )(place, pay, blocks, direc2, links, partner)

    def across(i):
        j = i + 1 if i % 2 else i - 1
        return j if 0 <= j < chain else None

    def beside(i):
        return i ^ 1

    got_cross = exchange(cross, "sub", chain, across)
    got_near = exchange(near, "sub", chain, beside)

    piece = jax.ShapeDtypeStruct((C, L), F32)
    cross_pick, near_pick = pl.pallas_call(
        coarse_kernel,
        out_shape=(piece, piece),
        in_specs=[smem()] + [vmem()] * 4,
        out_specs=(vmem(), vmem()),
        name="coarse",
        compiler_params=pltpu.CompilerParams(vmem_limit_bytes=16 * MIB),
        cost_estimate=pl.CostEstimate(flops=30_000_000_000, bytes_accessed=MIB, transcendentals=0),
    )(place, pay, *others)
    got_cross_pick = exchange(cross_pick, "sub", chain, across)
    got_near_pick = exchange(near_pick, "sub", chain, beside)

    part, sums = pl.pallas_call(
        inner_kernel,
        out_shape=(whole, jax.ShapeDtypeStruct((3, 8, L), F32)),
        in_specs=[smem()] + [vmem()] * 8,
        out_specs=(vmem(), vmem()),
        scratch_shapes=[
            pltpu.VMEM((2, N, L), F32),
            pltpu.VMEM((2, N, L), BF16),
            pltpu.VMEM((2, N, L), BF16),
        ],
        name="inner",
        compiler_params=pltpu.CompilerParams(vmem_limit_bytes=24 * MIB),
        cost_estimate=pl.CostEstimate(flops=2_500_000_000, bytes_accessed=8 * MIB, transcendentals=0),
    )(place, local, cross_pick, near_pick, links, direc2, resid2, scale, partner)

    jump, total = pl.pallas_call(
        outer_kernel,
        out_shape=(whole, jax.ShapeDtypeStruct((8, L), F32)),
        in_specs=[smem()] + [vmem()] * 7,
        out_specs=(vmem(), vmem()),
        name="outer",
        compiler_params=pltpu.CompilerParams(vmem_limit_bytes=24 * MIB),
    )(place, part, got_cross, got_near, got_cross_pick, got_near_pick, scale, sums)

    total = total + exchange(total, "sub", chain, beside)
    for m in (1, 3):
        total = total + exchange(total, "grp", 4, lambda i, m=m: i ^ m)
    for bit in (2, 8):
        for m in (1, 3):
            total = total + exchange(total, "sub", chain, lambda i, m=m, bit=bit: i ^ (m * bit))

    lam_next, resid_next, direc_next, ratio = pl.pallas_call(
        final_kernel,
        out_shape=(whole, whole, whole, jax.ShapeDtypeStruct((1, L), F32)),
        in_specs=[vmem()] * 6,
        out_specs=(hbm(), hbm(), hbm(), vmem()),
        scratch_shapes=[pltpu.VMEM((2, N, L), F32)] * 3 + [pltpu.SemaphoreType.DMA((24,))],
        name="final",
        compiler_params=pltpu.CompilerParams(vmem_limit_bytes=24 * MIB),
    )(total, scale, lam2, resid2, direc2, jump)
    return (lam_next[:, None], resid_next[:, None], direc_next[:, None], ratio[0])


def solution(mesh):
    placed = (
        P("sub", "grp", None, None),
        P("sub", "grp", None, None),
        P("sub", "grp", None),
        P("sub", "grp"),
        P("sub", "grp", None),
        P("sub", "grp", None),
        P("sub", "grp", None),
        P("sub", "grp", None, None),
        P("sub", "grp", None, None),
        P("sub", "grp", None, None),
    )
    return jax.shard_map(
        per_device,
        mesh=mesh,
        in_specs=placed,
        out_specs=(
            P("sub", "grp", None, None),
            P("sub", "grp", None, None),
            P("sub", "grp", None, None),
            P(),
        ),
        check_vma=False,
    )
```

```python
import functools

import jax
import jax.numpy as jnp
from jax import lax
from jax.experimental import pallas as pl
from jax.experimental.pallas import tpu as pltpu
from jax.sharding import PartitionSpec as P

F32 = jnp.float32
BF16 = jnp.bfloat16
N = 1024
L = 256
C = 64
HALF = 512
NAMES = HALF + 2 * C
STRIP = 512
ROUNDS = N // STRIP
MIB = 1 << 20


def dot(a, b):
    return lax.dot_general(a, b, (((1,), (0,)), ((), ())), preferred_element_type=F32)


def dot_t(a, b):
    return lax.dot_general(a, b, (((0,), (0,)), ((), ())), preferred_element_type=F32)


def split(x):
    high = x.astype(BF16)
    low = (x - high.astype(F32)).astype(BF16)
    return high, low


def iota(shape, dim):
    return lax.broadcasted_iota(jnp.int32, shape, dim)


def one_hot(test):
    return jnp.where(test, 1.0, 0.0).astype(BF16)


def fold(x):
    return jnp.sum(x.reshape(-1, 8, x.shape[-1]), axis=0)


def column(row):
    tall = jnp.transpose(jnp.broadcast_to(row, (128, row.shape[1])))
    return jnp.concatenate([tall, tall], axis=1)


def primal_kernel(direc_hbm, coup_hbm, map_hbm, factor_hbm, pay_ref, direc, coup, corner, sems):
    copies = [
        pltpu.make_async_copy(coup_hbm, coup, sems.at[0]),
        pltpu.make_async_copy(direc_hbm.at[0], direc.at[0], sems.at[1]),
        pltpu.make_async_copy(direc_hbm.at[1], direc.at[1], sems.at[2]),
        pltpu.make_async_copy(map_hbm, corner, sems.at[3]),
        pltpu.make_async_copy(factor_hbm, pay_ref.at[pl.ds(2 * C, C)], sems.at[4]),
    ]
    for copy in copies:
        copy.start()
    pay_ref[3 * C :] = jnp.zeros((8, L), F32)
    for copy in copies:
        copy.wait()
    for s in range(2):
        ch, cl = split(coup[s])
        dh, dl = split(direc[s])
        pay_ref[s * C : (s + 1) * C] = dot(ch, dh) + dot(ch, dl) + dot(cl, dh)
        pay_ref[3 * C + s : 3 * C + s + 1, 0:C] = corner[s].astype(F32)


def running_count(mask):
    total = mask.astype(jnp.int32)
    lane = iota(total.shape, 1)
    step = 1
    while step < total.shape[1]:
        total = total + jnp.where(lane >= step, pltpu.roll(total, step, 1), 0)
        step *= 2
    return total


def local_kernel(
    place_ref, pay_hbm, flex_hbm, direc_hbm, coup_hbm, partner_hbm,
    local_hbm, cross_hbm, near_hbm,
    flex, direc, coup, partner, local, packed, right, high, low, sems, out_sems,
):
    del pay_hbm
    direc_copy = pltpu.make_async_copy(direc_hbm, direc, sems.at[0])
    flex_copies = [
        pltpu.make_async_copy(flex_hbm.at[s], flex.at[s], sems.at[1 + s]) for s in range(2)
    ]
    others = [
        pltpu.make_async_copy(coup_hbm, coup, sems.at[3]),
        pltpu.make_async_copy(partner_hbm, partner, sems.at[4]),
    ]
    out_copies = [
        pltpu.make_async_copy(local.at[s], local_hbm.at[s], out_sems.at[s]) for s in range(2)
    ]
    direc_copy.start()
    for copy in flex_copies + others:
        copy.start()
    me = place_ref[0]
    odd = lax.rem(me, 2)
    direc_copy.wait()
    for s in range(2):
        dh, dl = split(direc[s])
        right[s, 0:N] = dh
        right[s, N:] = dl
    flex_copies[0].wait()
    for s in range(2):
        if s == 1:
            out_copies[0].start()
            flex_copies[1].wait()
            for copy in others:
                copy.wait()
        for r in range(ROUNDS):
            rows = slice(r * STRIP, (r + 1) * STRIP)
            ah, al = split(flex[s, rows])
            out = dot(ah, right[s, 0:N]) + dot(ah, right[s, N:]) + dot(al, right[s, 0:N])
            local[s, rows] = out
            oh, ol = split(out)
            high[s, rows] = oh
            low[s, rows] = ol
    out_copies[1].start()
    for s in range(2):
        target = partner[s] - (2 * me - 1) * N
        match = (target >= 3 * N) if s else (target < N)
        key = jnp.where(match, running_count(match) - 1, -1)
        name = jnp.where(match, jnp.bitwise_and(target, N - 1) + 1, 0)
        coarse = lax.shift_right_logical(name, 5)
        fine = jnp.bitwise_and(name, 31)
        digits = jnp.concatenate(
            [coarse, fine, jnp.zeros((14, N), jnp.int32)], axis=0
        ).astype(F32).astype(BF16)
        ch, cl = split(coup[s])
        stack = jnp.concatenate([ch, cl, digits], axis=0)
        packed[s, NAMES:] = jnp.zeros((8, L), F32)
        for c in range(2):
            place = one_hot(iota((L, N), 0) + c * L == key)
            packed[s, c * L : (c + 1) * L] = dot(place, high[s]) + dot(place, low[s])
            extra = lax.dot_general(
                stack, place, (((1,), (1,)), ((), ())), preferred_element_type=F32
            )
            packed[s, HALF + c * C : HALF + (c + 1) * C] = extra[0:C] + extra[C : 2 * C]
            packed[s, NAMES + c : NAMES + c + 1] = (
                extra[2 * C : 2 * C + 1] * 32.0 + extra[2 * C + 1 : 2 * C + 2]
            )
    cross_copy = pltpu.make_async_copy(packed.at[odd], cross_hbm, out_sems.at[2])
    near_copy = pltpu.make_async_copy(packed.at[1 - odd], near_hbm, out_sems.at[3])
    cross_copy.start()
    near_copy.start()
    for copy in out_copies:
        copy.wait()
    cross_copy.wait()
    near_copy.wait()


def selector(pay_ref):
    first = pay_ref[3 * C : 3 * C + 1, 0:C]
    second = pay_ref[3 * C + 1 : 3 * C + 2, 0:C]
    both = jnp.concatenate([first, second], axis=1).astype(jnp.int32)
    return one_hot(iota((L, 2 * C), 0) == both)


def coarse_kernel(place_ref, pay_ref, one_ref, two_ref, three_ref, cross_ref, near_ref):
    odd = lax.rem(place_ref[0], 2)
    members = (pay_ref, one_ref, two_ref, three_ref)
    sels, parts = [], []
    for member in members:
        sel = selector(member)
        ph, pl_ = split(member[0 : 2 * C])
        sels += [sel, sel]
        parts += [ph, pl_]
    rhs = dot(jnp.concatenate(sels, axis=1), jnp.concatenate(parts, axis=0))
    factor = jnp.concatenate([m[2 * C : 3 * C] for m in members], axis=0)
    fh, fl = split(factor)
    rh, rl = split(rhs)
    mid = dot(jnp.concatenate([fh, fh, fl], axis=1), jnp.concatenate([rh, rl, rh], axis=0))
    mh, ml = split(mid)
    sol = dot_t(jnp.concatenate([fh, fh, fl], axis=0), jnp.concatenate([mh, ml, mh], axis=0))
    sh, sl = split(sol)
    own = sels[0]
    picked = dot_t(jnp.concatenate([own, own], axis=0), jnp.concatenate([sh, sl], axis=0))

    @pl.when(odd == 0)
    def _():
        cross_ref[...] = picked[0:C]
        near_ref[...] = picked[C:]

    @pl.when(odd == 1)
    def _():
        near_ref[...] = picked[0:C]
        cross_ref[...] = picked[C:]


def inner_kernel(
    place_ref, local_ref, cross_ref, near_ref, coup_ref, direc_ref, resid_ref, weight_ref, partner_ref,
    jump_ref, sums_ref, image_ref, high, low,
):
    me = place_ref[0]
    odd = lax.rem(me, 2) == 1
    old = jnp.zeros((8, L), F32)
    curve = jnp.zeros((8, L), F32)
    mixed = jnp.zeros((8, L), F32)
    for s in range(2):
        ch, cl = split(coup_ref[s])
        qh, ql = split(jnp.where(odd == (s == 1), cross_ref[...], near_ref[...]))
        left = jnp.concatenate([ch, ch, cl], axis=0)
        right = jnp.concatenate([qh, ql, qh], axis=0)
        for r in range(0, N, L):
            image = local_ref[s, r : r + L] + dot_t(left[:, r : r + L], right)
            image_ref[s, r : r + L] = image
            ih, il = split(image)
            high[s, r : r + L] = ih
            low[s, r : r + L] = il
    for s in range(2):
        other = 1 - s
        theirs = partner_ref[other] - (2 * me + s) * N
        mine = partner_ref[s]
        awake = jnp.where(lax.shift_right_arithmetic(mine, 10) != 2 * me + s, 1.0, 0.0)
        for r in range(0, N, L):
            rows = slice(r, r + L)
            place = one_hot(iota((L, N), 0) + r == theirs)
            opposite = dot(place, high[other]) + dot(place, low[other])
            image = image_ref[s, rows]
            jump_ref[s, rows] = column(awake[:, rows]) * image - opposite
            scaled = column(weight_ref[s][:, rows]) * resid_ref[s, rows]
            old = old + fold(scaled * resid_ref[s, rows])
            curve = curve + fold(direc_ref[s, rows] * image)
            mixed = mixed + fold(scaled * image)
    sums_ref[0] = old
    sums_ref[1] = curve
    sums_ref[2] = mixed


def outer_kernel(
    place_ref, part_ref, cross_ref, near_ref, cross_pick_ref, near_pick_ref, weight_ref, sums_ref,
    jump_ref, total_ref,
):
    odd = lax.rem(place_ref[0], 2)
    square = jnp.zeros((8, L), F32)
    for ref, pick_ref, s in ((cross_ref, cross_pick_ref, odd), (near_ref, near_pick_ref, 1 - odd)):
        qh, ql = split(pick_ref[...])
        right = jnp.concatenate([qh, ql, qh], axis=0)
        highs, lows = [], []
        for c in range(2):
            ch, cl = split(ref[HALF + c * C : HALF + (c + 1) * C])
            left = jnp.concatenate([ch, ch, cl], axis=0)
            image_high, image_low = split(ref[c * L : (c + 1) * L] + dot_t(left, right))
            highs.append(image_high)
            lows.append(image_low)
        stacked = jnp.concatenate(highs + lows, axis=0)
        names = [ref[NAMES + c : NAMES + c + 1].astype(jnp.int32) for c in range(2)]
        for r in range(0, N, L):
            places = [one_hot(iota((L, L), 0) + (r + 1) == name) for name in names]
            opposite = dot(jnp.concatenate(places + places, axis=1), stacked)
            jump = part_ref[s, r : r + L] - opposite
            jump_ref[s, r : r + L] = jump
            square = square + fold(column(weight_ref[s][:, r : r + L]) * jump * jump)
    rows = [jnp.sum(x, axis=0, keepdims=True) for x in (sums_ref[0], sums_ref[1], sums_ref[2], square)]
    total_ref[...] = jnp.concatenate(rows + [jnp.zeros((4, L), F32)], axis=0)


def final_kernel(
    total_ref, weight_ref, lam_ref, resid_ref, direc_ref, jump_ref,
    lam_hbm, resid_hbm, direc_hbm, ratio_ref, lam_out, resid_out, direc_out, sems,
):
    old = total_ref[0:1]
    alpha = old / (2.0 * total_ref[1:2])
    new = old + alpha * (alpha * total_ref[3:4] - 4.0 * total_ref[2:3])
    ratio = new / old
    ratio_ref[...] = ratio
    copies = []
    for s in range(2):
        for r in range(4):
            rows = slice(r * L, (r + 1) * L)
            direc = direc_ref[s, rows]
            resid = resid_ref[s, rows] - alpha * jump_ref[s, rows]
            lam_out[s, rows] = lam_ref[s, rows] + alpha * direc
            resid_out[s, rows] = resid
            direc_out[s, rows] = column(weight_ref[s][:, rows]) * resid + ratio * direc
            piece = pl.ds(r * L, L)
            for k, (here, there) in enumerate(
                ((lam_out, lam_hbm), (resid_out, resid_hbm), (direc_out, direc_hbm))
            ):
                copy = pltpu.make_async_copy(
                    here.at[s, piece], there.at[s, piece], sems.at[(s * 4 + r) * 3 + k]
                )
                copy.start()
                copies.append(copy)
    for copy in copies:
        copy.wait()


def vmem():
    return pl.BlockSpec(memory_space=pltpu.VMEM)


def hbm():
    return pl.BlockSpec(memory_space=pltpu.HBM)


def smem():
    return pl.BlockSpec(memory_space=pltpu.SMEM)


def exchange(x, axes, size, route):
    pairs = []
    for i in range(size):
        j = route(i)
        if j is not None:
            pairs.append((i, j))
    return lax.ppermute(x, axes, pairs)


def per_device(
    flex, coupling, weight, iface_size, partner, corner_map, coarse_factor, lam, resid, direc
):
    del iface_size
    blocks, links, scale = flex[:, 0], coupling[:, 0], weight
    lam2, resid2, direc2 = lam[:, 0], resid[:, 0], direc[:, 0]
    chain = lax.axis_size("sub")
    place = lax.axis_index("sub").astype(jnp.int32).reshape(1)

    whole = jax.ShapeDtypeStruct((2, N, L), F32)
    pay = pl.pallas_call(
        primal_kernel,
        out_shape=jax.ShapeDtypeStruct((3 * C + 8, L), F32),
        in_specs=[hbm()] * 4,
        out_specs=vmem(),
        scratch_shapes=[
            pltpu.VMEM((2, N, L), F32),
            pltpu.VMEM((2, C, N), F32),
            pltpu.VMEM((2, 1, C), jnp.int32),
            pltpu.SemaphoreType.DMA((5,)),
        ],
        name="primal",
        compiler_params=pltpu.CompilerParams(vmem_limit_bytes=58 * MIB),
        cost_estimate=pl.CostEstimate(flops=200_000_000, bytes_accessed=3 * MIB, transcendentals=0),
    )(direc2, links, corner_map, coarse_factor[0])
    others = [exchange(pay, "grp", 4, lambda i, m=m: i ^ m) for m in (1, 3, 2)]

    packed = jax.ShapeDtypeStruct((NAMES + 8, L), F32)
    local, cross, near = pl.pallas_call(
        local_kernel,
        out_shape=(jax.ShapeDtypeStruct((2, N, L), F32), packed, packed),
        in_specs=[smem()] + [hbm()] * 5,
        out_specs=(hbm(), hbm(), hbm()),
        scratch_shapes=[
            pltpu.VMEM((2, N, N), F32),
            pltpu.VMEM((2, N, L), F32),
            pltpu.VMEM((2, C, N), F32),
            pltpu.VMEM((2, 1, N), jnp.int32),
            pltpu.VMEM((2, N, L), F32),
            pltpu.VMEM((2, NAMES + 8, L), F32),
            pltpu.VMEM((2, 2 * N, L), BF16),
            pltpu.VMEM((2, N, L), BF16),
            pltpu.VMEM((2, N, L), BF16),
            pltpu.SemaphoreType.DMA((5,)),
            pltpu.SemaphoreType.DMA((4,)),
        ],
        name="local",
        compiler_params=pltpu.CompilerParams(vmem_limit_bytes=58 * MIB),
        cost_estimate=pl.CostEstimate(flops=4_000_000_000, bytes_accessed=12 * MIB, transcendentals=0),
    )(place, pay, blocks, direc2, links, partner)

    def across(i):
        j = i + 1 if i % 2 else i - 1
        return j if 0 <= j < chain else None

    def beside(i):
        return i ^ 1

    got_cross = exchange(cross, "sub", chain, across)
    got_near = exchange(near, "sub", chain, beside)

    piece = jax.ShapeDtypeStruct((C, L), F32)
    cross_pick, near_pick = pl.pallas_call(
        coarse_kernel,
        out_shape=(piece, piece),
        in_specs=[smem()] + [vmem()] * 4,
        out_specs=(vmem(), vmem()),
        name="coarse",
        compiler_params=pltpu.CompilerParams(vmem_limit_bytes=16 * MIB),
        cost_estimate=pl.CostEstimate(flops=30_000_000_000, bytes_accessed=MIB, transcendentals=0),
    )(place, pay, *others)
    got_cross_pick = exchange(cross_pick, "sub", chain, across)
    got_near_pick = exchange(near_pick, "sub", chain, beside)

    part, sums = pl.pallas_call(
        inner_kernel,
        out_shape=(whole, jax.ShapeDtypeStruct((3, 8, L), F32)),
        in_specs=[smem()] + [vmem()] * 8,
        out_specs=(vmem(), vmem()),
        scratch_shapes=[
            pltpu.VMEM((2, N, L), F32),
            pltpu.VMEM((2, N, L), BF16),
            pltpu.VMEM((2, N, L), BF16),
        ],
        name="inner",
        compiler_params=pltpu.CompilerParams(vmem_limit_bytes=24 * MIB),
        cost_estimate=pl.CostEstimate(flops=2_500_000_000, bytes_accessed=8 * MIB, transcendentals=0),
    )(place, local, cross_pick, near_pick, links, direc2, resid2, scale, partner)

    jump, total = pl.pallas_call(
        outer_kernel,
        out_shape=(whole, jax.ShapeDtypeStruct((8, L), F32)),
        in_specs=[smem()] + [vmem()] * 7,
        out_specs=(vmem(), vmem()),
        name="outer",
        compiler_params=pltpu.CompilerParams(vmem_limit_bytes=24 * MIB),
    )(place, part, got_cross, got_near, got_cross_pick, got_near_pick, scale, sums)

    total = total + exchange(total, "sub", chain, beside)
    both = ("sub", "grp")
    size = 4 * chain
    for near_bit, far_bit in (((4 * 8, 1)), ((3 * 4 * 8, 3)), ((4 * 2, 3 * 4 * 2))):
        flips = (near_bit, far_bit, near_bit ^ far_bit)
        total = total + sum(exchange(total, both, size, lambda i, m=m: i ^ m) for m in flips)

    lam_next, resid_next, direc_next, ratio = pl.pallas_call(
        final_kernel,
        out_shape=(whole, whole, whole, jax.ShapeDtypeStruct((1, L), F32)),
        in_specs=[vmem()] * 6,
        out_specs=(hbm(), hbm(), hbm(), vmem()),
        scratch_shapes=[pltpu.VMEM((2, N, L), F32)] * 3 + [pltpu.SemaphoreType.DMA((24,))],
        name="final",
        compiler_params=pltpu.CompilerParams(vmem_limit_bytes=24 * MIB),
    )(total, scale, lam2, resid2, direc2, jump)
    return (lam_next[:, None], resid_next[:, None], direc_next[:, None], ratio[0])


def solution(mesh):
    placed = (
        P("sub", "grp", None, None),
        P("sub", "grp", None, None),
        P("sub", "grp", None),
        P("sub", "grp"),
        P("sub", "grp", None),
        P("sub", "grp", None),
        P("sub", "grp", None),
        P("sub", "grp", None, None),
        P("sub", "grp", None, None),
        P("sub", "grp", None, None),
    )
    return jax.shard_map(
        per_device,
        mesh=mesh,
        in_specs=placed,
        out_specs=(
            P("sub", "grp", None, None),
            P("sub", "grp", None, None),
            P("sub", "grp", None, None),
            P(),
        ),
        check_vma=False,
    )
```

```python
import functools

import jax
import jax.numpy as jnp
from jax import lax
from jax.experimental import pallas as pl
from jax.experimental.pallas import tpu as pltpu
from jax.sharding import PartitionSpec as P

F32 = jnp.float32
BF16 = jnp.bfloat16
N = 1024
L = 256
C = 64
HALF = 512
NAMES = HALF + 2 * C
STRIP = 512
ROUNDS = N // STRIP
MIB = 1 << 20


def dot(a, b):
    return lax.dot_general(a, b, (((1,), (0,)), ((), ())), preferred_element_type=F32)


def dot_t(a, b):
    return lax.dot_general(a, b, (((0,), (0,)), ((), ())), preferred_element_type=F32)


def split(x):
    high = x.astype(BF16)
    low = (x - high.astype(F32)).astype(BF16)
    return high, low


def iota(shape, dim):
    return lax.broadcasted_iota(jnp.int32, shape, dim)


def one_hot(test):
    return jnp.where(test, 1.0, 0.0).astype(BF16)


def fold(x):
    return jnp.sum(x.reshape(-1, 8, x.shape[-1]), axis=0)


def column(row):
    tall = jnp.transpose(jnp.broadcast_to(row, (128, row.shape[1])))
    return jnp.concatenate([tall, tall], axis=1)


def running_count(mask):
    total = mask.astype(jnp.int32)
    lane = iota(total.shape, 1)
    step = 1
    while step < total.shape[1]:
        total = total + jnp.where(lane >= step, pltpu.roll(total, step, 1), 0)
        step *= 2
    return total


def local_kernel(
    place_ref, flex_hbm, direc_hbm, coup_hbm, partner_hbm, map_hbm, factor_hbm,
    pay_hbm, local_hbm, cross_hbm, near_hbm,
    flex, direc, coup, partner, corner, pay, local, packed, right, high, low, sems, out_sems,
):
    first = [
        pltpu.make_async_copy(direc_hbm, direc, sems.at[0]),
        pltpu.make_async_copy(coup_hbm, coup, sems.at[1]),
        pltpu.make_async_copy(map_hbm, corner, sems.at[2]),
        pltpu.make_async_copy(factor_hbm, pay.at[pl.ds(2 * C, C)], sems.at[3]),
        pltpu.make_async_copy(partner_hbm, partner, sems.at[4]),
    ]
    flex_copies = [
        pltpu.make_async_copy(flex_hbm.at[s], flex.at[s], sems.at[5 + s]) for s in range(2)
    ]
    out_copies = [
        pltpu.make_async_copy(local.at[s], local_hbm.at[s], out_sems.at[s]) for s in range(2)
    ]
    pay_copy = pltpu.make_async_copy(pay, pay_hbm, out_sems.at[4])
    for copy in first + flex_copies:
        copy.start()
    me = place_ref[0]
    odd = lax.rem(me, 2)
    pay[3 * C :] = jnp.zeros((8, L), F32)
    for copy in first:
        copy.wait()
    for s in range(2):
        dh, dl = split(direc[s])
        right[s, 0:N] = dh
        right[s, N:] = dl
        ch, cl = split(coup[s])
        pay[s * C : (s + 1) * C] = dot(ch, dh) + dot(ch, dl) + dot(cl, dh)
        pay[3 * C + s : 3 * C + s + 1, 0:C] = corner[s].astype(F32)
    pay_copy.start()
    flex_copies[0].wait()
    for s in range(2):
        if s == 1:
            out_copies[0].start()
            flex_copies[1].wait()
        for r in range(ROUNDS):
            rows = slice(r * STRIP, (r + 1) * STRIP)
            ah, al = split(flex[s, rows])
            out = dot(ah, right[s, 0:N]) + dot(ah, right[s, N:]) + dot(al, right[s, 0:N])
            local[s, rows] = out
            oh, ol = split(out)
            high[s, rows] = oh
            low[s, rows] = ol
    for s in range(2):
        target = partner[s] - (2 * me - 1) * N
        match = (target >= 3 * N) if s else (target < N)
        key = jnp.where(match, running_count(match) - 1, -1)
        name = jnp.where(match, jnp.bitwise_and(target, N - 1) + 1, 0)
        coarse = lax.shift_right_logical(name, 5)
        fine = jnp.bitwise_and(name, 31)
        digits = jnp.concatenate(
            [coarse, fine, jnp.zeros((14, N), jnp.int32)], axis=0
        ).astype(F32).astype(BF16)
        ch, cl = split(coup[s])
        stack = jnp.concatenate([ch, cl, digits], axis=0)
        packed[s, NAMES:] = jnp.zeros((8, L), F32)
        for c in range(2):
            place = one_hot(iota((L, N), 0) + c * L == key)
            packed[s, c * L : (c + 1) * L] = dot(place, high[s]) + dot(place, low[s])
            extra = lax.dot_general(
                stack, place, (((1,), (1,)), ((), ())), preferred_element_type=F32
            )
            packed[s, HALF + c * C : HALF + (c + 1) * C] = extra[0:C] + extra[C : 2 * C]
            packed[s, NAMES + c : NAMES + c + 1] = (
                extra[2 * C : 2 * C + 1] * 32.0 + extra[2 * C + 1 : 2 * C + 2]
            )
    cross_copy = pltpu.make_async_copy(packed.at[odd], cross_hbm, out_sems.at[2])
    near_copy = pltpu.make_async_copy(packed.at[1 - odd], near_hbm, out_sems.at[3])
    cross_copy.start()
    near_copy.start()
    out_copies[1].start()
    for copy in out_copies:
        copy.wait()
    pay_copy.wait()
    cross_copy.wait()
    near_copy.wait()


def selector(pay_ref):
    first = pay_ref[3 * C : 3 * C + 1, 0:C]
    second = pay_ref[3 * C + 1 : 3 * C + 2, 0:C]
    both = jnp.concatenate([first, second], axis=1).astype(jnp.int32)
    return one_hot(iota((L, 2 * C), 0) == both)


def coarse_kernel(place_ref, pay_ref, one_ref, two_ref, three_ref, mix_hbm, cross_ref, near_ref):
    del mix_hbm
    odd = lax.rem(place_ref[0], 2)
    members = (pay_ref, one_ref, two_ref, three_ref)
    sels, parts = [], []
    for member in members:
        sel = selector(member)
        ph, pl_ = split(member[0 : 2 * C])
        sels += [sel, sel]
        parts += [ph, pl_]
    rhs = dot(jnp.concatenate(sels, axis=1), jnp.concatenate(parts, axis=0))
    factor = jnp.concatenate([m[2 * C : 3 * C] for m in members], axis=0)
    fh, fl = split(factor)
    rh, rl = split(rhs)
    mid = dot(jnp.concatenate([fh, fh, fl], axis=1), jnp.concatenate([rh, rl, rh], axis=0))
    mh, ml = split(mid)
    sol = dot_t(jnp.concatenate([fh, fh, fl], axis=0), jnp.concatenate([mh, ml, mh], axis=0))
    sh, sl = split(sol)
    own = sels[0]
    picked = dot_t(jnp.concatenate([own, own], axis=0), jnp.concatenate([sh, sl], axis=0))

    @pl.when(odd == 0)
    def _():
        cross_ref[...] = picked[0:C]
        near_ref[...] = picked[C:]

    @pl.when(odd == 1)
    def _():
        near_ref[...] = picked[0:C]
        cross_ref[...] = picked[C:]


def inner_kernel(place_ref, local_ref, coup_ref, partner_ref, part_ref, mix_ref, high, low):
    me = place_ref[0]
    stacks = []
    for s in range(2):
        ch, cl = split(coup_ref[s])
        stacks.append(jnp.concatenate([ch, cl], axis=0))
        for r in range(0, N, L):
            lh, ll = split(local_ref[s, r : r + L])
            high[s, r : r + L] = lh
            low[s, r : r + L] = ll
    for s in range(2):
        other = 1 - s
        theirs = partner_ref[other] - (2 * me + s) * N
        mine = partner_ref[s]
        awake = jnp.where(lax.shift_right_arithmetic(mine, 10) != 2 * me + s, 1.0, 0.0)
        mix_ref[s, 0:C] = coup_ref[s] * awake
        for r in range(0, N, L):
            rows = slice(r, r + L)
            place = one_hot(iota((L, N), 0) + r == theirs)
            opposite = dot(place, high[other]) + dot(place, low[other])
            part_ref[s, rows] = column(awake[:, rows]) * local_ref[s, rows] - opposite
            moved = lax.dot_general(
                stacks[other], place, (((1,), (1,)), ((), ())), preferred_element_type=F32
            )
            mix_ref[s, C:, rows] = -(moved[0:C] + moved[C:])


def triple(x, first):
    high, low = split(x)
    return jnp.concatenate([high, high, low] if first else [high, low, high], axis=0)


def outer_kernel(
    place_ref, part_ref, mix_ref, cross_ref, near_ref, cross_pick_ref, near_pick_ref,
    own_cross_ref, own_near_ref, weight_ref, resid_ref, direc_ref,
    jump_ref, total_ref, images, rows_ref,
):
    is_odd = lax.rem(place_ref[0], 2) == 1
    for k, (ref, pick_ref) in enumerate(((cross_ref, cross_pick_ref), (near_ref, near_pick_ref))):
        right = triple(pick_ref[...], False)
        for c in range(2):
            left = triple(ref[HALF + c * C : HALF + (c + 1) * C], True)
            image_high, image_low = split(ref[c * L : (c + 1) * L] + dot_t(left, right))
            images[k, c * L : (c + 1) * L] = image_high
            images[k, HALF + c * L : HALF + (c + 1) * L] = image_low
            rows_ref[k, c : c + 1] = ref[NAMES + c : NAMES + c + 1].astype(jnp.int32)
    flip = is_odd.astype(jnp.int32)
    picks = (
        jnp.where(is_odd, own_near_ref[...], own_cross_ref[...]),
        jnp.where(is_odd, own_cross_ref[...], own_near_ref[...]),
    )
    sums = [jnp.zeros((8, L), F32)] * 4
    for s in range(2):
        k = flip if s == 0 else 1 - flip
        stacked = images[k]
        names = [rows_ref[k, c : c + 1] for c in range(2)]
        right = triple(jnp.concatenate([picks[s], picks[1 - s]], axis=0), False)
        left = triple(mix_ref[s], True)
        for r in range(0, N, L):
            rows = slice(r, r + L)
            places = [one_hot(iota((L, L), 0) + (r + 1) == name) for name in names]
            opposite = dot(jnp.concatenate(places + places, axis=1), stacked)
            jump = part_ref[s, rows] + dot_t(left[:, rows], right) - opposite
            jump_ref[s, rows] = jump
            resid = resid_ref[s, rows]
            scale = column(weight_ref[s][:, rows])
            scaled = scale * resid
            terms = (scaled * resid, direc_ref[s, rows] * jump, scaled * jump, scale * jump * jump)
            sums = [total + fold(term) for total, term in zip(sums, terms)]
    lines = [jnp.sum(x, axis=0, keepdims=True) for x in sums]
    total_ref[...] = jnp.concatenate(lines + [jnp.zeros((4, L), F32)], axis=0)


def final_kernel(
    total_ref, weight_ref, lam_ref, resid_ref, direc_ref, jump_ref,
    lam_hbm, resid_hbm, direc_hbm, ratio_ref, lam_out, resid_out, direc_out, sems,
):
    old = total_ref[0:1]
    alpha = old / total_ref[1:2]
    new = old + alpha * (alpha * total_ref[3:4] - 2.0 * total_ref[2:3])
    ratio = new / old
    ratio_ref[...] = ratio
    copies = []
    for s in range(2):
        for r in range(4):
            rows = slice(r * L, (r + 1) * L)
            direc = direc_ref[s, rows]
            resid = resid_ref[s, rows] - alpha * jump_ref[s, rows]
            lam_out[s, rows] = lam_ref[s, rows] + alpha * direc
            resid_out[s, rows] = resid
            direc_out[s, rows] = column(weight_ref[s][:, rows]) * resid + ratio * direc
            piece = pl.ds(r * L, L)
            for k, (here, there) in enumerate(
                ((lam_out, lam_hbm), (resid_out, resid_hbm), (direc_out, direc_hbm))
            ):
                copy = pltpu.make_async_copy(
                    here.at[s, piece], there.at[s, piece], sems.at[(s * 4 + r) * 3 + k]
                )
                copy.start()
                copies.append(copy)
    for copy in copies:
        copy.wait()


def vmem():
    return pl.BlockSpec(memory_space=pltpu.VMEM)


def hbm():
    return pl.BlockSpec(memory_space=pltpu.HBM)


def smem():
    return pl.BlockSpec(memory_space=pltpu.SMEM)


def exchange(x, axes, size, route):
    pairs = []
    for i in range(size):
        j = route(i)
        if j is not None:
            pairs.append((i, j))
    return lax.ppermute(x, axes, pairs)


def per_device(
    flex, coupling, weight, iface_size, partner, corner_map, coarse_factor, lam, resid, direc
):
    del iface_size
    blocks, links, scale = flex[:, 0], coupling[:, 0], weight
    lam2, resid2, direc2 = lam[:, 0], resid[:, 0], direc[:, 0]
    chain = lax.axis_size("sub")
    place = lax.axis_index("sub").astype(jnp.int32).reshape(1)

    whole = jax.ShapeDtypeStruct((2, N, L), F32)
    packed = jax.ShapeDtypeStruct((NAMES + 8, L), F32)
    pay_shape = jax.ShapeDtypeStruct((3 * C + 8, L), F32)
    pay, local, cross, near = pl.pallas_call(
        local_kernel,
        out_shape=(pay_shape, whole, packed, packed),
        in_specs=[smem()] + [hbm()] * 6,
        out_specs=(hbm(), hbm(), hbm(), hbm()),
        scratch_shapes=[
            pltpu.VMEM((2, N, N), F32),
            pltpu.VMEM((2, N, L), F32),
            pltpu.VMEM((2, C, N), F32),
            pltpu.VMEM((2, 1, N), jnp.int32),
            pltpu.VMEM((2, 1, C), jnp.int32),
            pltpu.VMEM((3 * C + 8, L), F32),
            pltpu.VMEM((2, N, L), F32),
            pltpu.VMEM((2, NAMES + 8, L), F32),
            pltpu.VMEM((2, 2 * N, L), BF16),
            pltpu.VMEM((2, N, L), BF16),
            pltpu.VMEM((2, N, L), BF16),
            pltpu.SemaphoreType.DMA((7,)),
            pltpu.SemaphoreType.DMA((5,)),
        ],
        name="local",
        compiler_params=pltpu.CompilerParams(vmem_limit_bytes=58 * MIB),
        cost_estimate=pl.CostEstimate(flops=4_000_000_000, bytes_accessed=12 * MIB, transcendentals=0),
    )(place, blocks, direc2, links, partner, corner_map, coarse_factor[0])
    others = [exchange(pay, "grp", 4, lambda i, m=m: i ^ m) for m in (1, 3, 2)]

    def across(i):
        j = i + 1 if i % 2 else i - 1
        return j if 0 <= j < chain else None

    def beside(i):
        return i ^ 1

    got_cross = exchange(cross, "sub", chain, across)
    got_near = exchange(near, "sub", chain, beside)

    part, mix = pl.pallas_call(
        inner_kernel,
        out_shape=(whole, jax.ShapeDtypeStruct((2, 2 * C, N), F32)),
        in_specs=[smem()] + [vmem()] * 3,
        out_specs=(vmem(), vmem()),
        scratch_shapes=[pltpu.VMEM((2, N, L), BF16)] * 2,
        name="inner",
        compiler_params=pltpu.CompilerParams(vmem_limit_bytes=16 * MIB),
        cost_estimate=pl.CostEstimate(flops=3_500_000_000, bytes_accessed=8 * MIB, transcendentals=0),
    )(place, local, links, partner)

    piece = jax.ShapeDtypeStruct((C, L), F32)
    cross_pick, near_pick = pl.pallas_call(
        coarse_kernel,
        out_shape=(piece, piece),
        in_specs=[smem()] + [vmem()] * 4 + [hbm()],
        out_specs=(vmem(), vmem()),
        name="coarse",
        compiler_params=pltpu.CompilerParams(vmem_limit_bytes=16 * MIB),
        cost_estimate=pl.CostEstimate(flops=30_000_000_000, bytes_accessed=MIB, transcendentals=0),
    )(place, pay, *others, mix)
    got_cross_pick = exchange(cross_pick, "sub", chain, across)
    got_near_pick = exchange(near_pick, "sub", chain, beside)

    jump, total = pl.pallas_call(
        outer_kernel,
        out_shape=(whole, jax.ShapeDtypeStruct((8, L), F32)),
        in_specs=[smem()] + [vmem()] * 11,
        out_specs=(vmem(), vmem()),
        scratch_shapes=[pltpu.VMEM((2, N, L), BF16), pltpu.VMEM((2, 8, L), jnp.int32)],
        name="outer",
        compiler_params=pltpu.CompilerParams(vmem_limit_bytes=16 * MIB),
        cost_estimate=pl.CostEstimate(flops=2_000_000_000, bytes_accessed=8 * MIB, transcendentals=0),
    )(
        place, part, mix, got_cross, got_near, got_cross_pick, got_near_pick,
        cross_pick, near_pick, scale, resid2, direc2,
    )

    total = total + exchange(total, "sub", chain, beside)
    both = ("sub", "grp")
    size = 4 * chain
    for near_bit, far_bit in (((4 * 8, 1)), ((3 * 4 * 8, 3)), ((4 * 2, 3 * 4 * 2))):
        flips = (near_bit, far_bit, near_bit ^ far_bit)
        total = total + sum(exchange(total, both, size, lambda i, m=m: i ^ m) for m in flips)

    lam_next, resid_next, direc_next, ratio = pl.pallas_call(
        final_kernel,
        out_shape=(whole, whole, whole, jax.ShapeDtypeStruct((1, L), F32)),
        in_specs=[vmem()] * 6,
        out_specs=(hbm(), hbm(), hbm(), vmem()),
        scratch_shapes=[pltpu.VMEM((2, N, L), F32)] * 3 + [pltpu.SemaphoreType.DMA((24,))],
        name="final",
        compiler_params=pltpu.CompilerParams(vmem_limit_bytes=24 * MIB),
    )(total, scale, lam2, resid2, direc2, jump)
    return (lam_next[:, None], resid_next[:, None], direc_next[:, None], ratio[0])


def solution(mesh):
    placed = (
        P("sub", "grp", None, None),
        P("sub", "grp", None, None),
        P("sub", "grp", None),
        P("sub", "grp"),
        P("sub", "grp", None),
        P("sub", "grp", None),
        P("sub", "grp", None),
        P("sub", "grp", None, None),
        P("sub", "grp", None, None),
        P("sub", "grp", None, None),
    )
    return jax.shard_map(
        per_device,
        mesh=mesh,
        in_specs=placed,
        out_specs=(
            P("sub", "grp", None, None),
            P("sub", "grp", None, None),
            P("sub", "grp", None, None),
            P(),
        ),
        check_vma=False,
    )
```

```python
import functools

import jax
import jax.numpy as jnp
from jax import lax
from jax.experimental import pallas as pl
from jax.experimental.pallas import tpu as pltpu
from jax.sharding import PartitionSpec as P

F32 = jnp.float32
BF16 = jnp.bfloat16
N = 1024
L = 256
C = 64
HALF = 512
NAMES = HALF + 2 * C
STRIP = 512
ROUNDS = N // STRIP
MIB = 1 << 20


def dot(a, b):
    return lax.dot_general(a, b, (((1,), (0,)), ((), ())), preferred_element_type=F32)


def dot_t(a, b):
    return lax.dot_general(a, b, (((0,), (0,)), ((), ())), preferred_element_type=F32)


def split(x):
    high = x.astype(BF16)
    low = (x - high.astype(F32)).astype(BF16)
    return high, low


def iota(shape, dim):
    return lax.broadcasted_iota(jnp.int32, shape, dim)


def one_hot(test):
    return jnp.where(test, 1.0, 0.0).astype(BF16)


def fold(x):
    return jnp.sum(x.reshape(-1, 8, x.shape[-1]), axis=0)


def column(row):
    tall = jnp.transpose(jnp.broadcast_to(row, (128, row.shape[1])))
    return jnp.concatenate([tall, tall], axis=1)


def primal_kernel(direc_hbm, coup_hbm, map_hbm, factor_hbm, pay_ref, direc, coup, corner, sems):
    copies = [
        pltpu.make_async_copy(coup_hbm, coup, sems.at[0]),
        pltpu.make_async_copy(direc_hbm.at[0], direc.at[0], sems.at[1]),
        pltpu.make_async_copy(direc_hbm.at[1], direc.at[1], sems.at[2]),
        pltpu.make_async_copy(map_hbm, corner, sems.at[3]),
        pltpu.make_async_copy(factor_hbm, pay_ref.at[pl.ds(2 * C, C)], sems.at[4]),
    ]
    for copy in copies:
        copy.start()
    pay_ref[3 * C :] = jnp.zeros((8, L), F32)
    for copy in copies:
        copy.wait()
    for s in range(2):
        ch, cl = split(coup[s])
        dh, dl = split(direc[s])
        pay_ref[s * C : (s + 1) * C] = dot(ch, dh) + dot(ch, dl) + dot(cl, dh)
        pay_ref[3 * C + s : 3 * C + s + 1, 0:C] = corner[s].astype(F32)


def running_count(mask):
    total = mask.astype(jnp.int32)
    lane = iota(total.shape, 1)
    step = 1
    while step < total.shape[1]:
        total = total + jnp.where(lane >= step, pltpu.roll(total, step, 1), 0)
        step *= 2
    return total


def local_kernel(
    place_ref, pay_hbm, flex_hbm, direc_hbm, coup_hbm, partner_hbm,
    local_hbm, cross_hbm, near_hbm,
    flex, direc, coup, partner, local, packed, places, right, high, low, sems, out_sems,
):
    del pay_hbm
    direc_copy = pltpu.make_async_copy(direc_hbm, direc, sems.at[0])
    flex_copies = [
        pltpu.make_async_copy(flex_hbm.at[s], flex.at[s], sems.at[1 + s]) for s in range(2)
    ]
    others = [
        pltpu.make_async_copy(coup_hbm, coup, sems.at[3]),
        pltpu.make_async_copy(partner_hbm, partner, sems.at[4]),
    ]
    out_copies = [
        pltpu.make_async_copy(local.at[s], local_hbm.at[s], out_sems.at[s]) for s in range(2)
    ]
    for copy in others:
        copy.start()
    direc_copy.start()
    flex_copies[0].start()
    me = place_ref[0]
    odd = lax.rem(me, 2)
    for copy in others:
        copy.wait()
    for s in range(2):
        target = partner[s] - (2 * me - 1) * N
        match = (target >= 3 * N) if s else (target < N)
        key = jnp.where(match, running_count(match) - 1, -1)
        name = jnp.where(match, jnp.bitwise_and(target, N - 1) + 1, 0)
        coarse = lax.shift_right_logical(name, 5)
        fine = jnp.bitwise_and(name, 31)
        digits = jnp.concatenate(
            [coarse, fine, jnp.zeros((14, N), jnp.int32)], axis=0
        ).astype(F32).astype(BF16)
        ch, cl = split(coup[s])
        stack = jnp.concatenate([ch, cl, digits], axis=0)
        packed[s, NAMES:] = jnp.zeros((8, L), F32)
        for c in range(2):
            place = one_hot(iota((L, N), 0) + c * L == key)
            places[s, c * L : (c + 1) * L] = place
            extra = lax.dot_general(
                stack, place, (((1,), (1,)), ((), ())), preferred_element_type=F32
            )
            packed[s, HALF + c * C : HALF + (c + 1) * C] = extra[0:C] + extra[C : 2 * C]
            packed[s, NAMES + c : NAMES + c + 1] = (
                extra[2 * C : 2 * C + 1] * 32.0 + extra[2 * C + 1 : 2 * C + 2]
            )
    direc_copy.wait()
    flex_copies[1].start()
    for s in range(2):
        dh, dl = split(direc[s])
        right[s, 0:N] = dh
        right[s, N:] = dl
    flex_copies[0].wait()
    for s in range(2):
        if s == 1:
            out_copies[0].start()
            flex_copies[1].wait()
        for r in range(ROUNDS):
            rows = slice(r * STRIP, (r + 1) * STRIP)
            ah, al = split(flex[s, rows])
            out = dot(ah, right[s, 0:N]) + dot(ah, right[s, N:]) + dot(al, right[s, 0:N])
            local[s, rows] = out
            oh, ol = split(out)
            high[s, rows] = oh
            low[s, rows] = ol
    for s in range(2):
        packed[s, 0:HALF] = dot(places[s], high[s]) + dot(places[s], low[s])
    cross_copy = pltpu.make_async_copy(packed.at[odd], cross_hbm, out_sems.at[2])
    near_copy = pltpu.make_async_copy(packed.at[1 - odd], near_hbm, out_sems.at[3])
    cross_copy.start()
    near_copy.start()
    out_copies[1].start()
    for copy in out_copies:
        copy.wait()
    cross_copy.wait()
    near_copy.wait()


def selector(pay_ref):
    first = pay_ref[3 * C : 3 * C + 1, 0:C]
    second = pay_ref[3 * C + 1 : 3 * C + 2, 0:C]
    both = jnp.concatenate([first, second], axis=1).astype(jnp.int32)
    return one_hot(iota((L, 2 * C), 0) == both)


def coarse_kernel(place_ref, pay_ref, one_ref, two_ref, three_ref, cross_ref, near_ref):
    odd = lax.rem(place_ref[0], 2)
    members = (pay_ref, one_ref, two_ref, three_ref)
    sels, parts = [], []
    for member in members:
        sel = selector(member)
        ph, pl_ = split(member[0 : 2 * C])
        sels += [sel, sel]
        parts += [ph, pl_]
    rhs = dot(jnp.concatenate(sels, axis=1), jnp.concatenate(parts, axis=0))
    factor = jnp.concatenate([m[2 * C : 3 * C] for m in members], axis=0)
    fh, fl = split(factor)
    rh, rl = split(rhs)
    mid = dot(jnp.concatenate([fh, fh, fl], axis=1), jnp.concatenate([rh, rl, rh], axis=0))
    mh, ml = split(mid)
    sol = dot_t(jnp.concatenate([fh, fh, fl], axis=0), jnp.concatenate([mh, ml, mh], axis=0))
    sh, sl = split(sol)
    own = sels[0]
    picked = dot_t(jnp.concatenate([own, own], axis=0), jnp.concatenate([sh, sl], axis=0))

    @pl.when(odd == 0)
    def _():
        cross_ref[...] = picked[0:C]
        near_ref[...] = picked[C:]

    @pl.when(odd == 1)
    def _():
        near_ref[...] = picked[0:C]
        cross_ref[...] = picked[C:]


def inner_kernel(
    place_ref, local_ref, cross_ref, near_ref, coup_ref, direc_ref, resid_ref, weight_ref, partner_ref,
    jump_ref, sums_ref, image_ref, high, low,
):
    me = place_ref[0]
    odd = lax.rem(me, 2) == 1
    old = jnp.zeros((8, L), F32)
    curve = jnp.zeros((8, L), F32)
    mixed = jnp.zeros((8, L), F32)
    for s in range(2):
        ch, cl = split(coup_ref[s])
        qh, ql = split(jnp.where(odd == (s == 1), cross_ref[...], near_ref[...]))
        left = jnp.concatenate([ch, ch, cl], axis=0)
        right = jnp.concatenate([qh, ql, qh], axis=0)
        for r in range(0, N, L):
            image = local_ref[s, r : r + L] + dot_t(left[:, r : r + L], right)
            image_ref[s, r : r + L] = image
            ih, il = split(image)
            high[s, r : r + L] = ih
            low[s, r : r + L] = il
    for s in range(2):
        other = 1 - s
        theirs = partner_ref[other] - (2 * me + s) * N
        mine = partner_ref[s]
        awake = jnp.where(lax.shift_right_arithmetic(mine, 10) != 2 * me + s, 1.0, 0.0)
        for r in range(0, N, L):
            rows = slice(r, r + L)
            place = one_hot(iota((L, N), 0) + r == theirs)
            opposite = dot(place, high[other]) + dot(place, low[other])
            image = image_ref[s, rows]
            jump_ref[s, rows] = column(awake[:, rows]) * image - opposite
            scaled = column(weight_ref[s][:, rows]) * resid_ref[s, rows]
            old = old + fold(scaled * resid_ref[s, rows])
            curve = curve + fold(direc_ref[s, rows] * image)
            mixed = mixed + fold(scaled * image)
    sums_ref[0] = old
    sums_ref[1] = curve
    sums_ref[2] = mixed


def outer_kernel(
    place_ref, part_ref, cross_ref, near_ref, cross_pick_ref, near_pick_ref, weight_ref, sums_ref,
    jump_ref, total_ref,
):
    odd = lax.rem(place_ref[0], 2)
    square = jnp.zeros((8, L), F32)
    for ref, pick_ref, s in ((cross_ref, cross_pick_ref, odd), (near_ref, near_pick_ref, 1 - odd)):
        qh, ql = split(pick_ref[...])
        right = jnp.concatenate([qh, ql, qh], axis=0)
        highs, lows = [], []
        for c in range(2):
            ch, cl = split(ref[HALF + c * C : HALF + (c + 1) * C])
            left = jnp.concatenate([ch, ch, cl], axis=0)
            image_high, image_low = split(ref[c * L : (c + 1) * L] + dot_t(left, right))
            highs.append(image_high)
            lows.append(image_low)
        stacked = jnp.concatenate(highs + lows, axis=0)
        names = [ref[NAMES + c : NAMES + c + 1].astype(jnp.int32) for c in range(2)]
        for r in range(0, N, L):
            places = [one_hot(iota((L, L), 0) + (r + 1) == name) for name in names]
            opposite = dot(jnp.concatenate(places + places, axis=1), stacked)
            jump = part_ref[s, r : r + L] - opposite
            jump_ref[s, r : r + L] = jump
            square = square + fold(column(weight_ref[s][:, r : r + L]) * jump * jump)
    rows = [jnp.sum(x, axis=0, keepdims=True) for x in (sums_ref[0], sums_ref[1], sums_ref[2], square)]
    total_ref[...] = jnp.concatenate(rows + [jnp.zeros((4, L), F32)], axis=0)


def final_kernel(
    total_ref, weight_ref, lam_ref, resid_ref, direc_ref, jump_ref,
    lam_hbm, resid_hbm, direc_hbm, ratio_ref, lam_out, resid_out, direc_out, sems,
):
    old = total_ref[0:1]
    alpha = old / (2.0 * total_ref[1:2])
    new = old + alpha * (alpha * total_ref[3:4] - 4.0 * total_ref[2:3])
    ratio = new / old
    ratio_ref[...] = ratio
    copies = []
    for s in range(2):
        for r in range(4):
            rows = slice(r * L, (r + 1) * L)
            direc = direc_ref[s, rows]
            resid = resid_ref[s, rows] - alpha * jump_ref[s, rows]
            lam_out[s, rows] = lam_ref[s, rows] + alpha * direc
            resid_out[s, rows] = resid
            direc_out[s, rows] = column(weight_ref[s][:, rows]) * resid + ratio * direc
            piece = pl.ds(r * L, L)
            for k, (here, there) in enumerate(
                ((lam_out, lam_hbm), (resid_out, resid_hbm), (direc_out, direc_hbm))
            ):
                copy = pltpu.make_async_copy(
                    here.at[s, piece], there.at[s, piece], sems.at[(s * 4 + r) * 3 + k]
                )
                copy.start()
                copies.append(copy)
    for copy in copies:
        copy.wait()


def vmem():
    return pl.BlockSpec(memory_space=pltpu.VMEM)


def hbm():
    return pl.BlockSpec(memory_space=pltpu.HBM)


def smem():
    return pl.BlockSpec(memory_space=pltpu.SMEM)


def exchange(x, axes, size, route):
    pairs = []
    for i in range(size):
        j = route(i)
        if j is not None:
            pairs.append((i, j))
    return lax.ppermute(x, axes, pairs)


def per_device(
    flex, coupling, weight, iface_size, partner, corner_map, coarse_factor, lam, resid, direc
):
    del iface_size
    blocks, links, scale = flex[:, 0], coupling[:, 0], weight
    lam2, resid2, direc2 = lam[:, 0], resid[:, 0], direc[:, 0]
    chain = lax.axis_size("sub")
    place = lax.axis_index("sub").astype(jnp.int32).reshape(1)

    whole = jax.ShapeDtypeStruct((2, N, L), F32)
    pay = pl.pallas_call(
        primal_kernel,
        out_shape=jax.ShapeDtypeStruct((3 * C + 8, L), F32),
        in_specs=[hbm()] * 4,
        out_specs=vmem(),
        scratch_shapes=[
            pltpu.VMEM((2, N, L), F32),
            pltpu.VMEM((2, C, N), F32),
            pltpu.VMEM((2, 1, C), jnp.int32),
            pltpu.SemaphoreType.DMA((5,)),
        ],
        name="primal",
        compiler_params=pltpu.CompilerParams(vmem_limit_bytes=58 * MIB),
        cost_estimate=pl.CostEstimate(flops=200_000_000, bytes_accessed=3 * MIB, transcendentals=0),
    )(direc2, links, corner_map, coarse_factor[0])
    others = [exchange(pay, "grp", 4, lambda i, m=m: i ^ m) for m in (1, 3, 2)]

    packed = jax.ShapeDtypeStruct((NAMES + 8, L), F32)
    local, cross, near = pl.pallas_call(
        local_kernel,
        out_shape=(jax.ShapeDtypeStruct((2, N, L), F32), packed, packed),
        in_specs=[smem()] + [hbm()] * 5,
        out_specs=(hbm(), hbm(), hbm()),
        scratch_shapes=[
            pltpu.VMEM((2, N, N), F32),
            pltpu.VMEM((2, N, L), F32),
            pltpu.VMEM((2, C, N), F32),
            pltpu.VMEM((2, 1, N), jnp.int32),
            pltpu.VMEM((2, N, L), F32),
            pltpu.VMEM((2, NAMES + 8, L), F32),
            pltpu.VMEM((2, HALF, N), BF16),
            pltpu.VMEM((2, 2 * N, L), BF16),
            pltpu.VMEM((2, N, L), BF16),
            pltpu.VMEM((2, N, L), BF16),
            pltpu.SemaphoreType.DMA((5,)),
            pltpu.SemaphoreType.DMA((4,)),
        ],
        name="local",
        compiler_params=pltpu.CompilerParams(vmem_limit_bytes=58 * MIB),
        cost_estimate=pl.CostEstimate(flops=4_000_000_000, bytes_accessed=12 * MIB, transcendentals=0),
    )(place, pay, blocks, direc2, links, partner)

    def across(i):
        j = i + 1 if i % 2 else i - 1
        return j if 0 <= j < chain else None

    def beside(i):
        return i ^ 1

    got_cross = exchange(cross, "sub", chain, across)
    got_near = exchange(near, "sub", chain, beside)

    piece = jax.ShapeDtypeStruct((C, L), F32)
    cross_pick, near_pick = pl.pallas_call(
        coarse_kernel,
        out_shape=(piece, piece),
        in_specs=[smem()] + [vmem()] * 4,
        out_specs=(vmem(), vmem()),
        name="coarse",
        compiler_params=pltpu.CompilerParams(vmem_limit_bytes=16 * MIB),
        cost_estimate=pl.CostEstimate(flops=30_000_000_000, bytes_accessed=MIB, transcendentals=0),
    )(place, pay, *others)
    got_cross_pick = exchange(cross_pick, "sub", chain, across)
    got_near_pick = exchange(near_pick, "sub", chain, beside)

    part, sums = pl.pallas_call(
        inner_kernel,
        out_shape=(whole, jax.ShapeDtypeStruct((3, 8, L), F32)),
        in_specs=[smem()] + [vmem()] * 8,
        out_specs=(vmem(), vmem()),
        scratch_shapes=[
            pltpu.VMEM((2, N, L), F32),
            pltpu.VMEM((2, N, L), BF16),
            pltpu.VMEM((2, N, L), BF16),
        ],
        name="inner",
        compiler_params=pltpu.CompilerParams(vmem_limit_bytes=24 * MIB),
        cost_estimate=pl.CostEstimate(flops=2_500_000_000, bytes_accessed=8 * MIB, transcendentals=0),
    )(place, local, cross_pick, near_pick, links, direc2, resid2, scale, partner)

    jump, total = pl.pallas_call(
        outer_kernel,
        out_shape=(whole, jax.ShapeDtypeStruct((8, L), F32)),
        in_specs=[smem()] + [vmem()] * 7,
        out_specs=(vmem(), vmem()),
        name="outer",
        compiler_params=pltpu.CompilerParams(vmem_limit_bytes=24 * MIB),
    )(place, part, got_cross, got_near, got_cross_pick, got_near_pick, scale, sums)

    total = total + exchange(total, "sub", chain, beside)
    both = ("sub", "grp")
    size = 4 * chain
    for near_bit, far_bit in (((4 * 8, 1)), ((3 * 4 * 8, 3)), ((4 * 2, 3 * 4 * 2))):
        flips = (near_bit, far_bit, near_bit ^ far_bit)
        total = total + sum(exchange(total, both, size, lambda i, m=m: i ^ m) for m in flips)

    lam_next, resid_next, direc_next, ratio = pl.pallas_call(
        final_kernel,
        out_shape=(whole, whole, whole, jax.ShapeDtypeStruct((1, L), F32)),
        in_specs=[vmem()] * 6,
        out_specs=(hbm(), hbm(), hbm(), vmem()),
        scratch_shapes=[pltpu.VMEM((2, N, L), F32)] * 3 + [pltpu.SemaphoreType.DMA((24,))],
        name="final",
        compiler_params=pltpu.CompilerParams(vmem_limit_bytes=24 * MIB),
    )(total, scale, lam2, resid2, direc2, jump)
    return (lam_next[:, None], resid_next[:, None], direc_next[:, None], ratio[0])


def solution(mesh):
    placed = (
        P("sub", "grp", None, None),
        P("sub", "grp", None, None),
        P("sub", "grp", None),
        P("sub", "grp"),
        P("sub", "grp", None),
        P("sub", "grp", None),
        P("sub", "grp", None),
        P("sub", "grp", None, None),
        P("sub", "grp", None, None),
        P("sub", "grp", None, None),
    )
    return jax.shard_map(
        per_device,
        mesh=mesh,
        in_specs=placed,
        out_specs=(
            P("sub", "grp", None, None),
            P("sub", "grp", None, None),
            P("sub", "grp", None, None),
            P(),
        ),
        check_vma=False,
    )
```

```python
import functools

import jax
import jax.numpy as jnp
from jax import lax
from jax.experimental import pallas as pl
from jax.experimental.pallas import tpu as pltpu
from jax.sharding import PartitionSpec as P

F32 = jnp.float32
BF16 = jnp.bfloat16
N = 1024
L = 256
C = 64
HALF = 512
NAMES = HALF + 2 * C
STRIP = 512
ROUNDS = N // STRIP
MIB = 1 << 20
LIMIT = 46 * MIB


def dot(a, b):
    return lax.dot_general(a, b, (((1,), (0,)), ((), ())), preferred_element_type=F32)


def dot_t(a, b):
    return lax.dot_general(a, b, (((0,), (0,)), ((), ())), preferred_element_type=F32)


def split(x):
    high = x.astype(BF16)
    low = (x - high.astype(F32)).astype(BF16)
    return high, low


def iota(shape, dim):
    return lax.broadcasted_iota(jnp.int32, shape, dim)


def one_hot(test):
    return jnp.where(test, 1.0, 0.0).astype(BF16)


def fold(x):
    return jnp.sum(x.reshape(-1, 8, x.shape[-1]), axis=0)


def column(row):
    tall = jnp.transpose(jnp.broadcast_to(row, (128, row.shape[1])))
    return jnp.concatenate([tall, tall], axis=1)


def primal_kernel(
    place_ref, direc_hbm, coup_hbm, map_hbm, factor_hbm, pay_ref, token_ref, direc, coup, corner, sems
):
    token_ref[0] = place_ref[0]
    copies = [
        pltpu.make_async_copy(coup_hbm, coup, sems.at[0]),
        pltpu.make_async_copy(direc_hbm.at[0], direc.at[0], sems.at[1]),
        pltpu.make_async_copy(direc_hbm.at[1], direc.at[1], sems.at[2]),
        pltpu.make_async_copy(map_hbm, corner, sems.at[3]),
        pltpu.make_async_copy(factor_hbm, pay_ref.at[pl.ds(2 * C, C)], sems.at[4]),
    ]
    for copy in copies:
        copy.start()
    pay_ref[3 * C :] = jnp.zeros((8, L), F32)
    for copy in copies:
        copy.wait()
    for s in range(2):
        ch, cl = split(coup[s])
        dh, dl = split(direc[s])
        pay_ref[s * C : (s + 1) * C] = dot(ch, dh) + dot(ch, dl) + dot(cl, dh)
        pay_ref[3 * C + s : 3 * C + s + 1, 0:C] = corner[s].astype(F32)


def running_count(mask):
    total = mask.astype(jnp.int32)
    lane = iota(total.shape, 1)
    step = 1
    while step < total.shape[1]:
        total = total + jnp.where(lane >= step, pltpu.roll(total, step, 1), 0)
        step *= 2
    return total


def local_kernel(
    place_ref, flex_hbm, direc, coup, partner,
    local, cross_hbm, near_hbm,
    flex, packed, places, right, high, low, sems, out_sems,
):
    flex_copies = [
        pltpu.make_async_copy(flex_hbm.at[s], flex.at[s], sems.at[s]) for s in range(2)
    ]
    for copy in flex_copies:
        copy.start()
    me = place_ref[0]
    odd = lax.rem(me, 2)
    for s in range(2):
        target = partner[s] - (2 * me - 1) * N
        match = (target >= 3 * N) if s else (target < N)
        key = jnp.where(match, running_count(match) - 1, -1)
        name = jnp.where(match, jnp.bitwise_and(target, N - 1) + 1, 0)
        coarse = lax.shift_right_logical(name, 5)
        fine = jnp.bitwise_and(name, 31)
        digits = jnp.concatenate(
            [coarse, fine, jnp.zeros((14, N), jnp.int32)], axis=0
        ).astype(F32).astype(BF16)
        ch, cl = split(coup[s])
        stack = jnp.concatenate([ch, cl, digits], axis=0)
        packed[s, NAMES:] = jnp.zeros((8, L), F32)
        for c in range(2):
            place = one_hot(iota((L, N), 0) + c * L == key)
            places[s, c * L : (c + 1) * L] = place
            extra = lax.dot_general(
                stack, place, (((1,), (1,)), ((), ())), preferred_element_type=F32
            )
            packed[s, HALF + c * C : HALF + (c + 1) * C] = extra[0:C] + extra[C : 2 * C]
            packed[s, NAMES + c : NAMES + c + 1] = (
                extra[2 * C : 2 * C + 1] * 32.0 + extra[2 * C + 1 : 2 * C + 2]
            )
    for s in range(2):
        dh, dl = split(direc[s])
        right[s, 0:N] = dh
        right[s, N:] = dl
    flex_copies[0].wait()
    for s in range(2):
        if s == 1:
            flex_copies[1].wait()
        for r in range(ROUNDS):
            rows = slice(r * STRIP, (r + 1) * STRIP)
            ah, al = split(flex[s, rows])
            out = dot(ah, right[s, 0:N]) + dot(ah, right[s, N:]) + dot(al, right[s, 0:N])
            local[s, rows] = out
            oh, ol = split(out)
            high[s, rows] = oh
            low[s, rows] = ol
    for s in range(2):
        packed[s, 0:HALF] = dot(places[s], high[s]) + dot(places[s], low[s])
    cross_copy = pltpu.make_async_copy(packed.at[odd], cross_hbm, out_sems.at[0])
    near_copy = pltpu.make_async_copy(packed.at[1 - odd], near_hbm, out_sems.at[1])
    cross_copy.start()
    near_copy.start()
    cross_copy.wait()
    near_copy.wait()


def selector(pay_ref):
    first = pay_ref[3 * C : 3 * C + 1, 0:C]
    second = pay_ref[3 * C + 1 : 3 * C + 2, 0:C]
    both = jnp.concatenate([first, second], axis=1).astype(jnp.int32)
    return one_hot(iota((L, 2 * C), 0) == both)


def coarse_kernel(place_ref, pay_ref, one_ref, two_ref, three_ref, cross_ref, near_ref):
    odd = lax.rem(place_ref[0], 2)
    members = (pay_ref, one_ref, two_ref, three_ref)
    sels, parts = [], []
    for member in members:
        sel = selector(member)
        ph, pl_ = split(member[0 : 2 * C])
        sels += [sel, sel]
        parts += [ph, pl_]
    rhs = dot(jnp.concatenate(sels, axis=1), jnp.concatenate(parts, axis=0))
    factor = jnp.concatenate([m[2 * C : 3 * C] for m in members], axis=0)
    fh, fl = split(factor)
    rh, rl = split(rhs)
    mid = dot(jnp.concatenate([fh, fh, fl], axis=1), jnp.concatenate([rh, rl, rh], axis=0))
    mh, ml = split(mid)
    sol = dot_t(jnp.concatenate([fh, fh, fl], axis=0), jnp.concatenate([mh, ml, mh], axis=0))
    sh, sl = split(sol)
    own = sels[0]
    picked = dot_t(jnp.concatenate([own, own], axis=0), jnp.concatenate([sh, sl], axis=0))

    @pl.when(odd == 0)
    def _():
        cross_ref[...] = picked[0:C]
        near_ref[...] = picked[C:]

    @pl.when(odd == 1)
    def _():
        near_ref[...] = picked[0:C]
        cross_ref[...] = picked[C:]


def inner_kernel(
    place_ref, local_ref, cross_ref, near_ref, coup_ref, direc_ref, resid_ref, weight_ref, partner_ref,
    jump_ref, sums_ref, image_ref, high, low,
):
    me = place_ref[0]
    odd = lax.rem(me, 2) == 1
    old = jnp.zeros((8, L), F32)
    curve = jnp.zeros((8, L), F32)
    mixed = jnp.zeros((8, L), F32)
    for s in range(2):
        ch, cl = split(coup_ref[s])
        qh, ql = split(jnp.where(odd == (s == 1), cross_ref[...], near_ref[...]))
        left = jnp.concatenate([ch, ch, cl], axis=0)
        right = jnp.concatenate([qh, ql, qh], axis=0)
        for r in range(0, N, L):
            image = local_ref[s, r : r + L] + dot_t(left[:, r : r + L], right)
            image_ref[s, r : r + L] = image
            ih, il = split(image)
            high[s, r : r + L] = ih
            low[s, r : r + L] = il
    for s in range(2):
        other = 1 - s
        theirs = partner_ref[other] - (2 * me + s) * N
        mine = partner_ref[s]
        awake = jnp.where(lax.shift_right_arithmetic(mine, 10) != 2 * me + s, 1.0, 0.0)
        for r in range(0, N, L):
            rows = slice(r, r + L)
            place = one_hot(iota((L, N), 0) + r == theirs)
            opposite = dot(place, high[other]) + dot(place, low[other])
            image = image_ref[s, rows]
            jump_ref[s, rows] = column(awake[:, rows]) * image - opposite
            scaled = column(weight_ref[s][:, rows]) * resid_ref[s, rows]
            old = old + fold(scaled * resid_ref[s, rows])
            curve = curve + fold(direc_ref[s, rows] * image)
            mixed = mixed + fold(scaled * image)
    sums_ref[0] = old
    sums_ref[1] = curve
    sums_ref[2] = mixed


def outer_kernel(
    place_ref, part_ref, cross_ref, near_ref, cross_pick_ref, near_pick_ref, weight_ref, sums_ref,
    jump_ref, total_ref,
):
    odd = lax.rem(place_ref[0], 2)
    square = jnp.zeros((8, L), F32)
    for ref, pick_ref, s in ((cross_ref, cross_pick_ref, odd), (near_ref, near_pick_ref, 1 - odd)):
        qh, ql = split(pick_ref[...])
        right = jnp.concatenate([qh, ql, qh], axis=0)
        highs, lows = [], []
        for c in range(2):
            ch, cl = split(ref[HALF + c * C : HALF + (c + 1) * C])
            left = jnp.concatenate([ch, ch, cl], axis=0)
            image_high, image_low = split(ref[c * L : (c + 1) * L] + dot_t(left, right))
            highs.append(image_high)
            lows.append(image_low)
        stacked = jnp.concatenate(highs + lows, axis=0)
        names = [ref[NAMES + c : NAMES + c + 1].astype(jnp.int32) for c in range(2)]
        for r in range(0, N, L):
            places = [one_hot(iota((L, L), 0) + (r + 1) == name) for name in names]
            opposite = dot(jnp.concatenate(places + places, axis=1), stacked)
            jump = part_ref[s, r : r + L] - opposite
            jump_ref[s, r : r + L] = jump
            square = square + fold(column(weight_ref[s][:, r : r + L]) * jump * jump)
    rows = [jnp.sum(x, axis=0, keepdims=True) for x in (sums_ref[0], sums_ref[1], sums_ref[2], square)]
    total_ref[...] = jnp.concatenate(rows + [jnp.zeros((4, L), F32)], axis=0)


def final_kernel(
    total_ref, weight_ref, lam_ref, resid_ref, direc_ref, jump_ref,
    lam_hbm, resid_hbm, direc_hbm, ratio_ref, lam_out, resid_out, direc_out, sems,
):
    old = total_ref[0:1]
    alpha = old / (2.0 * total_ref[1:2])
    new = old + alpha * (alpha * total_ref[3:4] - 4.0 * total_ref[2:3])
    ratio = new / old
    ratio_ref[...] = ratio
    copies = []
    for s in range(2):
        for r in range(4):
            rows = slice(r * L, (r + 1) * L)
            direc = direc_ref[s, rows]
            resid = resid_ref[s, rows] - alpha * jump_ref[s, rows]
            lam_out[s, rows] = lam_ref[s, rows] + alpha * direc
            resid_out[s, rows] = resid
            direc_out[s, rows] = column(weight_ref[s][:, rows]) * resid + ratio * direc
            piece = pl.ds(r * L, L)
            for k, (here, there) in enumerate(
                ((lam_out, lam_hbm), (resid_out, resid_hbm), (direc_out, direc_hbm))
            ):
                copy = pltpu.make_async_copy(
                    here.at[s, piece], there.at[s, piece], sems.at[(s * 4 + r) * 3 + k]
                )
                copy.start()
                copies.append(copy)
    for copy in copies:
        copy.wait()


def vmem():
    return pl.BlockSpec(memory_space=pltpu.VMEM)


def hbm():
    return pl.BlockSpec(memory_space=pltpu.HBM)


def smem():
    return pl.BlockSpec(memory_space=pltpu.SMEM)


def exchange(x, axes, size, route):
    pairs = []
    for i in range(size):
        j = route(i)
        if j is not None:
            pairs.append((i, j))
    return lax.ppermute(x, axes, pairs)


def per_device(
    flex, coupling, weight, iface_size, partner, corner_map, coarse_factor, lam, resid, direc
):
    del iface_size
    blocks, links, scale = flex[:, 0], coupling[:, 0], weight
    lam2, resid2, direc2 = lam[:, 0], resid[:, 0], direc[:, 0]
    chain = lax.axis_size("sub")
    place = lax.axis_index("sub").astype(jnp.int32).reshape(1)

    whole = jax.ShapeDtypeStruct((2, N, L), F32)
    pay, token = pl.pallas_call(
        primal_kernel,
        out_shape=(
            jax.ShapeDtypeStruct((3 * C + 8, L), F32),
            jax.ShapeDtypeStruct((1,), jnp.int32),
        ),
        in_specs=[smem()] + [hbm()] * 4,
        out_specs=(vmem(), smem()),
        scratch_shapes=[
            pltpu.VMEM((2, N, L), F32),
            pltpu.VMEM((2, C, N), F32),
            pltpu.VMEM((2, 1, C), jnp.int32),
            pltpu.SemaphoreType.DMA((5,)),
        ],
        name="primal",
        compiler_params=pltpu.CompilerParams(vmem_limit_bytes=58 * MIB),
        cost_estimate=pl.CostEstimate(flops=200_000_000, bytes_accessed=3 * MIB, transcendentals=0),
    )(place, direc2, links, corner_map, coarse_factor[0])
    others = [exchange(pay, "grp", 4, lambda i, m=m: i ^ m) for m in (1, 3, 2)]

    packed = jax.ShapeDtypeStruct((NAMES + 8, L), F32)
    local, cross, near = pl.pallas_call(
        local_kernel,
        out_shape=(jax.ShapeDtypeStruct((2, N, L), F32), packed, packed),
        in_specs=[smem(), hbm()] + [vmem()] * 3,
        out_specs=(vmem(), hbm(), hbm()),
        scratch_shapes=[
            pltpu.VMEM((2, N, N), F32),
            pltpu.VMEM((2, NAMES + 8, L), F32),
            pltpu.VMEM((2, HALF, N), BF16),
            pltpu.VMEM((2, 2 * N, L), BF16),
            pltpu.VMEM((2, N, L), BF16),
            pltpu.VMEM((2, N, L), BF16),
            pltpu.SemaphoreType.DMA((2,)),
            pltpu.SemaphoreType.DMA((2,)),
        ],
        name="local",
        compiler_params=pltpu.CompilerParams(vmem_limit_bytes=LIMIT),
        cost_estimate=pl.CostEstimate(flops=4_000_000_000, bytes_accessed=12 * MIB, transcendentals=0),
    )(token, blocks, direc2, links, partner)

    def across(i):
        j = i + 1 if i % 2 else i - 1
        return j if 0 <= j < chain else None

    def beside(i):
        return i ^ 1

    got_cross = exchange(cross, "sub", chain, across)
    got_near = exchange(near, "sub", chain, beside)

    piece = jax.ShapeDtypeStruct((C, L), F32)
    cross_pick, near_pick = pl.pallas_call(
        coarse_kernel,
        out_shape=(piece, piece),
        in_specs=[smem()] + [vmem()] * 4,
        out_specs=(vmem(), vmem()),
        name="coarse",
        compiler_params=pltpu.CompilerParams(vmem_limit_bytes=16 * MIB),
        cost_estimate=pl.CostEstimate(flops=30_000_000_000, bytes_accessed=MIB, transcendentals=0),
    )(place, pay, *others)
    got_cross_pick = exchange(cross_pick, "sub", chain, across)
    got_near_pick = exchange(near_pick, "sub", chain, beside)

    part, sums = pl.pallas_call(
        inner_kernel,
        out_shape=(whole, jax.ShapeDtypeStruct((3, 8, L), F32)),
        in_specs=[smem()] + [vmem()] * 8,
        out_specs=(vmem(), vmem()),
        scratch_shapes=[
            pltpu.VMEM((2, N, L), F32),
            pltpu.VMEM((2, N, L), BF16),
            pltpu.VMEM((2, N, L), BF16),
        ],
        name="inner",
        compiler_params=pltpu.CompilerParams(vmem_limit_bytes=24 * MIB),
        cost_estimate=pl.CostEstimate(flops=2_500_000_000, bytes_accessed=8 * MIB, transcendentals=0),
    )(place, local, cross_pick, near_pick, links, direc2, resid2, scale, partner)

    jump, total = pl.pallas_call(
        outer_kernel,
        out_shape=(whole, jax.ShapeDtypeStruct((8, L), F32)),
        in_specs=[smem()] + [vmem()] * 7,
        out_specs=(vmem(), vmem()),
        name="outer",
        compiler_params=pltpu.CompilerParams(vmem_limit_bytes=24 * MIB),
    )(place, part, got_cross, got_near, got_cross_pick, got_near_pick, scale, sums)

    total = total + exchange(total, "sub", chain, beside)
    both = ("sub", "grp")
    size = 4 * chain
    for near_bit, far_bit in (((4 * 8, 1)), ((3 * 4 * 8, 3)), ((4 * 2, 3 * 4 * 2))):
        flips = (near_bit, far_bit, near_bit ^ far_bit)
        total = total + sum(exchange(total, both, size, lambda i, m=m: i ^ m) for m in flips)

    lam_next, resid_next, direc_next, ratio = pl.pallas_call(
        final_kernel,
        out_shape=(whole, whole, whole, jax.ShapeDtypeStruct((1, L), F32)),
        in_specs=[vmem()] * 6,
        out_specs=(hbm(), hbm(), hbm(), vmem()),
        scratch_shapes=[pltpu.VMEM((2, N, L), F32)] * 3 + [pltpu.SemaphoreType.DMA((24,))],
        name="final",
        compiler_params=pltpu.CompilerParams(vmem_limit_bytes=24 * MIB),
    )(total, scale, lam2, resid2, direc2, jump)
    return (lam_next[:, None], resid_next[:, None], direc_next[:, None], ratio[0])


def solution(mesh):
    placed = (
        P("sub", "grp", None, None),
        P("sub", "grp", None, None),
        P("sub", "grp", None),
        P("sub", "grp"),
        P("sub", "grp", None),
        P("sub", "grp", None),
        P("sub", "grp", None),
        P("sub", "grp", None, None),
        P("sub", "grp", None, None),
        P("sub", "grp", None, None),
    )
    return jax.shard_map(
        per_device,
        mesh=mesh,
        in_specs=placed,
        out_specs=(
            P("sub", "grp", None, None),
            P("sub", "grp", None, None),
            P("sub", "grp", None, None),
            P(),
        ),
        check_vma=False,
    )
```

```python
import functools

import jax
import jax.numpy as jnp
from jax import lax
from jax.experimental import pallas as pl
from jax.experimental.pallas import tpu as pltpu
from jax.sharding import PartitionSpec as P

F32 = jnp.float32
BF16 = jnp.bfloat16
N = 1024
L = 256
C = 64
HALF = 512
NAMES = HALF + 2 * C
STRIP = 512
ROUNDS = N // STRIP
MIB = 1 << 20
LIMIT = 46 * MIB


def dot(a, b):
    return lax.dot_general(a, b, (((1,), (0,)), ((), ())), preferred_element_type=F32)


def dot_t(a, b):
    return lax.dot_general(a, b, (((0,), (0,)), ((), ())), preferred_element_type=F32)


def split(x):
    high = x.astype(BF16)
    low = (x - high.astype(F32)).astype(BF16)
    return high, low


def iota(shape, dim):
    return lax.broadcasted_iota(jnp.int32, shape, dim)


def one_hot(test):
    return jnp.where(test, 1.0, 0.0).astype(BF16)


def fold(x):
    return jnp.sum(x.reshape(-1, 8, x.shape[-1]), axis=0)


def column(row):
    tall = jnp.transpose(jnp.broadcast_to(row, (128, row.shape[1])))
    return jnp.concatenate([tall, tall], axis=1)


def primal_kernel(
    place_ref, direc_hbm, coup_hbm, map_hbm, factor_hbm, pay_ref, token_ref, direc, coup, corner, sems
):
    token_ref[0] = place_ref[0]
    copies = [
        pltpu.make_async_copy(coup_hbm, coup, sems.at[0]),
        pltpu.make_async_copy(direc_hbm.at[0], direc.at[0], sems.at[1]),
        pltpu.make_async_copy(direc_hbm.at[1], direc.at[1], sems.at[2]),
        pltpu.make_async_copy(map_hbm, corner, sems.at[3]),
        pltpu.make_async_copy(factor_hbm, pay_ref.at[pl.ds(2 * C, C)], sems.at[4]),
    ]
    for copy in copies:
        copy.start()
    pay_ref[3 * C :] = jnp.zeros((8, L), F32)
    for copy in copies:
        copy.wait()
    for s in range(2):
        ch, cl = split(coup[s])
        dh, dl = split(direc[s])
        pay_ref[s * C : (s + 1) * C] = dot(ch, dh) + dot(ch, dl) + dot(cl, dh)
        pay_ref[3 * C + s : 3 * C + s + 1, 0:C] = corner[s].astype(F32)


def running_count(mask):
    total = mask.astype(jnp.int32)
    lane = iota(total.shape, 1)
    step = 1
    while step < total.shape[1]:
        total = total + jnp.where(lane >= step, pltpu.roll(total, step, 1), 0)
        step *= 2
    return total


def local_kernel(
    place_ref, flex_hbm, direc, coup, partner,
    local, cross_hbm, near_hbm,
    flex, packed, places, right, high, low, sems, out_sems,
):
    flex_copies = [
        pltpu.make_async_copy(flex_hbm.at[s], flex.at[s], sems.at[s]) for s in range(2)
    ]
    flex_copies[0].start()
    me = place_ref[0]
    odd = lax.rem(me, 2)
    for s in range(2):
        target = partner[s] - (2 * me - 1) * N
        match = (target >= 3 * N) if s else (target < N)
        key = jnp.where(match, running_count(match) - 1, -1)
        name = jnp.where(match, jnp.bitwise_and(target, N - 1) + 1, 0)
        coarse = lax.shift_right_logical(name, 5)
        fine = jnp.bitwise_and(name, 31)
        digits = jnp.concatenate(
            [coarse, fine, jnp.zeros((14, N), jnp.int32)], axis=0
        ).astype(F32).astype(BF16)
        ch, cl = split(coup[s])
        stack = jnp.concatenate([ch, cl, digits], axis=0)
        packed[s, NAMES:] = jnp.zeros((8, L), F32)
        for c in range(2):
            place = one_hot(iota((L, N), 0) + c * L == key)
            places[s, c * L : (c + 1) * L] = place
            extra = lax.dot_general(
                stack, place, (((1,), (1,)), ((), ())), preferred_element_type=F32
            )
            packed[s, HALF + c * C : HALF + (c + 1) * C] = extra[0:C] + extra[C : 2 * C]
            packed[s, NAMES + c : NAMES + c + 1] = (
                extra[2 * C : 2 * C + 1] * 32.0 + extra[2 * C + 1 : 2 * C + 2]
            )
    flex_copies[1].start()
    for s in range(2):
        dh, dl = split(direc[s])
        right[s, 0:N] = dh
        right[s, N:] = dl
    flex_copies[0].wait()
    for s in range(2):
        if s == 1:
            flex_copies[1].wait()
        for r in range(ROUNDS):
            rows = slice(r * STRIP, (r + 1) * STRIP)
            ah, al = split(flex[s, rows])
            out = dot(ah, right[s, 0:N]) + dot(ah, right[s, N:]) + dot(al, right[s, 0:N])
            local[s, rows] = out
            oh, ol = split(out)
            high[s, rows] = oh
            low[s, rows] = ol
    for s in range(2):
        packed[s, 0:HALF] = dot(places[s], high[s]) + dot(places[s], low[s])
    cross_copy = pltpu.make_async_copy(packed.at[odd], cross_hbm, out_sems.at[0])
    near_copy = pltpu.make_async_copy(packed.at[1 - odd], near_hbm, out_sems.at[1])
    cross_copy.start()
    near_copy.start()
    cross_copy.wait()
    near_copy.wait()


def selector(pay_ref):
    first = pay_ref[3 * C : 3 * C + 1, 0:C]
    second = pay_ref[3 * C + 1 : 3 * C + 2, 0:C]
    both = jnp.concatenate([first, second], axis=1).astype(jnp.int32)
    return one_hot(iota((L, 2 * C), 0) == both)


def coarse_kernel(place_ref, pay_ref, one_ref, two_ref, three_ref, cross_ref, near_ref):
    odd = lax.rem(place_ref[0], 2)
    members = (pay_ref, one_ref, two_ref, three_ref)
    sels, parts = [], []
    for member in members:
        sel = selector(member)
        ph, pl_ = split(member[0 : 2 * C])
        sels += [sel, sel]
        parts += [ph, pl_]
    rhs = dot(jnp.concatenate(sels, axis=1), jnp.concatenate(parts, axis=0))
    factor = jnp.concatenate([m[2 * C : 3 * C] for m in members], axis=0)
    fh, fl = split(factor)
    rh, rl = split(rhs)
    mid = dot(jnp.concatenate([fh, fh, fl], axis=1), jnp.concatenate([rh, rl, rh], axis=0))
    mh, ml = split(mid)
    sol = dot_t(jnp.concatenate([fh, fh, fl], axis=0), jnp.concatenate([mh, ml, mh], axis=0))
    sh, sl = split(sol)
    own = sels[0]
    picked = dot_t(jnp.concatenate([own, own], axis=0), jnp.concatenate([sh, sl], axis=0))

    @pl.when(odd == 0)
    def _():
        cross_ref[...] = picked[0:C]
        near_ref[...] = picked[C:]

    @pl.when(odd == 1)
    def _():
        near_ref[...] = picked[0:C]
        cross_ref[...] = picked[C:]


def inner_kernel(
    place_ref, local_ref, cross_ref, near_ref, coup_ref, direc_ref, resid_ref, weight_ref, partner_ref,
    jump_ref, sums_ref, image_ref, high, low,
):
    me = place_ref[0]
    odd = lax.rem(me, 2) == 1
    old = jnp.zeros((8, L), F32)
    curve = jnp.zeros((8, L), F32)
    mixed = jnp.zeros((8, L), F32)
    for s in range(2):
        ch, cl = split(coup_ref[s])
        qh, ql = split(jnp.where(odd == (s == 1), cross_ref[...], near_ref[...]))
        left = jnp.concatenate([ch, ch, cl], axis=0)
        right = jnp.concatenate([qh, ql, qh], axis=0)
        for r in range(0, N, L):
            image = local_ref[s, r : r + L] + dot_t(left[:, r : r + L], right)
            image_ref[s, r : r + L] = image
            ih, il = split(image)
            high[s, r : r + L] = ih
            low[s, r : r + L] = il
    for s in range(2):
        other = 1 - s
        theirs = partner_ref[other] - (2 * me + s) * N
        mine = partner_ref[s]
        awake = jnp.where(lax.shift_right_arithmetic(mine, 10) != 2 * me + s, 1.0, 0.0)
        for r in range(0, N, L):
            rows = slice(r, r + L)
            place = one_hot(iota((L, N), 0) + r == theirs)
            opposite = dot(place, high[other]) + dot(place, low[other])
            image = image_ref[s, rows]
            jump_ref[s, rows] = column(awake[:, rows]) * image - opposite
            scaled = column(weight_ref[s][:, rows]) * resid_ref[s, rows]
            old = old + fold(scaled * resid_ref[s, rows])
            curve = curve + fold(direc_ref[s, rows] * image)
            mixed = mixed + fold(scaled * image)
    sums_ref[0] = old
    sums_ref[1] = curve
    sums_ref[2] = mixed


def outer_kernel(
    place_ref, part_ref, cross_ref, near_ref, cross_pick_ref, near_pick_ref, weight_ref, sums_ref,
    jump_ref, total_ref,
):
    odd = lax.rem(place_ref[0], 2)
    square = jnp.zeros((8, L), F32)
    for ref, pick_ref, s in ((cross_ref, cross_pick_ref, odd), (near_ref, near_pick_ref, 1 - odd)):
        qh, ql = split(pick_ref[...])
        right = jnp.concatenate([qh, ql, qh], axis=0)
        highs, lows = [], []
        for c in range(2):
            ch, cl = split(ref[HALF + c * C : HALF + (c + 1) * C])
            left = jnp.concatenate([ch, ch, cl], axis=0)
            image_high, image_low = split(ref[c * L : (c + 1) * L] + dot_t(left, right))
            highs.append(image_high)
            lows.append(image_low)
        stacked = jnp.concatenate(highs + lows, axis=0)
        names = [ref[NAMES + c : NAMES + c + 1].astype(jnp.int32) for c in range(2)]
        for r in range(0, N, L):
            places = [one_hot(iota((L, L), 0) + (r + 1) == name) for name in names]
            opposite = dot(jnp.concatenate(places + places, axis=1), stacked)
            jump = part_ref[s, r : r + L] - opposite
            jump_ref[s, r : r + L] = jump
            square = square + fold(column(weight_ref[s][:, r : r + L]) * jump * jump)
    rows = [jnp.sum(x, axis=0, keepdims=True) for x in (sums_ref[0], sums_ref[1], sums_ref[2], square)]
    total_ref[...] = jnp.concatenate(rows + [jnp.zeros((4, L), F32)], axis=0)


def final_kernel(
    total_ref, weight_ref, lam_ref, resid_ref, direc_ref, jump_ref,
    lam_hbm, resid_hbm, direc_hbm, ratio_ref, lam_out, resid_out, direc_out, sems,
):
    old = total_ref[0:1]
    alpha = old / (2.0 * total_ref[1:2])
    new = old + alpha * (alpha * total_ref[3:4] - 4.0 * total_ref[2:3])
    ratio = new / old
    ratio_ref[...] = ratio
    copies = []
    for s in range(2):
        for r in range(4):
            rows = slice(r * L, (r + 1) * L)
            direc = direc_ref[s, rows]
            resid = resid_ref[s, rows] - alpha * jump_ref[s, rows]
            lam_out[s, rows] = lam_ref[s, rows] + alpha * direc
            resid_out[s, rows] = resid
            direc_out[s, rows] = column(weight_ref[s][:, rows]) * resid + ratio * direc
            piece = pl.ds(r * L, L)
            for k, (here, there) in enumerate(
                ((lam_out, lam_hbm), (resid_out, resid_hbm), (direc_out, direc_hbm))
            ):
                copy = pltpu.make_async_copy(
                    here.at[s, piece], there.at[s, piece], sems.at[(s * 4 + r) * 3 + k]
                )
                copy.start()
                copies.append(copy)
    for copy in copies:
        copy.wait()


def vmem():
    return pl.BlockSpec(memory_space=pltpu.VMEM)


def hbm():
    return pl.BlockSpec(memory_space=pltpu.HBM)


def smem():
    return pl.BlockSpec(memory_space=pltpu.SMEM)


def exchange(x, axes, size, route):
    pairs = []
    for i in range(size):
        j = route(i)
        if j is not None:
            pairs.append((i, j))
    return lax.ppermute(x, axes, pairs)


def per_device(
    flex, coupling, weight, iface_size, partner, corner_map, coarse_factor, lam, resid, direc
):
    del iface_size
    blocks, links, scale = flex[:, 0], coupling[:, 0], weight
    lam2, resid2, direc2 = lam[:, 0], resid[:, 0], direc[:, 0]
    chain = lax.axis_size("sub")
    place = lax.axis_index("sub").astype(jnp.int32).reshape(1)

    whole = jax.ShapeDtypeStruct((2, N, L), F32)
    pay, token = pl.pallas_call(
        primal_kernel,
        out_shape=(
            jax.ShapeDtypeStruct((3 * C + 8, L), F32),
            jax.ShapeDtypeStruct((1,), jnp.int32),
        ),
        in_specs=[smem()] + [hbm()] * 4,
        out_specs=(vmem(), smem()),
        scratch_shapes=[
            pltpu.VMEM((2, N, L), F32),
            pltpu.VMEM((2, C, N), F32),
            pltpu.VMEM((2, 1, C), jnp.int32),
            pltpu.SemaphoreType.DMA((5,)),
        ],
        name="primal",
        compiler_params=pltpu.CompilerParams(vmem_limit_bytes=58 * MIB),
        cost_estimate=pl.CostEstimate(flops=200_000_000, bytes_accessed=3 * MIB, transcendentals=0),
    )(place, direc2, links, corner_map, coarse_factor[0])
    others = [exchange(pay, "grp", 4, lambda i, m=m: i ^ m) for m in (1, 3, 2)]

    packed = jax.ShapeDtypeStruct((NAMES + 8, L), F32)
    local, cross, near = pl.pallas_call(
        local_kernel,
        out_shape=(jax.ShapeDtypeStruct((2, N, L), F32), packed, packed),
        in_specs=[smem(), hbm()] + [vmem()] * 3,
        out_specs=(vmem(), hbm(), hbm()),
        scratch_shapes=[
            pltpu.VMEM((2, N, N), F32),
            pltpu.VMEM((2, NAMES + 8, L), F32),
            pltpu.VMEM((2, HALF, N), BF16),
            pltpu.VMEM((2, 2 * N, L), BF16),
            pltpu.VMEM((2, N, L), BF16),
            pltpu.VMEM((2, N, L), BF16),
            pltpu.SemaphoreType.DMA((2,)),
            pltpu.SemaphoreType.DMA((2,)),
        ],
        name="local",
        compiler_params=pltpu.CompilerParams(vmem_limit_bytes=LIMIT),
        cost_estimate=pl.CostEstimate(flops=4_000_000_000, bytes_accessed=12 * MIB, transcendentals=0),
    )(token, blocks, direc2, links, partner)

    def across(i):
        j = i + 1 if i % 2 else i - 1
        return j if 0 <= j < chain else None

    def beside(i):
        return i ^ 1

    got_cross = exchange(cross, "sub", chain, across)
    got_near = exchange(near, "sub", chain, beside)

    piece = jax.ShapeDtypeStruct((C, L), F32)
    cross_pick, near_pick = pl.pallas_call(
        coarse_kernel,
        out_shape=(piece, piece),
        in_specs=[smem()] + [vmem()] * 4,
        out_specs=(vmem(), vmem()),
        name="coarse",
        compiler_params=pltpu.CompilerParams(vmem_limit_bytes=16 * MIB),
        cost_estimate=pl.CostEstimate(flops=30_000_000_000, bytes_accessed=MIB, transcendentals=0),
    )(place, pay, *others)
    got_cross_pick = exchange(cross_pick, "sub", chain, across)
    got_near_pick = exchange(near_pick, "sub", chain, beside)

    part, sums = pl.pallas_call(
        inner_kernel,
        out_shape=(whole, jax.ShapeDtypeStruct((3, 8, L), F32)),
        in_specs=[smem()] + [vmem()] * 8,
        out_specs=(vmem(), vmem()),
        scratch_shapes=[
            pltpu.VMEM((2, N, L), F32),
            pltpu.VMEM((2, N, L), BF16),
            pltpu.VMEM((2, N, L), BF16),
        ],
        name="inner",
        compiler_params=pltpu.CompilerParams(vmem_limit_bytes=24 * MIB),
        cost_estimate=pl.CostEstimate(flops=2_500_000_000, bytes_accessed=8 * MIB, transcendentals=0),
    )(place, local, cross_pick, near_pick, links, direc2, resid2, scale, partner)

    jump, total = pl.pallas_call(
        outer_kernel,
        out_shape=(whole, jax.ShapeDtypeStruct((8, L), F32)),
        in_specs=[smem()] + [vmem()] * 7,
        out_specs=(vmem(), vmem()),
        name="outer",
        compiler_params=pltpu.CompilerParams(vmem_limit_bytes=24 * MIB),
    )(place, part, got_cross, got_near, got_cross_pick, got_near_pick, scale, sums)

    total = total + exchange(total, "sub", chain, beside)
    both = ("sub", "grp")
    size = 4 * chain
    for near_bit, far_bit in (((4 * 8, 1)), ((3 * 4 * 8, 3)), ((4 * 2, 3 * 4 * 2))):
        flips = (near_bit, far_bit, near_bit ^ far_bit)
        total = total + sum(exchange(total, both, size, lambda i, m=m: i ^ m) for m in flips)

    lam_next, resid_next, direc_next, ratio = pl.pallas_call(
        final_kernel,
        out_shape=(whole, whole, whole, jax.ShapeDtypeStruct((1, L), F32)),
        in_specs=[vmem()] * 6,
        out_specs=(hbm(), hbm(), hbm(), vmem()),
        scratch_shapes=[pltpu.VMEM((2, N, L), F32)] * 3 + [pltpu.SemaphoreType.DMA((24,))],
        name="final",
        compiler_params=pltpu.CompilerParams(vmem_limit_bytes=24 * MIB),
    )(total, scale, lam2, resid2, direc2, jump)
    return (lam_next[:, None], resid_next[:, None], direc_next[:, None], ratio[0])


def solution(mesh):
    placed = (
        P("sub", "grp", None, None),
        P("sub", "grp", None, None),
        P("sub", "grp", None),
        P("sub", "grp"),
        P("sub", "grp", None),
        P("sub", "grp", None),
        P("sub", "grp", None),
        P("sub", "grp", None, None),
        P("sub", "grp", None, None),
        P("sub", "grp", None, None),
    )
    return jax.shard_map(
        per_device,
        mesh=mesh,
        in_specs=placed,
        out_specs=(
            P("sub", "grp", None, None),
            P("sub", "grp", None, None),
            P("sub", "grp", None, None),
            P(),
        ),
        check_vma=False,
    )
```

```python
import functools

import jax
import jax.numpy as jnp
from jax import lax
from jax.experimental import pallas as pl
from jax.experimental.pallas import tpu as pltpu
from jax.sharding import PartitionSpec as P

F32 = jnp.float32
BF16 = jnp.bfloat16
N = 1024
L = 256
C = 64
HALF = 512
NAMES = HALF + 2 * C
STRIP = 512
ROUNDS = N // STRIP
MIB = 1 << 20


def dot(a, b):
    return lax.dot_general(a, b, (((1,), (0,)), ((), ())), preferred_element_type=F32)


def dot_t(a, b):
    return lax.dot_general(a, b, (((0,), (0,)), ((), ())), preferred_element_type=F32)


def split(x):
    high = x.astype(BF16)
    low = (x - high.astype(F32)).astype(BF16)
    return high, low


def iota(shape, dim):
    return lax.broadcasted_iota(jnp.int32, shape, dim)


def one_hot(test):
    return jnp.where(test, 1.0, 0.0).astype(BF16)


def fold(x):
    return jnp.sum(x.reshape(-1, 8, x.shape[-1]), axis=0)


def column(row):
    tall = jnp.transpose(jnp.broadcast_to(row, (128, row.shape[1])))
    return jnp.concatenate([tall, tall], axis=1)


def primal_kernel(direc_hbm, coup_hbm, map_hbm, factor_hbm, pay_ref, direc, coup, corner, sems):
    copies = [
        pltpu.make_async_copy(coup_hbm, coup, sems.at[0]),
        pltpu.make_async_copy(direc_hbm.at[0], direc.at[0], sems.at[1]),
        pltpu.make_async_copy(direc_hbm.at[1], direc.at[1], sems.at[2]),
        pltpu.make_async_copy(map_hbm, corner, sems.at[3]),
        pltpu.make_async_copy(factor_hbm, pay_ref.at[pl.ds(2 * C, C)], sems.at[4]),
    ]
    for copy in copies:
        copy.start()
    pay_ref[3 * C :] = jnp.zeros((8, L), F32)
    for copy in copies:
        copy.wait()
    for s in range(2):
        ch, cl = split(coup[s])
        dh, dl = split(direc[s])
        pay_ref[s * C : (s + 1) * C] = dot(ch, dh) + dot(ch, dl) + dot(cl, dh)
        pay_ref[3 * C + s : 3 * C + s + 1, 0:C] = corner[s].astype(F32)


def running_count(mask):
    total = mask.astype(jnp.int32)
    lane = iota(total.shape, 1)
    step = 1
    while step < total.shape[1]:
        total = total + jnp.where(lane >= step, pltpu.roll(total, step, 1), 0)
        step *= 2
    return total


def local_kernel(
    place_ref, pay_hbm, flex_hbm, direc_hbm, coup_hbm, partner_hbm,
    local_hbm, cross_hbm, near_hbm,
    flex, direc, coup, partner, local, packed, right, high, low, sems, out_sems,
):
    del pay_hbm
    direc_copy = pltpu.make_async_copy(direc_hbm, direc, sems.at[0])
    flex_copies = [
        pltpu.make_async_copy(flex_hbm.at[s], flex.at[s], sems.at[1 + s]) for s in range(2)
    ]
    others = [
        pltpu.make_async_copy(coup_hbm, coup, sems.at[3]),
        pltpu.make_async_copy(partner_hbm, partner, sems.at[4]),
    ]
    out_copies = [
        pltpu.make_async_copy(local.at[s], local_hbm.at[s], out_sems.at[s]) for s in range(2)
    ]
    direc_copy.start()
    for copy in flex_copies + others:
        copy.start()
    me = place_ref[0]
    odd = lax.rem(me, 2)
    direc_copy.wait()
    for s in range(2):
        dh, dl = split(direc[s])
        right[s, 0:N] = dh
        right[s, N:] = dl
    flex_copies[0].wait()
    for s in range(2):
        if s == 1:
            out_copies[0].start()
            flex_copies[1].wait()
            for copy in others:
                copy.wait()
        for r in range(ROUNDS):
            rows = slice(r * STRIP, (r + 1) * STRIP)
            ah, al = split(flex[s, rows])
            out = dot(ah, right[s, 0:N]) + dot(ah, right[s, N:]) + dot(al, right[s, 0:N])
            local[s, rows] = out
            oh, ol = split(out)
            high[s, rows] = oh
            low[s, rows] = ol
    out_copies[1].start()
    for s in range(2):
        target = partner[s] - (2 * me - 1) * N
        match = (target >= 3 * N) if s else (target < N)
        key = jnp.where(match, running_count(match) - 1, -1)
        name = jnp.where(match, jnp.bitwise_and(target, N - 1) + 1, 0)
        coarse = lax.shift_right_logical(name, 5)
        fine = jnp.bitwise_and(name, 31)
        digits = jnp.concatenate(
            [coarse, fine, jnp.zeros((14, N), jnp.int32)], axis=0
        ).astype(F32).astype(BF16)
        ch, cl = split(coup[s])
        stack = jnp.concatenate([ch, cl, digits], axis=0)
        packed[s, NAMES:] = jnp.zeros((8, L), F32)
        place = one_hot(iota((HALF, N), 0) == key)
        packed[s, 0:HALF] = dot(place, high[s]) + dot(place, low[s])
        extra = lax.dot_general(
            stack, place, (((1,), (1,)), ((), ())), preferred_element_type=F32
        )
        for c in range(2):
            part = extra[:, c * L : (c + 1) * L]
            packed[s, HALF + c * C : HALF + (c + 1) * C] = part[0:C] + part[C : 2 * C]
            packed[s, NAMES + c : NAMES + c + 1] = (
                part[2 * C : 2 * C + 1] * 32.0 + part[2 * C + 1 : 2 * C + 2]
            )
    cross_copy = pltpu.make_async_copy(packed.at[odd], cross_hbm, out_sems.at[2])
    near_copy = pltpu.make_async_copy(packed.at[1 - odd], near_hbm, out_sems.at[3])
    cross_copy.start()
    near_copy.start()
    for copy in out_copies:
        copy.wait()
    cross_copy.wait()
    near_copy.wait()


def selector(pay_ref):
    first = pay_ref[3 * C : 3 * C + 1, 0:C]
    second = pay_ref[3 * C + 1 : 3 * C + 2, 0:C]
    both = jnp.concatenate([first, second], axis=1).astype(jnp.int32)
    return one_hot(iota((L, 2 * C), 0) == both)


def coarse_kernel(place_ref, pay_ref, one_ref, two_ref, three_ref, cross_ref, near_ref):
    odd = lax.rem(place_ref[0], 2)
    members = (pay_ref, one_ref, two_ref, three_ref)
    sels, parts = [], []
    for member in members:
        sel = selector(member)
        ph, pl_ = split(member[0 : 2 * C])
        sels += [sel, sel]
        parts += [ph, pl_]
    rhs = dot(jnp.concatenate(sels, axis=1), jnp.concatenate(parts, axis=0))
    factor = jnp.concatenate([m[2 * C : 3 * C] for m in members], axis=0)
    fh, fl = split(factor)
    rh, rl = split(rhs)
    mid = dot(jnp.concatenate([fh, fh, fl], axis=1), jnp.concatenate([rh, rl, rh], axis=0))
    mh, ml = split(mid)
    sol = dot_t(jnp.concatenate([fh, fh, fl], axis=0), jnp.concatenate([mh, ml, mh], axis=0))
    sh, sl = split(sol)
    own = sels[0]
    picked = dot_t(jnp.concatenate([own, own], axis=0), jnp.concatenate([sh, sl], axis=0))

    @pl.when(odd == 0)
    def _():
        cross_ref[...] = picked[0:C]
        near_ref[...] = picked[C:]

    @pl.when(odd == 1)
    def _():
        near_ref[...] = picked[0:C]
        cross_ref[...] = picked[C:]


def inner_kernel(
    place_ref, local_ref, cross_ref, near_ref, coup_ref, direc_ref, resid_ref, weight_ref, partner_ref,
    jump_ref, sums_ref, image_ref, high, low,
):
    me = place_ref[0]
    odd = lax.rem(me, 2) == 1
    old = jnp.zeros((8, L), F32)
    curve = jnp.zeros((8, L), F32)
    mixed = jnp.zeros((8, L), F32)
    for s in range(2):
        ch, cl = split(coup_ref[s])
        qh, ql = split(jnp.where(odd == (s == 1), cross_ref[...], near_ref[...]))
        left = jnp.concatenate([ch, ch, cl], axis=0)
        right = jnp.concatenate([qh, ql, qh], axis=0)
        for r in range(0, N, L):
            image = local_ref[s, r : r + L] + dot_t(left[:, r : r + L], right)
            image_ref[s, r : r + L] = image
            ih, il = split(image)
            high[s, r : r + L] = ih
            low[s, r : r + L] = il
    for s in range(2):
        other = 1 - s
        theirs = partner_ref[other] - (2 * me + s) * N
        mine = partner_ref[s]
        awake = jnp.where(lax.shift_right_arithmetic(mine, 10) != 2 * me + s, 1.0, 0.0)
        for r in range(0, N, STRIP):
            rows = slice(r, r + STRIP)
            place = one_hot(iota((STRIP, N), 0) + r == theirs)
            opposite = dot(place, high[other]) + dot(place, low[other])
            image = image_ref[s, rows]
            jump_ref[s, rows] = column(awake[:, rows]) * image - opposite
            scaled = column(weight_ref[s][:, rows]) * resid_ref[s, rows]
            old = old + fold(scaled * resid_ref[s, rows])
            curve = curve + fold(direc_ref[s, rows] * image)
            mixed = mixed + fold(scaled * image)
    sums_ref[0] = old
    sums_ref[1] = curve
    sums_ref[2] = mixed


def outer_kernel(
    place_ref, part_ref, cross_ref, near_ref, cross_pick_ref, near_pick_ref, weight_ref, sums_ref,
    jump_ref, total_ref,
):
    odd = lax.rem(place_ref[0], 2)
    square = jnp.zeros((8, L), F32)
    for ref, pick_ref, s in ((cross_ref, cross_pick_ref, odd), (near_ref, near_pick_ref, 1 - odd)):
        qh, ql = split(pick_ref[...])
        right = jnp.concatenate([qh, ql, qh], axis=0)
        highs, lows = [], []
        for c in range(2):
            ch, cl = split(ref[HALF + c * C : HALF + (c + 1) * C])
            left = jnp.concatenate([ch, ch, cl], axis=0)
            image_high, image_low = split(ref[c * L : (c + 1) * L] + dot_t(left, right))
            highs.append(image_high)
            lows.append(image_low)
        stacked = jnp.concatenate(highs + lows, axis=0)
        names = [ref[NAMES + c : NAMES + c + 1].astype(jnp.int32) for c in range(2)]
        for r in range(0, N, STRIP):
            places = [one_hot(iota((STRIP, L), 0) + (r + 1) == name) for name in names]
            opposite = dot(jnp.concatenate(places + places, axis=1), stacked)
            jump = part_ref[s, r : r + STRIP] - opposite
            jump_ref[s, r : r + STRIP] = jump
            square = square + fold(column(weight_ref[s][:, r : r + STRIP]) * jump * jump)
    rows = [jnp.sum(x, axis=0, keepdims=True) for x in (sums_ref[0], sums_ref[1], sums_ref[2], square)]
    total_ref[...] = jnp.concatenate(rows + [jnp.zeros((4, L), F32)], axis=0)


def final_kernel(
    total_ref, weight_ref, lam_ref, resid_ref, direc_ref, jump_ref,
    lam_hbm, resid_hbm, direc_hbm, ratio_ref, lam_out, resid_out, direc_out, sems,
):
    old = total_ref[0:1]
    alpha = old / (2.0 * total_ref[1:2])
    new = old + alpha * (alpha * total_ref[3:4] - 4.0 * total_ref[2:3])
    ratio = new / old
    ratio_ref[...] = ratio
    copies = []
    for s in range(2):
        for r in range(4):
            rows = slice(r * L, (r + 1) * L)
            direc = direc_ref[s, rows]
            resid = resid_ref[s, rows] - alpha * jump_ref[s, rows]
            lam_out[s, rows] = lam_ref[s, rows] + alpha * direc
            resid_out[s, rows] = resid
            direc_out[s, rows] = column(weight_ref[s][:, rows]) * resid + ratio * direc
            piece = pl.ds(r * L, L)
            for k, (here, there) in enumerate(
                ((lam_out, lam_hbm), (resid_out, resid_hbm), (direc_out, direc_hbm))
            ):
                copy = pltpu.make_async_copy(
                    here.at[s, piece], there.at[s, piece], sems.at[(s * 4 + r) * 3 + k]
                )
                copy.start()
                copies.append(copy)
    for copy in copies:
        copy.wait()


def vmem():
    return pl.BlockSpec(memory_space=pltpu.VMEM)


def hbm():
    return pl.BlockSpec(memory_space=pltpu.HBM)


def smem():
    return pl.BlockSpec(memory_space=pltpu.SMEM)


def exchange(x, axes, size, route):
    pairs = []
    for i in range(size):
        j = route(i)
        if j is not None:
            pairs.append((i, j))
    return lax.ppermute(x, axes, pairs)


def per_device(
    flex, coupling, weight, iface_size, partner, corner_map, coarse_factor, lam, resid, direc
):
    del iface_size
    blocks, links, scale = flex[:, 0], coupling[:, 0], weight
    lam2, resid2, direc2 = lam[:, 0], resid[:, 0], direc[:, 0]
    chain = lax.axis_size("sub")
    place = lax.axis_index("sub").astype(jnp.int32).reshape(1)

    whole = jax.ShapeDtypeStruct((2, N, L), F32)
    pay = pl.pallas_call(
        primal_kernel,
        out_shape=jax.ShapeDtypeStruct((3 * C + 8, L), F32),
        in_specs=[hbm()] * 4,
        out_specs=vmem(),
        scratch_shapes=[
            pltpu.VMEM((2, N, L), F32),
            pltpu.VMEM((2, C, N), F32),
            pltpu.VMEM((2, 1, C), jnp.int32),
            pltpu.SemaphoreType.DMA((5,)),
        ],
        name="primal",
        compiler_params=pltpu.CompilerParams(vmem_limit_bytes=58 * MIB),
        cost_estimate=pl.CostEstimate(flops=200_000_000, bytes_accessed=3 * MIB, transcendentals=0),
    )(direc2, links, corner_map, coarse_factor[0])
    others = [exchange(pay, "grp", 4, lambda i, m=m: i ^ m) for m in (1, 3, 2)]

    packed = jax.ShapeDtypeStruct((NAMES + 8, L), F32)
    local, cross, near = pl.pallas_call(
        local_kernel,
        out_shape=(jax.ShapeDtypeStruct((2, N, L), F32), packed, packed),
        in_specs=[smem()] + [hbm()] * 5,
        out_specs=(hbm(), hbm(), hbm()),
        scratch_shapes=[
            pltpu.VMEM((2, N, N), F32),
            pltpu.VMEM((2, N, L), F32),
            pltpu.VMEM((2, C, N), F32),
            pltpu.VMEM((2, 1, N), jnp.int32),
            pltpu.VMEM((2, N, L), F32),
            pltpu.VMEM((2, NAMES + 8, L), F32),
            pltpu.VMEM((2, 2 * N, L), BF16),
            pltpu.VMEM((2, N, L), BF16),
            pltpu.VMEM((2, N, L), BF16),
            pltpu.SemaphoreType.DMA((5,)),
            pltpu.SemaphoreType.DMA((4,)),
        ],
        name="local",
        compiler_params=pltpu.CompilerParams(vmem_limit_bytes=58 * MIB),
        cost_estimate=pl.CostEstimate(flops=4_000_000_000, bytes_accessed=12 * MIB, transcendentals=0),
    )(place, pay, blocks, direc2, links, partner)

    def across(i):
        j = i + 1 if i % 2 else i - 1
        return j if 0 <= j < chain else None

    def beside(i):
        return i ^ 1

    got_cross = exchange(cross, "sub", chain, across)
    got_near = exchange(near, "sub", chain, beside)

    piece = jax.ShapeDtypeStruct((C, L), F32)
    cross_pick, near_pick = pl.pallas_call(
        coarse_kernel,
        out_shape=(piece, piece),
        in_specs=[smem()] + [vmem()] * 4,
        out_specs=(vmem(), vmem()),
        name="coarse",
        compiler_params=pltpu.CompilerParams(vmem_limit_bytes=16 * MIB),
        cost_estimate=pl.CostEstimate(flops=30_000_000_000, bytes_accessed=MIB, transcendentals=0),
    )(place, pay, *others)
    got_cross_pick = exchange(cross_pick, "sub", chain, across)
    got_near_pick = exchange(near_pick, "sub", chain, beside)

    part, sums = pl.pallas_call(
        inner_kernel,
        out_shape=(whole, jax.ShapeDtypeStruct((3, 8, L), F32)),
        in_specs=[smem()] + [vmem()] * 8,
        out_specs=(vmem(), vmem()),
        scratch_shapes=[
            pltpu.VMEM((2, N, L), F32),
            pltpu.VMEM((2, N, L), BF16),
            pltpu.VMEM((2, N, L), BF16),
        ],
        name="inner",
        compiler_params=pltpu.CompilerParams(vmem_limit_bytes=24 * MIB),
        cost_estimate=pl.CostEstimate(flops=2_500_000_000, bytes_accessed=8 * MIB, transcendentals=0),
    )(place, local, cross_pick, near_pick, links, direc2, resid2, scale, partner)

    jump, total = pl.pallas_call(
        outer_kernel,
        out_shape=(whole, jax.ShapeDtypeStruct((8, L), F32)),
        in_specs=[smem()] + [vmem()] * 7,
        out_specs=(vmem(), vmem()),
        name="outer",
        compiler_params=pltpu.CompilerParams(vmem_limit_bytes=24 * MIB),
    )(place, part, got_cross, got_near, got_cross_pick, got_near_pick, scale, sums)

    total = total + exchange(total, "sub", chain, beside)
    both = ("sub", "grp")
    size = 4 * chain
    for near_bit, far_bit in (((4 * 8, 1)), ((3 * 4 * 8, 3)), ((4 * 2, 3 * 4 * 2))):
        flips = (near_bit, far_bit, near_bit ^ far_bit)
        total = total + sum(exchange(total, both, size, lambda i, m=m: i ^ m) for m in flips)

    lam_next, resid_next, direc_next, ratio = pl.pallas_call(
        final_kernel,
        out_shape=(whole, whole, whole, jax.ShapeDtypeStruct((1, L), F32)),
        in_specs=[vmem()] * 6,
        out_specs=(hbm(), hbm(), hbm(), vmem()),
        scratch_shapes=[pltpu.VMEM((2, N, L), F32)] * 3 + [pltpu.SemaphoreType.DMA((24,))],
        name="final",
        compiler_params=pltpu.CompilerParams(vmem_limit_bytes=24 * MIB),
    )(total, scale, lam2, resid2, direc2, jump)
    return (lam_next[:, None], resid_next[:, None], direc_next[:, None], ratio[0])


def solution(mesh):
    placed = (
        P("sub", "grp", None, None),
        P("sub", "grp", None, None),
        P("sub", "grp", None),
        P("sub", "grp"),
        P("sub", "grp", None),
        P("sub", "grp", None),
        P("sub", "grp", None),
        P("sub", "grp", None, None),
        P("sub", "grp", None, None),
        P("sub", "grp", None, None),
    )
    return jax.shard_map(
        per_device,
        mesh=mesh,
        in_specs=placed,
        out_specs=(
            P("sub", "grp", None, None),
            P("sub", "grp", None, None),
            P("sub", "grp", None, None),
            P(),
        ),
        check_vma=False,
    )
```

```python
import functools

import jax
import jax.numpy as jnp
from jax import lax
from jax.experimental import pallas as pl
from jax.experimental.pallas import tpu as pltpu
from jax.sharding import PartitionSpec as P

F32 = jnp.float32
BF16 = jnp.bfloat16
N = 1024
L = 256
C = 64
HALF = 512
NAMES = HALF + 2 * C
STRIP = 512
ROUNDS = N // STRIP
MIB = 1 << 20


def dot(a, b):
    return lax.dot_general(a, b, (((1,), (0,)), ((), ())), preferred_element_type=F32)


def dot_t(a, b):
    return lax.dot_general(a, b, (((0,), (0,)), ((), ())), preferred_element_type=F32)


def split(x):
    high = x.astype(BF16)
    low = (x - high.astype(F32)).astype(BF16)
    return high, low


def iota(shape, dim):
    return lax.broadcasted_iota(jnp.int32, shape, dim)


def one_hot(test):
    return jnp.where(test, 1.0, 0.0).astype(BF16)


def fold(x):
    return jnp.sum(x.reshape(-1, 8, x.shape[-1]), axis=0)


def column(row):
    tall = jnp.transpose(jnp.broadcast_to(row, (128, row.shape[1])))
    return jnp.concatenate([tall, tall], axis=1)


def primal_kernel(direc_hbm, coup_hbm, map_hbm, factor_hbm, pay_ref, direc, coup, corner, sems):
    copies = [
        pltpu.make_async_copy(coup_hbm, coup, sems.at[0]),
        pltpu.make_async_copy(direc_hbm.at[0], direc.at[0], sems.at[1]),
        pltpu.make_async_copy(direc_hbm.at[1], direc.at[1], sems.at[2]),
        pltpu.make_async_copy(map_hbm, corner, sems.at[3]),
        pltpu.make_async_copy(factor_hbm, pay_ref.at[pl.ds(2 * C, C)], sems.at[4]),
    ]
    for copy in copies:
        copy.start()
    pay_ref[3 * C :] = jnp.zeros((8, L), F32)
    for copy in copies:
        copy.wait()
    for s in range(2):
        ch, cl = split(coup[s])
        dh, dl = split(direc[s])
        both = dot(jnp.concatenate([ch, cl], axis=0), dh)
        pay_ref[s * C : (s + 1) * C] = both[0:C] + both[C:] + dot(ch, dl)
        pay_ref[3 * C + s : 3 * C + s + 1, 0:C] = corner[s].astype(F32)


def running_count(mask):
    total = mask.astype(jnp.int32)
    lane = iota(total.shape, 1)
    step = 1
    while step < total.shape[1]:
        total = total + jnp.where(lane >= step, pltpu.roll(total, step, 1), 0)
        step *= 2
    return total


def local_kernel(
    place_ref, pay_hbm, flex_hbm, direc_hbm, coup_hbm, partner_hbm,
    local_hbm, cross_hbm, near_hbm,
    flex, direc, coup, partner, local, packed, right, high, low, sems, out_sems,
):
    del pay_hbm
    direc_copy = pltpu.make_async_copy(direc_hbm, direc, sems.at[0])
    flex_copies = [
        pltpu.make_async_copy(flex_hbm.at[s], flex.at[s], sems.at[1 + s]) for s in range(2)
    ]
    others = [
        pltpu.make_async_copy(coup_hbm, coup, sems.at[3]),
        pltpu.make_async_copy(partner_hbm, partner, sems.at[4]),
    ]
    out_copies = [
        pltpu.make_async_copy(local.at[s], local_hbm.at[s], out_sems.at[s]) for s in range(2)
    ]
    direc_copy.start()
    for copy in flex_copies + others:
        copy.start()
    me = place_ref[0]
    odd = lax.rem(me, 2)
    direc_copy.wait()
    for s in range(2):
        dh, dl = split(direc[s])
        right[s, 0:N] = dh
        right[s, N:] = dl
    flex_copies[0].wait()
    for s in range(2):
        if s == 1:
            out_copies[0].start()
            flex_copies[1].wait()
            for copy in others:
                copy.wait()
        for r in range(ROUNDS):
            rows = slice(r * STRIP, (r + 1) * STRIP)
            ah, al = split(flex[s, rows])
            both = dot(jnp.concatenate([ah, al], axis=0), right[s, 0:N])
            out = both[0:STRIP] + both[STRIP:] + dot(ah, right[s, N:])
            local[s, rows] = out
            oh, ol = split(out)
            high[s, rows] = oh
            low[s, rows] = ol
    out_copies[1].start()
    for s in range(2):
        target = partner[s] - (2 * me - 1) * N
        match = (target >= 3 * N) if s else (target < N)
        key = jnp.where(match, running_count(match) - 1, -1)
        name = jnp.where(match, jnp.bitwise_and(target, N - 1) + 1, 0)
        coarse = lax.shift_right_logical(name, 5)
        fine = jnp.bitwise_and(name, 31)
        digits = jnp.concatenate(
            [coarse, fine, jnp.zeros((14, N), jnp.int32)], axis=0
        ).astype(F32).astype(BF16)
        ch, cl = split(coup[s])
        stack = jnp.concatenate([ch, cl, digits], axis=0)
        packed[s, NAMES:] = jnp.zeros((8, L), F32)
        place = one_hot(iota((HALF, N), 0) == key)
        packed[s, 0:HALF] = dot(place, high[s]) + dot(place, low[s])
        extra = lax.dot_general(
            stack, place, (((1,), (1,)), ((), ())), preferred_element_type=F32
        )
        for c in range(2):
            part = extra[:, c * L : (c + 1) * L]
            packed[s, HALF + c * C : HALF + (c + 1) * C] = part[0:C] + part[C : 2 * C]
            packed[s, NAMES + c : NAMES + c + 1] = (
                part[2 * C : 2 * C + 1] * 32.0 + part[2 * C + 1 : 2 * C + 2]
            )
    cross_copy = pltpu.make_async_copy(packed.at[odd], cross_hbm, out_sems.at[2])
    near_copy = pltpu.make_async_copy(packed.at[1 - odd], near_hbm, out_sems.at[3])
    cross_copy.start()
    near_copy.start()
    for copy in out_copies:
        copy.wait()
    cross_copy.wait()
    near_copy.wait()


def selector(pay_ref):
    first = pay_ref[3 * C : 3 * C + 1, 0:C]
    second = pay_ref[3 * C + 1 : 3 * C + 2, 0:C]
    both = jnp.concatenate([first, second], axis=1).astype(jnp.int32)
    return one_hot(iota((L, 2 * C), 0) == both)


def coarse_kernel(place_ref, pay_ref, one_ref, two_ref, three_ref, cross_ref, near_ref):
    odd = lax.rem(place_ref[0], 2)
    members = (pay_ref, one_ref, two_ref, three_ref)
    sels, parts = [], []
    for member in members:
        sel = selector(member)
        ph, pl_ = split(member[0 : 2 * C])
        sels += [sel, sel]
        parts += [ph, pl_]
    rhs = dot(jnp.concatenate(sels, axis=1), jnp.concatenate(parts, axis=0))
    factor = jnp.concatenate([m[2 * C : 3 * C] for m in members], axis=0)
    fh, fl = split(factor)
    rh, rl = split(rhs)
    mid = dot(jnp.concatenate([fh, fh, fl], axis=1), jnp.concatenate([rh, rl, rh], axis=0))
    mh, ml = split(mid)
    sol = dot_t(jnp.concatenate([fh, fh, fl], axis=0), jnp.concatenate([mh, ml, mh], axis=0))
    sh, sl = split(sol)
    own = sels[0]
    picked = dot_t(jnp.concatenate([own, own], axis=0), jnp.concatenate([sh, sl], axis=0))

    @pl.when(odd == 0)
    def _():
        cross_ref[...] = picked[0:C]
        near_ref[...] = picked[C:]

    @pl.when(odd == 1)
    def _():
        near_ref[...] = picked[0:C]
        cross_ref[...] = picked[C:]


def inner_kernel(
    place_ref, local_ref, cross_ref, near_ref, coup_ref, direc_ref, resid_ref, weight_ref, partner_ref,
    jump_ref, sums_ref, image_ref, high, low,
):
    me = place_ref[0]
    odd = lax.rem(me, 2) == 1
    old = jnp.zeros((8, L), F32)
    curve = jnp.zeros((8, L), F32)
    mixed = jnp.zeros((8, L), F32)
    for s in range(2):
        ch, cl = split(coup_ref[s])
        qh, ql = split(jnp.where(odd == (s == 1), cross_ref[...], near_ref[...]))
        left = jnp.concatenate([ch, ch, cl], axis=0)
        right = jnp.concatenate([qh, ql, qh], axis=0)
        for r in range(0, N, L):
            image = local_ref[s, r : r + L] + dot_t(left[:, r : r + L], right)
            image_ref[s, r : r + L] = image
            ih, il = split(image)
            high[s, r : r + L] = ih
            low[s, r : r + L] = il
    for s in range(2):
        other = 1 - s
        theirs = partner_ref[other] - (2 * me + s) * N
        mine = partner_ref[s]
        awake = jnp.where(lax.shift_right_arithmetic(mine, 10) != 2 * me + s, 1.0, 0.0)
        for r in range(0, N, STRIP):
            rows = slice(r, r + STRIP)
            place = one_hot(iota((STRIP, N), 0) + r == theirs)
            opposite = dot(place, high[other]) + dot(place, low[other])
            image = image_ref[s, rows]
            jump_ref[s, rows] = column(awake[:, rows]) * image - opposite
            scaled = column(weight_ref[s][:, rows]) * resid_ref[s, rows]
            old = old + fold(scaled * resid_ref[s, rows])
            curve = curve + fold(direc_ref[s, rows] * image)
            mixed = mixed + fold(scaled * image)
    sums_ref[0] = old
    sums_ref[1] = curve
    sums_ref[2] = mixed


def outer_kernel(
    place_ref, part_ref, cross_ref, near_ref, cross_pick_ref, near_pick_ref, weight_ref, sums_ref,
    jump_ref, total_ref,
):
    odd = lax.rem(place_ref[0], 2)
    square = jnp.zeros((8, L), F32)
    for ref, pick_ref, s in ((cross_ref, cross_pick_ref, odd), (near_ref, near_pick_ref, 1 - odd)):
        qh, ql = split(pick_ref[...])
        right = jnp.concatenate([qh, ql, qh], axis=0)
        highs, lows = [], []
        for c in range(2):
            ch, cl = split(ref[HALF + c * C : HALF + (c + 1) * C])
            left = jnp.concatenate([ch, ch, cl], axis=0)
            image_high, image_low = split(ref[c * L : (c + 1) * L] + dot_t(left, right))
            highs.append(image_high)
            lows.append(image_low)
        stacked = jnp.concatenate(highs + lows, axis=0)
        names = [ref[NAMES + c : NAMES + c + 1].astype(jnp.int32) for c in range(2)]
        for r in range(0, N, STRIP):
            places = [one_hot(iota((STRIP, L), 0) + (r + 1) == name) for name in names]
            opposite = dot(jnp.concatenate(places + places, axis=1), stacked)
            jump = part_ref[s, r : r + STRIP] - opposite
            jump_ref[s, r : r + STRIP] = jump
            square = square + fold(column(weight_ref[s][:, r : r + STRIP]) * jump * jump)
    rows = [jnp.sum(x, axis=0, keepdims=True) for x in (sums_ref[0], sums_ref[1], sums_ref[2], square)]
    total_ref[...] = jnp.concatenate(rows + [jnp.zeros((4, L), F32)], axis=0)


def final_kernel(
    total_ref, weight_ref, lam_ref, resid_ref, direc_ref, jump_ref,
    lam_hbm, resid_hbm, direc_hbm, ratio_ref, lam_out, resid_out, direc_out, sems,
):
    old = total_ref[0:1]
    alpha = old / (2.0 * total_ref[1:2])
    new = old + alpha * (alpha * total_ref[3:4] - 4.0 * total_ref[2:3])
    ratio = new / old
    ratio_ref[...] = ratio
    copies = []
    for s in range(2):
        for r in range(4):
            rows = slice(r * L, (r + 1) * L)
            direc = direc_ref[s, rows]
            resid = resid_ref[s, rows] - alpha * jump_ref[s, rows]
            lam_out[s, rows] = lam_ref[s, rows] + alpha * direc
            resid_out[s, rows] = resid
            direc_out[s, rows] = column(weight_ref[s][:, rows]) * resid + ratio * direc
            piece = pl.ds(r * L, L)
            for k, (here, there) in enumerate(
                ((lam_out, lam_hbm), (resid_out, resid_hbm), (direc_out, direc_hbm))
            ):
                copy = pltpu.make_async_copy(
                    here.at[s, piece], there.at[s, piece], sems.at[(s * 4 + r) * 3 + k]
                )
                copy.start()
                copies.append(copy)
    for copy in copies:
        copy.wait()


def vmem():
    return pl.BlockSpec(memory_space=pltpu.VMEM)


def hbm():
    return pl.BlockSpec(memory_space=pltpu.HBM)


def smem():
    return pl.BlockSpec(memory_space=pltpu.SMEM)


def exchange(x, axes, size, route):
    pairs = []
    for i in range(size):
        j = route(i)
        if j is not None:
            pairs.append((i, j))
    return lax.ppermute(x, axes, pairs)


def per_device(
    flex, coupling, weight, iface_size, partner, corner_map, coarse_factor, lam, resid, direc
):
    del iface_size
    blocks, links, scale = flex[:, 0], coupling[:, 0], weight
    lam2, resid2, direc2 = lam[:, 0], resid[:, 0], direc[:, 0]
    chain = lax.axis_size("sub")
    place = lax.axis_index("sub").astype(jnp.int32).reshape(1)

    whole = jax.ShapeDtypeStruct((2, N, L), F32)
    pay = pl.pallas_call(
        primal_kernel,
        out_shape=jax.ShapeDtypeStruct((3 * C + 8, L), F32),
        in_specs=[hbm()] * 4,
        out_specs=vmem(),
        scratch_shapes=[
            pltpu.VMEM((2, N, L), F32),
            pltpu.VMEM((2, C, N), F32),
            pltpu.VMEM((2, 1, C), jnp.int32),
            pltpu.SemaphoreType.DMA((5,)),
        ],
        name="primal",
        compiler_params=pltpu.CompilerParams(vmem_limit_bytes=58 * MIB),
        cost_estimate=pl.CostEstimate(flops=200_000_000, bytes_accessed=3 * MIB, transcendentals=0),
    )(direc2, links, corner_map, coarse_factor[0])
    others = [exchange(pay, "grp", 4, lambda i, m=m: i ^ m) for m in (1, 3, 2)]

    packed = jax.ShapeDtypeStruct((NAMES + 8, L), F32)
    local, cross, near = pl.pallas_call(
        local_kernel,
        out_shape=(jax.ShapeDtypeStruct((2, N, L), F32), packed, packed),
        in_specs=[smem()] + [hbm()] * 5,
        out_specs=(hbm(), hbm(), hbm()),
        scratch_shapes=[
            pltpu.VMEM((2, N, N), F32),
            pltpu.VMEM((2, N, L), F32),
            pltpu.VMEM((2, C, N), F32),
            pltpu.VMEM((2, 1, N), jnp.int32),
            pltpu.VMEM((2, N, L), F32),
            pltpu.VMEM((2, NAMES + 8, L), F32),
            pltpu.VMEM((2, 2 * N, L), BF16),
            pltpu.VMEM((2, N, L), BF16),
            pltpu.VMEM((2, N, L), BF16),
            pltpu.SemaphoreType.DMA((5,)),
            pltpu.SemaphoreType.DMA((4,)),
        ],
        name="local",
        compiler_params=pltpu.CompilerParams(vmem_limit_bytes=58 * MIB),
        cost_estimate=pl.CostEstimate(flops=4_000_000_000, bytes_accessed=12 * MIB, transcendentals=0),
    )(place, pay, blocks, direc2, links, partner)

    def across(i):
        j = i + 1 if i % 2 else i - 1
        return j if 0 <= j < chain else None

    def beside(i):
        return i ^ 1

    got_cross = exchange(cross, "sub", chain, across)
    got_near = exchange(near, "sub", chain, beside)

    piece = jax.ShapeDtypeStruct((C, L), F32)
    cross_pick, near_pick = pl.pallas_call(
        coarse_kernel,
        out_shape=(piece, piece),
        in_specs=[smem()] + [vmem()] * 4,
        out_specs=(vmem(), vmem()),
        name="coarse",
        compiler_params=pltpu.CompilerParams(vmem_limit_bytes=16 * MIB),
        cost_estimate=pl.CostEstimate(flops=30_000_000_000, bytes_accessed=MIB, transcendentals=0),
    )(place, pay, *others)
    got_cross_pick = exchange(cross_pick, "sub", chain, across)
    got_near_pick = exchange(near_pick, "sub", chain, beside)

    part, sums = pl.pallas_call(
        inner_kernel,
        out_shape=(whole, jax.ShapeDtypeStruct((3, 8, L), F32)),
        in_specs=[smem()] + [vmem()] * 8,
        out_specs=(vmem(), vmem()),
        scratch_shapes=[
            pltpu.VMEM((2, N, L), F32),
            pltpu.VMEM((2, N, L), BF16),
            pltpu.VMEM((2, N, L), BF16),
        ],
        name="inner",
        compiler_params=pltpu.CompilerParams(vmem_limit_bytes=24 * MIB),
        cost_estimate=pl.CostEstimate(flops=2_500_000_000, bytes_accessed=8 * MIB, transcendentals=0),
    )(place, local, cross_pick, near_pick, links, direc2, resid2, scale, partner)

    jump, total = pl.pallas_call(
        outer_kernel,
        out_shape=(whole, jax.ShapeDtypeStruct((8, L), F32)),
        in_specs=[smem()] + [vmem()] * 7,
        out_specs=(vmem(), vmem()),
        name="outer",
        compiler_params=pltpu.CompilerParams(vmem_limit_bytes=24 * MIB),
    )(place, part, got_cross, got_near, got_cross_pick, got_near_pick, scale, sums)

    total = total + exchange(total, "sub", chain, beside)
    both = ("sub", "grp")
    size = 4 * chain
    for near_bit, far_bit in (((4 * 8, 1)), ((3 * 4 * 8, 3)), ((4 * 2, 3 * 4 * 2))):
        flips = (near_bit, far_bit, near_bit ^ far_bit)
        total = total + sum(exchange(total, both, size, lambda i, m=m: i ^ m) for m in flips)

    lam_next, resid_next, direc_next, ratio = pl.pallas_call(
        final_kernel,
        out_shape=(whole, whole, whole, jax.ShapeDtypeStruct((1, L), F32)),
        in_specs=[vmem()] * 6,
        out_specs=(hbm(), hbm(), hbm(), vmem()),
        scratch_shapes=[pltpu.VMEM((2, N, L), F32)] * 3 + [pltpu.SemaphoreType.DMA((24,))],
        name="final",
        compiler_params=pltpu.CompilerParams(vmem_limit_bytes=24 * MIB),
    )(total, scale, lam2, resid2, direc2, jump)
    return (lam_next[:, None], resid_next[:, None], direc_next[:, None], ratio[0])


def solution(mesh):
    placed = (
        P("sub", "grp", None, None),
        P("sub", "grp", None, None),
        P("sub", "grp", None),
        P("sub", "grp"),
        P("sub", "grp", None),
        P("sub", "grp", None),
        P("sub", "grp", None),
        P("sub", "grp", None, None),
        P("sub", "grp", None, None),
        P("sub", "grp", None, None),
    )
    return jax.shard_map(
        per_device,
        mesh=mesh,
        in_specs=placed,
        out_specs=(
            P("sub", "grp", None, None),
            P("sub", "grp", None, None),
            P("sub", "grp", None, None),
            P(),
        ),
        check_vma=False,
    )
```

```python
import functools

import jax
import jax.numpy as jnp
from jax import lax
from jax.experimental import pallas as pl
from jax.experimental.pallas import tpu as pltpu
from jax.sharding import PartitionSpec as P

F32 = jnp.float32
BF16 = jnp.bfloat16
N = 1024
L = 256
C = 64
HALF = 512
NAMES = HALF + 2 * C
STRIP = 512
PIECE = 128
ROUNDS = N // STRIP
MIB = 1 << 20


def dot(a, b):
    return lax.dot_general(a, b, (((1,), (0,)), ((), ())), preferred_element_type=F32)


def dot_t(a, b):
    return lax.dot_general(a, b, (((0,), (0,)), ((), ())), preferred_element_type=F32)


def split(x):
    high = x.astype(BF16)
    low = (x - high.astype(F32)).astype(BF16)
    return high, low


def iota(shape, dim):
    return lax.broadcasted_iota(jnp.int32, shape, dim)


def one_hot(test):
    return jnp.where(test, 1.0, 0.0).astype(BF16)


def fold(x):
    return jnp.sum(x.reshape(-1, 8, x.shape[-1]), axis=0)


def column(row):
    tall = jnp.transpose(jnp.broadcast_to(row, (128, row.shape[1])))
    return jnp.concatenate([tall, tall], axis=1)


def primal_kernel(direc_hbm, coup_hbm, map_hbm, factor_hbm, pay_ref, direc, coup, corner, sems):
    copies = [
        pltpu.make_async_copy(coup_hbm, coup, sems.at[0]),
        pltpu.make_async_copy(direc_hbm.at[0], direc.at[0], sems.at[1]),
        pltpu.make_async_copy(direc_hbm.at[1], direc.at[1], sems.at[2]),
        pltpu.make_async_copy(map_hbm, corner, sems.at[3]),
        pltpu.make_async_copy(factor_hbm, pay_ref.at[pl.ds(2 * C, C)], sems.at[4]),
    ]
    for copy in copies:
        copy.start()
    pay_ref[3 * C :] = jnp.zeros((8, L), F32)
    for copy in copies:
        copy.wait()
    for s in range(2):
        ch, cl = split(coup[s])
        dh, dl = split(direc[s])
        both = dot(jnp.concatenate([ch, cl], axis=0), dh)
        pay_ref[s * C : (s + 1) * C] = both[0:C] + both[C:] + dot(ch, dl)
        pay_ref[3 * C + s : 3 * C + s + 1, 0:C] = corner[s].astype(F32)


def running_count(mask):
    total = mask.astype(jnp.int32)
    lane = iota(total.shape, 1)
    step = 1
    while step < total.shape[1]:
        total = total + jnp.where(lane >= step, pltpu.roll(total, step, 1), 0)
        step *= 2
    return total


def local_kernel(
    place_ref, pay_hbm, flex_hbm, direc_hbm, coup_hbm, partner_hbm,
    local_hbm, cross_hbm, near_hbm,
    flex, direc, coup, partner, local, packed, right, high, low, sems, out_sems,
):
    del pay_hbm
    direc_copy = pltpu.make_async_copy(direc_hbm, direc, sems.at[0])
    flex_copies = [
        pltpu.make_async_copy(flex_hbm.at[s], flex.at[s], sems.at[1 + s]) for s in range(2)
    ]
    others = [
        pltpu.make_async_copy(coup_hbm, coup, sems.at[3]),
        pltpu.make_async_copy(partner_hbm, partner, sems.at[4]),
    ]
    out_copies = [
        pltpu.make_async_copy(local.at[s], local_hbm.at[s], out_sems.at[s]) for s in range(2)
    ]
    direc_copy.start()
    for copy in flex_copies + others:
        copy.start()
    me = place_ref[0]
    odd = lax.rem(me, 2)
    direc_copy.wait()
    for s in range(2):
        dh, dl = split(direc[s])
        right[s, 0:N] = dh
        right[s, N:] = dl
    flex_copies[0].wait()
    for s in range(2):
        if s == 1:
            out_copies[0].start()
            flex_copies[1].wait()
            for copy in others:
                copy.wait()
        for r in range(ROUNDS):
            rows = slice(r * STRIP, (r + 1) * STRIP)
            ah, al = split(flex[s, rows])
            both = dot(jnp.concatenate([ah, al], axis=0), right[s, 0:N])
            out = both[0:STRIP] + both[STRIP:] + dot(ah, right[s, N:])
            local[s, rows] = out
            oh, ol = split(out)
            high[s, rows] = oh
            low[s, rows] = ol
    out_copies[1].start()
    for s in range(2):
        target = partner[s] - (2 * me - 1) * N
        match = (target >= 3 * N) if s else (target < N)
        key = jnp.where(match, running_count(match) - 1, -1)
        name = jnp.where(match, jnp.bitwise_and(target, N - 1) + 1, 0)
        coarse = lax.shift_right_logical(name, 5)
        fine = jnp.bitwise_and(name, 31)
        digits = jnp.concatenate(
            [coarse, fine, jnp.zeros((14, N), jnp.int32)], axis=0
        ).astype(F32).astype(BF16)
        ch, cl = split(coup[s])
        stack = jnp.concatenate([ch, cl, digits], axis=0)
        packed[s, NAMES:] = jnp.zeros((8, L), F32)
        place = one_hot(iota((HALF, N), 0) == key)
        packed[s, 0:HALF] = dot(place, high[s]) + dot(place, low[s])
        extra = lax.dot_general(
            stack, place, (((1,), (1,)), ((), ())), preferred_element_type=F32
        )
        for c in range(2):
            part = extra[:, c * L : (c + 1) * L]
            packed[s, HALF + c * C : HALF + (c + 1) * C] = part[0:C] + part[C : 2 * C]
            packed[s, NAMES + c : NAMES + c + 1] = (
                part[2 * C : 2 * C + 1] * 32.0 + part[2 * C + 1 : 2 * C + 2]
            )
    cross_copy = pltpu.make_async_copy(packed.at[odd], cross_hbm, out_sems.at[2])
    near_copy = pltpu.make_async_copy(packed.at[1 - odd], near_hbm, out_sems.at[3])
    cross_copy.start()
    near_copy.start()
    for copy in out_copies:
        copy.wait()
    cross_copy.wait()
    near_copy.wait()


def selector(pay_ref):
    first = pay_ref[3 * C : 3 * C + 1, 0:C]
    second = pay_ref[3 * C + 1 : 3 * C + 2, 0:C]
    both = jnp.concatenate([first, second], axis=1).astype(jnp.int32)
    return one_hot(iota((L, 2 * C), 0) == both)


def coarse_kernel(place_ref, pay_ref, one_ref, two_ref, three_ref, cross_ref, near_ref):
    odd = lax.rem(place_ref[0], 2)
    members = (pay_ref, one_ref, two_ref, three_ref)
    sels, parts = [], []
    for member in members:
        sel = selector(member)
        ph, pl_ = split(member[0 : 2 * C])
        sels += [sel, sel]
        parts += [ph, pl_]
    rhs = dot(jnp.concatenate(sels, axis=1), jnp.concatenate(parts, axis=0))
    factor = jnp.concatenate([m[2 * C : 3 * C] for m in members], axis=0)
    fh, fl = split(factor)
    rh, rl = split(rhs)
    mid = dot(jnp.concatenate([fh, fh, fl], axis=1), jnp.concatenate([rh, rl, rh], axis=0))
    mh, ml = split(mid)
    sol = dot_t(jnp.concatenate([fh, fh, fl], axis=0), jnp.concatenate([mh, ml, mh], axis=0))
    sh, sl = split(sol)
    own = sels[0]
    picked = dot_t(jnp.concatenate([own, own], axis=0), jnp.concatenate([sh, sl], axis=0))

    @pl.when(odd == 0)
    def _():
        cross_ref[...] = picked[0:C]
        near_ref[...] = picked[C:]

    @pl.when(odd == 1)
    def _():
        near_ref[...] = picked[0:C]
        cross_ref[...] = picked[C:]


def inner_kernel(
    place_ref, local_ref, cross_ref, near_ref, coup_ref, direc_ref, resid_ref, weight_ref, partner_ref,
    jump_ref, sums_ref, image_ref, high, low,
):
    me = place_ref[0]
    odd = lax.rem(me, 2) == 1
    old = jnp.zeros((8, L), F32)
    curve = jnp.zeros((8, L), F32)
    mixed = jnp.zeros((8, L), F32)
    for s in range(2):
        ch, cl = split(coup_ref[s])
        qh, ql = split(jnp.where(odd == (s == 1), cross_ref[...], near_ref[...]))
        left = jnp.concatenate([ch, ch, cl], axis=0)
        right = jnp.concatenate([qh, ql, qh], axis=0)
        for r in range(0, N, L):
            image = local_ref[s, r : r + L] + dot_t(left[:, r : r + L], right)
            image_ref[s, r : r + L] = image
            ih, il = split(image)
            high[s, r : r + L] = ih
            low[s, r : r + L] = il
    for s in range(2):
        other = 1 - s
        theirs = partner_ref[other] - (2 * me + s) * N
        mine = partner_ref[s]
        awake = jnp.where(lax.shift_right_arithmetic(mine, 10) != 2 * me + s, 1.0, 0.0)
        for r in range(0, N, STRIP):
            rows = slice(r, r + STRIP)
            place = one_hot(iota((STRIP, N), 0) + r == theirs)
            opposite = dot(place, high[other]) + dot(place, low[other])
            image = image_ref[s, rows]
            jump_ref[s, rows] = column(awake[:, rows]) * image - opposite
            scaled = column(weight_ref[s][:, rows]) * resid_ref[s, rows]
            old = old + fold(scaled * resid_ref[s, rows])
            curve = curve + fold(direc_ref[s, rows] * image)
            mixed = mixed + fold(scaled * image)
    sums_ref[0] = old
    sums_ref[1] = curve
    sums_ref[2] = mixed


def outer_kernel(
    place_ref, part_ref, cross_ref, near_ref, cross_pick_ref, near_pick_ref, weight_ref, sums_ref,
    jump_ref, total_ref,
):
    odd = lax.rem(place_ref[0], 2)
    square = jnp.zeros((8, L), F32)
    for ref, pick_ref, s in ((cross_ref, cross_pick_ref, odd), (near_ref, near_pick_ref, 1 - odd)):
        qh, ql = split(pick_ref[...])
        right = jnp.concatenate([qh, ql, qh], axis=0)
        highs, lows = [], []
        for c in range(2):
            ch, cl = split(ref[HALF + c * C : HALF + (c + 1) * C])
            left = jnp.concatenate([ch, ch, cl], axis=0)
            image_high, image_low = split(ref[c * L : (c + 1) * L] + dot_t(left, right))
            highs.append(image_high)
            lows.append(image_low)
        stacked = jnp.concatenate(highs + lows, axis=0)
        names = [ref[NAMES + c : NAMES + c + 1].astype(jnp.int32) for c in range(2)]
        for r in range(0, N, STRIP):
            places = [one_hot(iota((STRIP, L), 0) + (r + 1) == name) for name in names]
            opposite = dot(jnp.concatenate(places + places, axis=1), stacked)
            jump = part_ref[s, r : r + STRIP] - opposite
            jump_ref[s, r : r + STRIP] = jump
            square = square + fold(column(weight_ref[s][:, r : r + STRIP]) * jump * jump)
    rows = [jnp.sum(x, axis=0, keepdims=True) for x in (sums_ref[0], sums_ref[1], sums_ref[2], square)]
    total_ref[...] = jnp.concatenate(rows + [jnp.zeros((4, L), F32)], axis=0)


def final_kernel(
    total_ref, weight_ref, lam_ref, resid_ref, direc_ref, jump_ref,
    lam_hbm, resid_hbm, direc_hbm, ratio_ref, lam_out, resid_out, direc_out, sems,
):
    old = total_ref[0:1]
    alpha = old / (2.0 * total_ref[1:2])
    new = old + alpha * (alpha * total_ref[3:4] - 4.0 * total_ref[2:3])
    ratio = new / old
    ratio_ref[...] = ratio
    copies = []
    for s in range(2):
        for r in range(N // PIECE):
            rows = slice(r * PIECE, (r + 1) * PIECE)
            direc = direc_ref[s, rows]
            resid = resid_ref[s, rows] - alpha * jump_ref[s, rows]
            lam_out[s, rows] = lam_ref[s, rows] + alpha * direc
            resid_out[s, rows] = resid
            direc_out[s, rows] = column(weight_ref[s][:, rows]) * resid + ratio * direc
            piece = pl.ds(r * PIECE, PIECE)
            for k, (here, there) in enumerate(
                ((lam_out, lam_hbm), (resid_out, resid_hbm), (direc_out, direc_hbm))
            ):
                copy = pltpu.make_async_copy(
                    here.at[s, piece], there.at[s, piece], sems.at[(s * (N // PIECE) + r) * 3 + k]
                )
                copy.start()
                copies.append(copy)
    for copy in copies:
        copy.wait()


def vmem():
    return pl.BlockSpec(memory_space=pltpu.VMEM)


def hbm():
    return pl.BlockSpec(memory_space=pltpu.HBM)


def smem():
    return pl.BlockSpec(memory_space=pltpu.SMEM)


def exchange(x, axes, size, route):
    pairs = []
    for i in range(size):
        j = route(i)
        if j is not None:
            pairs.append((i, j))
    return lax.ppermute(x, axes, pairs)


def per_device(
    flex, coupling, weight, iface_size, partner, corner_map, coarse_factor, lam, resid, direc
):
    del iface_size
    blocks, links, scale = flex[:, 0], coupling[:, 0], weight
    lam2, resid2, direc2 = lam[:, 0], resid[:, 0], direc[:, 0]
    chain = lax.axis_size("sub")
    place = lax.axis_index("sub").astype(jnp.int32).reshape(1)

    whole = jax.ShapeDtypeStruct((2, N, L), F32)
    pay = pl.pallas_call(
        primal_kernel,
        out_shape=jax.ShapeDtypeStruct((3 * C + 8, L), F32),
        in_specs=[hbm()] * 4,
        out_specs=vmem(),
        scratch_shapes=[
            pltpu.VMEM((2, N, L), F32),
            pltpu.VMEM((2, C, N), F32),
            pltpu.VMEM((2, 1, C), jnp.int32),
            pltpu.SemaphoreType.DMA((5,)),
        ],
        name="primal",
        compiler_params=pltpu.CompilerParams(vmem_limit_bytes=58 * MIB),
        cost_estimate=pl.CostEstimate(flops=200_000_000, bytes_accessed=3 * MIB, transcendentals=0),
    )(direc2, links, corner_map, coarse_factor[0])
    others = [exchange(pay, "grp", 4, lambda i, m=m: i ^ m) for m in (1, 3, 2)]

    packed = jax.ShapeDtypeStruct((NAMES + 8, L), F32)
    local, cross, near = pl.pallas_call(
        local_kernel,
        out_shape=(jax.ShapeDtypeStruct((2, N, L), F32), packed, packed),
        in_specs=[smem()] + [hbm()] * 5,
        out_specs=(hbm(), hbm(), hbm()),
        scratch_shapes=[
            pltpu.VMEM((2, N, N), F32),
            pltpu.VMEM((2, N, L), F32),
            pltpu.VMEM((2, C, N), F32),
            pltpu.VMEM((2, 1, N), jnp.int32),
            pltpu.VMEM((2, N, L), F32),
            pltpu.VMEM((2, NAMES + 8, L), F32),
            pltpu.VMEM((2, 2 * N, L), BF16),
            pltpu.VMEM((2, N, L), BF16),
            pltpu.VMEM((2, N, L), BF16),
            pltpu.SemaphoreType.DMA((5,)),
            pltpu.SemaphoreType.DMA((4,)),
        ],
        name="local",
        compiler_params=pltpu.CompilerParams(vmem_limit_bytes=58 * MIB),
        cost_estimate=pl.CostEstimate(flops=4_000_000_000, bytes_accessed=12 * MIB, transcendentals=0),
    )(place, pay, blocks, direc2, links, partner)

    def across(i):
        j = i + 1 if i % 2 else i - 1
        return j if 0 <= j < chain else None

    def beside(i):
        return i ^ 1

    got_cross = exchange(cross, "sub", chain, across)
    got_near = exchange(near, "sub", chain, beside)

    piece = jax.ShapeDtypeStruct((C, L), F32)
    cross_pick, near_pick = pl.pallas_call(
        coarse_kernel,
        out_shape=(piece, piece),
        in_specs=[smem()] + [vmem()] * 4,
        out_specs=(vmem(), vmem()),
        name="coarse",
        compiler_params=pltpu.CompilerParams(vmem_limit_bytes=16 * MIB),
        cost_estimate=pl.CostEstimate(flops=30_000_000_000, bytes_accessed=MIB, transcendentals=0),
    )(place, pay, *others)
    got_cross_pick = exchange(cross_pick, "sub", chain, across)
    got_near_pick = exchange(near_pick, "sub", chain, beside)

    part, sums = pl.pallas_call(
        inner_kernel,
        out_shape=(whole, jax.ShapeDtypeStruct((3, 8, L), F32)),
        in_specs=[smem()] + [vmem()] * 8,
        out_specs=(vmem(), vmem()),
        scratch_shapes=[
            pltpu.VMEM((2, N, L), F32),
            pltpu.VMEM((2, N, L), BF16),
            pltpu.VMEM((2, N, L), BF16),
        ],
        name="inner",
        compiler_params=pltpu.CompilerParams(vmem_limit_bytes=24 * MIB),
        cost_estimate=pl.CostEstimate(flops=2_500_000_000, bytes_accessed=8 * MIB, transcendentals=0),
    )(place, local, cross_pick, near_pick, links, direc2, resid2, scale, partner)

    jump, total = pl.pallas_call(
        outer_kernel,
        out_shape=(whole, jax.ShapeDtypeStruct((8, L), F32)),
        in_specs=[smem()] + [vmem()] * 7,
        out_specs=(vmem(), vmem()),
        name="outer",
        compiler_params=pltpu.CompilerParams(vmem_limit_bytes=24 * MIB),
    )(place, part, got_cross, got_near, got_cross_pick, got_near_pick, scale, sums)

    total = total + exchange(total, "sub", chain, beside)
    both = ("sub", "grp")
    size = 4 * chain
    for near_bit, far_bit in (((4 * 8, 1)), ((3 * 4 * 8, 3)), ((4 * 2, 3 * 4 * 2))):
        flips = (near_bit, far_bit, near_bit ^ far_bit)
        total = total + sum(exchange(total, both, size, lambda i, m=m: i ^ m) for m in flips)

    lam_next, resid_next, direc_next, ratio = pl.pallas_call(
        final_kernel,
        out_shape=(whole, whole, whole, jax.ShapeDtypeStruct((1, L), F32)),
        in_specs=[vmem()] * 6,
        out_specs=(hbm(), hbm(), hbm(), vmem()),
        scratch_shapes=[pltpu.VMEM((2, N, L), F32)] * 3 + [pltpu.SemaphoreType.DMA((6 * N // PIECE,))],
        name="final",
        compiler_params=pltpu.CompilerParams(vmem_limit_bytes=24 * MIB),
    )(total, scale, lam2, resid2, direc2, jump)
    return (lam_next[:, None], resid_next[:, None], direc_next[:, None], ratio[0])


def solution(mesh):
    placed = (
        P("sub", "grp", None, None),
        P("sub", "grp", None, None),
        P("sub", "grp", None),
        P("sub", "grp"),
        P("sub", "grp", None),
        P("sub", "grp", None),
        P("sub", "grp", None),
        P("sub", "grp", None, None),
        P("sub", "grp", None, None),
        P("sub", "grp", None, None),
    )
    return jax.shard_map(
        per_device,
        mesh=mesh,
        in_specs=placed,
        out_specs=(
            P("sub", "grp", None, None),
            P("sub", "grp", None, None),
            P("sub", "grp", None, None),
            P(),
        ),
        check_vma=False,
    )
```
